512 devices in a mesh: brick: 128 (over y, z, core), ch: 4 (over x).
Axes of the slice: x: 4, y: 8, z: 8, core: 2. Of those that a mesh axis runs over, the one named last changes fastest.
Arguments:
- features: bfloat16 [256, 16384], P('ch', 'brick'), may hold values from -6 to 6
- owner_map: int32 [16384, 1], P('brick'), may hold values from 0 to 127; in each aligned block of 128 rows (0 to 127, 128 to 255, ...) at most 2 rows name the same one
- kernel_map: int32 [27, 32768], P(None, 'brick'), may hold values from 0 to 320, as said below
- send_lists: int32 [2, 4096], P(None, 'brick'), may hold values from 0 to 255
- drop_first: int32 [256, 32768], P('ch', 'brick'), may hold values 0 or 1
- drop_second: int32 [256, 32768], P('ch', 'brick'), may hold values 0 or 1
- weight_first: bfloat16 [27, 256, 256], P(None, 'ch'), may hold values from -0.15625 to 0.15625
- weight_second: bfloat16 [27, 256, 256], P(None, 'ch'), may hold values from -0.15625 to 0.15625
- cotangent: bfloat16 [256, 32768], P('ch', 'brick'), may hold values from -24 to 24
Outputs:
- block_out: bfloat16 [256, 32768], P('ch', 'brick')
- grad_features: bfloat16 [256, 16384], P('ch', 'brick')
- grad_weight_first: bfloat16 [27, 256, 256], P(None, 'ch')
- grad_weight_second: bfloat16 [27, 256, 256], P(None, 'ch')
The draws below stay inside these ranges and needn't reach their ends.
Inputs may be any that keep to these rules, and one draw needn't show every extreme that they name: `owner_map`: among the rows of one scan group, at most 2 are owned by the same brick. `kernel_map`: column 320 means that the neighbour is absent; in the middle offset row, slot i of every brick names column 32 + i.
All inputs are finite; a program needn't handle non-finite values. No bound on the sum of `drop_first` or of `drop_second` on one device may be relied on, other than what follows from the above.
Results may differ from the reference program's by a relative error of at most 0.0064.
Values may be sent and summed in bfloat16 or wider, within the bound.
A program may use at most 64 MiB of HBM per device.

```python
import math
import jax
import jax.numpy as jnp
import numpy as np
from jax import lax

C = 256
KOFF = 27
SCAN_DEV = 128
BRICKS = 128
CAP = 2
SLOTS = 256
HALO = 32
EXT = 320
TOTAL_SLOTS = 32768


def draw_kernel_map(key, part):
    kind_key, inner_key, rim_key, side_key = jax.random.split(key, 4)
    shape = (KOFF, TOTAL_SLOTS)
    kinds = jax.random.randint(kind_key, shape, 0, 20)
    inner = jax.random.randint(inner_key, shape, HALO, HALO + SLOTS)
    border = jax.random.randint(rim_key, shape, 0, HALO)
    sides = jax.random.randint(side_key, shape, 0, 2)
    border = border + sides * (HALO + SLOTS)
    absent = SLOTS + 2 * HALO
    picked = jnp.where(kinds < 6, absent, jnp.where(kinds < 11, inner, border))
    centre = HALO + jnp.arange(TOTAL_SLOTS, dtype=jnp.int32) % SLOTS
    offsets = jnp.arange(KOFF, dtype=jnp.int32)[:, None]
    picked = jnp.where(offsets == KOFF // 2, centre[None, :], picked)
    picked = picked.at[0, 0].set(0)
    picked = picked.at[KOFF - 1, TOTAL_SLOTS - 1].set(absent)
    return picked.astype(jnp.int32)


def set_ends(result, stream_key, smallest, top_value):
    index_at = [jax.random.randint(jax.random.fold_in(stream_key, axis), (), 0, length) for axis, length in enumerate(result.shape)]
    main_axis = result.shape.index(max(result.shape))
    neighbour = index_at[:main_axis] + [(index_at[main_axis] + 1) % result.shape[main_axis]] + index_at[main_axis + 1:]
    return result.at[tuple(index_at)].set(smallest).at[tuple(neighbour)].set(top_value)


def with_spikes(array, stream_key, source, target, blocks, factor):
    owner, partner = [(jnp.arange(array.shape[position]) // (array.shape[position] // blocks)).reshape([-1 if axis == position else 1 for axis in range(array.ndim)]) for position in (source, target)]
    chosen = jax.random.permutation(stream_key, blocks)[partner]
    strong = (owner == chosen) | (owner == (partner + blocks // 2) % blocks)
    return jnp.where(strong, factor * array, array)


def block_levels(key, extent, pieces, low, largest):
    level, own = 1.0, jax.random.fold_in(key, 6)
    for position, blocks in pieces:
        steps = jnp.exp(jax.random.uniform(jax.random.fold_in(own, position), (blocks,), jnp.float32, low / len(pieces), largest / len(pieces)))
        level = level * jnp.repeat(steps, extent[position] // blocks).reshape([-1 if axis == position else 1 for axis in range(len(extent))])
    return level


def deal_out(key, own, number, rows, number_of, top, bound, lean):
    order = jax.random.permutation(key, number_of)
    heavy_load, common = load_shares(number_of, rows * top, bound, lean, True), load_shares(number_of, rows * top, bound, lean, False)
    places = jnp.arange(number_of)

    def named(lengths, turn):
        used = int((lengths > 0).sum())
        fixed = max(1, used // 4)
        shifted = fixed + (places - fixed + turn * (used - fixed)) % max(1, number_of - fixed)
        return jnp.zeros((number_of,), jnp.int32).at[order[jnp.where(places < fixed, places, shifted)]].set(jnp.asarray(lengths, jnp.int32))

    lengths = jnp.where(number % 4 == 0, named(heavy_load, number // 4), named(common, number - number // 4 - 1))
    mixed = jax.random.permutation(jax.random.fold_in(own, 3), number_of)
    donor, sink = mixed[0:number_of // 2 * 2:2], mixed[1:number_of // 2 * 2:2]
    room = jnp.minimum(lengths[donor] - 1, bound - lengths[sink]) // 2
    room = jnp.where((donor == order[0]) | (sink == order[0]) | (lengths[sink] == 0), 0, jnp.maximum(room, 0))
    shifted = jax.random.randint(jax.random.fold_in(own, 4), (number_of // 2,), 0, 1 << 20) % (room + 1)
    lengths = lengths.at[donor].add(-shifted).at[sink].add(shifted)
    items = jnp.searchsorted(jnp.cumsum(lengths), jnp.arange(rows * top), side="right").astype(jnp.int32)
    listing = items.reshape(top, rows).T
    listing = listing[jax.random.permutation(jax.random.fold_in(own, 1), rows)]
    turn = jax.random.randint(jax.random.fold_in(own, 2), (rows, 1), 0, top)
    return jnp.take_along_axis(listing, (jnp.arange(top)[None, :] + turn) % top, axis=1)


def load_shares(amount, total, limit, lean, full):
    weights = [(1 << 20) // math.isqrt(standing ** lean) + 1 for standing in range(1, amount + 1)]
    largest = limit if full else min(limit, max(-(-total // amount), total * weights[0] // sum(weights)))
    least = 1 if total - largest >= amount - 1 else 0
    holding, surplus = [largest] + [least] * (amount - 1), total - largest - least * (amount - 1)
    while surplus > 0:
        candidates = [i for i in range(1, amount) if holding[i] < largest] or [i for i in range(1, amount) if holding[i] < limit]
        mass, remaining = sum([weights[i] for i in candidates]), surplus
        for i in candidates:
            extra = min(limit - holding[i], max(1, remaining * weights[i] // mass), surplus)
            holding[i] = holding[i] + extra
            surplus = surplus - extra
    return np.array(holding)


def normal_values(own_key, dims, deviation, reach, shards=(), held_as=jnp.bfloat16):
    result = jax.random.normal(own_key, dims, jnp.float32) * deviation
    if len(shards) > 0:
        result = block_levels(own_key, dims, shards, -0.22, 0.18) * result
    return jnp.clip(result, min=-reach, max=reach).astype(held_as)


def gaussian_with(own_key, shape, spread, reach, shards, heavy, kind=jnp.bfloat16):
    result = spread * jax.random.normal(own_key, shape, jnp.float32)
    if shards:
        result = result * block_levels(own_key, shape, shards, -0.22, 0.18)
    return jnp.clip(with_spikes(result, jax.random.fold_in(own_key, 3), *heavy), -reach, reach).astype(kind)


def setup_inputs(seed: int = 0) -> dict:
    key_of = jax.random.split(jax.random.key(seed), 10)
    features = normal_values(key_of[0], (C, BRICKS * SCAN_DEV), 1.0, 6.0, ((0, 4), (1, 128)))
    owner_map_keys = jax.random.split(jax.random.fold_in(key_of[1], 1), (BRICKS * SCAN_DEV) // SCAN_DEV)
    owner_map_turns = jax.random.permutation(jax.random.fold_in(key_of[1], 3), (BRICKS * SCAN_DEV) // SCAN_DEV)
    owner_map = jax.vmap(lambda own, number: deal_out(jax.random.fold_in(key_of[1], 2), own, number, SCAN_DEV, BRICKS, 1, CAP, 1))(owner_map_keys, owner_map_turns).reshape((BRICKS * SCAN_DEV, 1))
    kernel_map = draw_kernel_map(jax.random.fold_in(key_of[9], 71), 0)
    send_lists = set_ends(jax.random.randint(key_of[3], (2, BRICKS * HALO), 0, SLOTS), jax.random.fold_in(key_of[3], 1), 0, SLOTS - 1).astype(jnp.int32)
    drop_first = set_ends((jax.random.randint(key_of[4], (C, TOTAL_SLOTS), 0, 10) < 9).astype(jnp.int32), jax.random.fold_in(key_of[4], 1), 0, 1)
    drop_second = set_ends((jax.random.randint(key_of[5], (C, TOTAL_SLOTS), 0, 10) < 9).astype(jnp.int32), jax.random.fold_in(key_of[5], 1), 0, 1)
    weight_first = normal_values(key_of[6], (KOFF, C, C), (KOFF * C // 4) ** -0.5, 0.15625, ((1, 4),))
    weight_second = normal_values(key_of[7], (KOFF, C, C), (KOFF * C // 4) ** -0.5, 0.15625, ((1, 4),))
    cotangent = gaussian_with(key_of[8], (C, TOTAL_SLOTS), 1.0, 24.0, ((0, 4), (1, 128)), (1, 0, 128, 5.5))
    return dict(features=features, owner_map=owner_map, kernel_map=kernel_map, send_lists=send_lists, drop_first=drop_first, drop_second=drop_second, weight_first=weight_first, weight_second=weight_second, cotangent=cotangent)


KEEP_RATE = 0.9


def slope_silu(value):
    sig = jax.nn.sigmoid(value)
    return sig * (1.0 + value * (1.0 - sig))


def relay_slots(owner_map):
    targets = owner_map[:, 0].reshape(BRICKS, SCAN_DEV).astype(jnp.int32)
    matches = (targets[:, :, None] == jnp.arange(BRICKS, dtype=jnp.int32)[None, None, :]).astype(jnp.int32)
    running = jnp.cumsum(matches, axis=1).astype(jnp.int32)
    ordinal = jnp.sum((running - 1) * matches, axis=2).astype(jnp.int32)
    source = jnp.arange(BRICKS, dtype=jnp.int32)[:, None]
    columns = (targets * SLOTS + source * CAP + ordinal).reshape(BRICKS * SCAN_DEV).astype(jnp.int32)
    tallies = jnp.sum(matches, axis=1).astype(jnp.int32)
    occupied = jnp.arange(CAP, dtype=jnp.int32)[None, None, :] < tallies.T[:, :, None]
    return columns, occupied.reshape(TOTAL_SLOTS).astype(jnp.float32)


def select_columns(block, indices):
    return jnp.take(block, indices, axis=1)


def add_columns(block, indices, values):
    return block.at[:, indices].add(values)


def extend(field, send_lists):
    blocks = field.reshape(C, BRICKS, SLOTS).transpose(1, 0, 2)
    to_previous_list = send_lists[0].reshape(BRICKS, HALO)
    to_next_list = send_lists[1].reshape(BRICKS, HALO)
    to_previous = jax.vmap(select_columns)(blocks, to_previous_list)
    to_next = jax.vmap(select_columns)(blocks, to_next_list)
    zero_rim = jnp.zeros((1, C, HALO), field.dtype)
    from_previous = jnp.concatenate([zero_rim, to_next[:-1]], axis=0)
    from_next = jnp.concatenate([to_previous[1:], zero_rim], axis=0)
    return jnp.concatenate([from_previous, blocks, from_next], axis=2)


def convolve(extended, offset_maps, weight):
    weight_full = weight.astype(jnp.float32)

    def single(element):
        brick_ext, brick_map = element
        gathered = jnp.take(brick_ext, brick_map, axis=1, mode="fill", fill_value=0).astype(jnp.float32)
        return jnp.einsum("ckr,kco->or", gathered, weight_full)

    results = lax.map(single, (extended, offset_maps))
    return results.transpose(1, 0, 2).reshape(C, TOTAL_SLOTS)


def transpose_conv(extended, offset_maps, grad, weight):
    grads = grad.reshape(C, BRICKS, SLOTS).transpose(1, 0, 2)
    weight_full = weight.astype(jnp.float32)

    def accumulate(summed_grad, element):
        brick_ext, brick_map, brick_grad = element
        gathered = jnp.take(brick_ext, brick_map, axis=1, mode="fill", fill_value=0).astype(jnp.float32)
        grad_full = brick_grad.astype(jnp.float32)
        summed_grad = summed_grad + jnp.einsum("ckr,or->kco", gathered, grad_full)
        pushed = jnp.einsum("kco,or->ckr", weight_full, grad_full)
        returned = jnp.zeros((C, EXT), jnp.float32).at[:, brick_map].add(pushed, mode="drop")
        return summed_grad, returned

    summed_grad, returned = lax.scan(accumulate, jnp.zeros((KOFF, C, C), jnp.float32), (extended, offset_maps, grads))
    return summed_grad, returned


def fold_back(returned, send_lists):
    to_previous_list = send_lists[0].reshape(BRICKS, HALO)
    to_next_list = send_lists[1].reshape(BRICKS, HALO)
    interior = returned[:, :, HALO:HALO + SLOTS]
    previous_part = returned[:, :, :HALO]
    next_part = returned[:, :, HALO + SLOTS:]
    zero_rim = jnp.zeros((1, C, HALO), jnp.float32)
    from_previous = jnp.concatenate([zero_rim, next_part[:-1]], axis=0)
    from_next = jnp.concatenate([previous_part[1:], zero_rim], axis=0)
    interior = jax.vmap(add_columns)(interior, to_previous_list, from_previous)
    interior = jax.vmap(add_columns)(interior, to_next_list, from_next)
    return interior.transpose(1, 0, 2).reshape(C, TOTAL_SLOTS)


def reference(features, owner_map, kernel_map, send_lists, drop_first, drop_second, weight_first, weight_second, cotangent):
    columns, occupied = relay_slots(owner_map)
    voxels = jnp.zeros((C, TOTAL_SLOTS), jnp.bfloat16).at[:, columns].set(features)
    keep_first = occupied[None, :] * drop_first.astype(jnp.float32) / KEEP_RATE
    keep_second = occupied[None, :] * drop_second.astype(jnp.float32) / KEEP_RATE
    offset_maps = kernel_map.reshape(KOFF, BRICKS, SLOTS).transpose(1, 0, 2)
    extended_voxels = extend(voxels, send_lists)
    conv_first = convolve(extended_voxels, offset_maps, weight_first)
    hidden = (jax.nn.silu(conv_first) * keep_first).astype(jnp.bfloat16)
    extended_hidden = extend(hidden, send_lists)
    conv_second = convolve(extended_hidden, offset_maps, weight_second)
    summed = voxels.astype(jnp.float32) + keep_second * conv_second
    block_out = jax.nn.silu(summed).astype(jnp.bfloat16)
    grad_pre = cotangent.astype(jnp.float32) * slope_silu(summed)
    grad_second = (grad_pre * keep_second).astype(jnp.bfloat16)
    weight_grad_second, returned_second = transpose_conv(extended_hidden, offset_maps, grad_second, weight_second)
    grad_hidden = fold_back(returned_second, send_lists)
    grad_first = (grad_hidden * keep_first * slope_silu(conv_first)).astype(jnp.bfloat16)
    weight_grad_first, returned_first = transpose_conv(extended_voxels, offset_maps, grad_first, weight_first)
    grad_voxels = (grad_pre + fold_back(returned_first, send_lists)).astype(jnp.bfloat16)
    grad_features = jnp.take(grad_voxels, columns, axis=1)
    factor = TOTAL_SLOTS ** -0.5
    return (block_out, grad_features, (weight_grad_first * factor).astype(jnp.bfloat16), (weight_grad_second * factor).astype(jnp.bfloat16))
```

```python
import functools

import jax
import jax.numpy as jnp
from jax import lax
from jax.experimental import pallas as pl
from jax.experimental.pallas import tpu as pltpu
from jax.sharding import PartitionSpec as P

KEEP_RATE = 0.9
MESH = pl.DeviceIdType.MESH
BF = jnp.bfloat16
F32 = jnp.float32
I32 = jnp.int32
CORES = 2
LANE = 128


def dot(a, b):
    return jnp.dot(a, b, preferred_element_type=F32)


def dot_nt(a, b):
    return lax.dot_general(a, b, (((1,), (1,)), ((), ())), preferred_element_type=F32)


def onehot(mask):
    return jnp.where(mask, 1.0, 0.0).astype(BF)


def iota(shape, dim):
    return lax.broadcasted_iota(I32, shape, dim)


def split(value):
    high = value.astype(BF)
    return high, (value - high.astype(F32)).astype(BF)


def slope_silu(value):
    sig = jax.nn.sigmoid(value)
    return sig * (1.0 + value * (1.0 - sig))


def loop(low, high, body):
    def step(index, carry):
        body(index)
        return carry

    lax.fori_loop(low, high, step, 0)


class Swap:
    def __init__(self, n, peer, src, dst, land, sems):
        self.n, self.peer, self.src, self.dst, self.land = n, peer, src, dst, land
        self.ss, self.rs = sems

    def _copy(self, d, src, dst):
        return pltpu.make_async_remote_copy(
            src_ref=src,
            dst_ref=dst,
            send_sem=self.ss.at[d - 1],
            recv_sem=self.rs.at[d - 1],
            device_id=self.peer(d),
            device_id_type=MESH,
        )

    def start(self):
        loop(1, self.n, lambda d: self._copy(d, self.src(d), self.dst(d)).start())

    def wait(self):
        loop(1, self.n, lambda d: self._copy(d, self.land(d), self.land(d)).wait_recv())

    def done(self):
        loop(1, self.n, lambda d: self._copy(d, self.src(d), self.dst(d)).wait_send())


def sizes(bricks, ys, koff, chans, outs):
    zs = bricks // CORES // ys
    rows = koff * chans
    unit = CORES * ys * 16
    padded = -(-rows // unit) * unit
    padded = -(-padded // LANE) * LANE
    half = padded // CORES
    first = half // ys
    second = -(-first // zs // 16) * 16 if first % zs == 0 else -(-first // (16 * zs)) * 16
    return zs, rows, padded, half, first, second


def kernel(
    dims,
    feat,
    owner,
    aux,
    kmap,
    drop1,
    drop2,
    w1,
    w2,
    cot,
    out_ref,
    gf_ref,
    wg1_ref,
    wg2_ref,
    oh,
    wt1,
    wt2,
    tab,
    gath1,
    gath2,
    pushed,
    ret,
    pm,
    em,
    perm,
    a_send,
    a_recv,
    b_send,
    b_recv,
    bb_send,
    bb_recv,
    ba_send,
    ba_recv,
    hs,
    hr,
    fs,
    fr,
    rs_send,
    rs_recv,
    full_g,
    wgf,
    wgb,
    c_recv,
    s1_src,
    s1_ra,
    s1_rb,
    s2_src,
    s2_ra,
    s2_rb,
    fin,
    chunk,
    halves,
    whole,
    *sems,
):
    bricks, ys, zs, chs, koff, chans, rows, padded, half, first, second, scale = dims
    qs = zs * CORES
    b, x = lax.axis_index("brick"), lax.axis_index("ch")
    y, q = b // qs, b % qs
    z, core = q // CORES, q % CORES
    slots = kmap.shape[1]
    sem_at = iter([(sems[i], sems[i + 1]) for i in range(0, len(sems), 2)])

    def ring(count, at, step):
        return lax.rem(at + step, count)

    to_y = lambda d: (ring(ys, y, d) * qs + q, x)
    to_q = lambda d: (y * qs + ring(qs, q, d), x)
    to_z = lambda d: (y * qs + ring(zs, z, d) * CORES + core, x)
    to_core = lambda d: (y * qs + z * CORES + (1 - core), x)
    to_ch = lambda d: (b, ring(chs, x, d))
    to_brick = lambda d: (lax.rem(b + 1 + (d - 1) * (bricks - 2), bricks), x)

    barrier = pltpu.get_barrier_semaphore()
    groups = ((to_y, ys), (to_q, qs), (to_ch, chs), (to_brick, 3))
    for peer, n in groups:
        loop(
            1,
            n,
            lambda d, peer=peer: pl.semaphore_signal(
                barrier, inc=1, device_id=peer(d), device_id_type=MESH
            ),
        )

    prows = 2 * bricks
    t_col, t_row = owner[...], aux[0:1, :]
    scan = t_row.shape[1]
    earlier = (t_col == t_row) & (iota((scan, scan), 0) < iota((scan, scan), 1))
    ordinal = jnp.sum(jnp.where(earlier, 1.0, 0.0), axis=0, keepdims=True)
    code = (t_row // qs) * (2 * qs) + ordinal.astype(I32) * qs + t_row % qs
    pm[...] = onehot(iota((prows, scan), 0) == code)
    carried = jnp.concatenate(
        [feat[...], jnp.where(iota((LANE - chans, scan), 0) == 0, 1.0, 0.0).astype(BF)], axis=0
    )
    a_send[...] = dot_nt(pm[...], carried).astype(BF)

    pl.semaphore_wait(barrier, sum(n - 1 for _, n in groups))

    def chunk_of(ref, index, size):
        return ref.at[pl.ds(pl.multiple_of(index * size, size), size)]

    ya, qa = 2 * qs, 2 * ys
    swap_a = Swap(
        ys,
        to_y,
        lambda d: chunk_of(a_send, ring(ys, y, d), ya),
        lambda d: chunk_of(a_recv, y, ya),
        lambda d: chunk_of(a_recv, ring(ys, y, ys - d), ya),
        next(sem_at),
    )
    swap_b = Swap(
        qs,
        to_q,
        lambda d: chunk_of(b_send, ring(qs, q, d), qa),
        lambda d: chunk_of(b_recv, q, qa),
        lambda d: chunk_of(b_recv, ring(qs, q, qs - d), qa),
        next(sem_at),
    )
    back_b = Swap(
        qs,
        to_q,
        lambda d: chunk_of(bb_send, ring(qs, q, d), qa),
        lambda d: chunk_of(bb_recv, q, qa),
        lambda d: chunk_of(bb_recv, ring(qs, q, qs - d), qa),
        next(sem_at),
    )
    back_a = Swap(
        ys,
        to_y,
        lambda d: chunk_of(ba_send, ring(ys, y, d), ya),
        lambda d: chunk_of(ba_recv, y, ya),
        lambda d: chunk_of(ba_recv, ring(ys, y, ys - d), ya),
        next(sem_at),
    )

    def neighbours(send, recv, at):
        return Swap(
            3,
            to_brick,
            lambda d: send.at[at, d - 1],
            lambda d: recv.at[at, d - 1],
            lambda d: recv.at[at, d - 1],
            next(sem_at),
        )

    halo1, halo2 = neighbours(hs, hr, 0), neighbours(hs, hr, 1)
    fold2, fold1 = neighbours(fs, fr, 0), neighbours(fs, fr, 1)

    def scatter_sum(at):
        return Swap(
            chs,
            to_ch,
            lambda d: chunk_of(rs_send.at[at], ring(chs, x, d), chans),
            lambda d: rs_recv.at[at, d - 1],
            lambda d: rs_recv.at[at, d - 1],
            next(sem_at),
        )

    sum1, sum2 = scatter_sum(0), scatter_sum(1)

    def share(at):
        return Swap(
            chs,
            to_ch,
            lambda d: chunk_of(full_g.at[at], x, chans),
            lambda d: chunk_of(full_g.at[at], x, chans),
            lambda d: chunk_of(full_g.at[at], ring(chs, x, chs - d), chans),
            next(sem_at),
        )

    share2, share1 = share(0), share(1)

    left, right = pl.ds(0, LANE), pl.ds(LANE, LANE)

    def rows_of(ref, start, size, lanes):
        return ref.at[pl.ds(pl.multiple_of(start, 16), size), lanes]

    def second_at(index):
        return jnp.minimum(index * second, first - second)

    class Total:
        def __init__(self, at):
            self.at = at
            other = (1 - core) * half
            self.cores = Swap(
                2,
                to_core,
                lambda d: wgb.at[at, pl.ds(pl.multiple_of(other, 16), half)],
                lambda d: c_recv.at[at],
                lambda d: c_recv.at[at],
                next(sem_at),
            )
            src = s1_src.at[at]
            self.first = (
                Swap(
                    ys,
                    to_y,
                    lambda d: rows_of(src, ring(ys, y, d) * first, first, left),
                    lambda d: s1_ra.at[at, d - 1],
                    lambda d: s1_ra.at[at, d - 1],
                    next(sem_at),
                ),
                Swap(
                    zs,
                    to_z,
                    lambda d: rows_of(src, ring(zs, z, d) * first, first, right),
                    lambda d: s1_rb.at[at, d - 1],
                    lambda d: s1_rb.at[at, d - 1],
                    next(sem_at),
                ),
            )
            self.second = (
                Swap(
                    zs,
                    to_z,
                    lambda d: s2_src.at[at, 0, pl.ds(pl.multiple_of(second_at(ring(zs, z, d)), 16), second)],
                    lambda d: s2_ra.at[at, d - 1],
                    lambda d: s2_ra.at[at, d - 1],
                    next(sem_at),
                ),
                Swap(
                    ys,
                    to_y,
                    lambda d: s2_src.at[at, 1, pl.ds(pl.multiple_of(second_at(ring(ys, y, d)), 16), second)],
                    lambda d: s2_rb.at[at, d - 1],
                    lambda d: s2_rb.at[at, d - 1],
                    next(sem_at),
                ),
            )
            self.third = (
                Swap(
                    zs,
                    to_z,
                    lambda d: fin.at[at, 0],
                    lambda d: chunk_of(chunk.at[at, 0], z, second),
                    lambda d: chunk_of(chunk.at[at, 0], ring(zs, z, zs - d), second),
                    next(sem_at),
                ),
                Swap(
                    ys,
                    to_y,
                    lambda d: fin.at[at, 1],
                    lambda d: chunk_of(chunk.at[at, 1], y, second),
                    lambda d: chunk_of(chunk.at[at, 1], ring(ys, y, ys - d), second),
                    next(sem_at),
                ),
            )
            dst = halves.at[at]
            self.fourth = (
                Swap(
                    ys,
                    to_y,
                    lambda d: chunk.at[at, 0, pl.ds(0, first)],
                    lambda d: rows_of(dst, y * first, first, left),
                    lambda d: rows_of(dst, ring(ys, y, ys - d) * first, first, left),
                    next(sem_at),
                ),
                Swap(
                    zs,
                    to_z,
                    lambda d: chunk.at[at, 1, pl.ds(0, first)],
                    lambda d: rows_of(dst, z * first, first, right),
                    lambda d: rows_of(dst, ring(zs, z, zs - d) * first, first, right),
                    next(sem_at),
                ),
            )
            self.last = Swap(
                2,
                to_core,
                lambda d: halves.at[at],
                lambda d: whole.at[at],
                lambda d: whole.at[at],
                next(sem_at),
            )
            self.all = (self.cores, *self.first, *self.second, *self.third, *self.fourth, self.last)

        def compute(self, gath, grads):
            at, block = self.at, half // 2
            g = grads[...]

            def step(i):
                span = pl.ds(pl.multiple_of(i * block, 16), block)
                part = dot_nt(gath[span, :], g)
                wgf[at, span, :] = part
                wgb[at, span, :] = part.astype(BF)

            loop(0, 2 * CORES, step)
            self.cores.start()

        def to_first(self):
            self.cores.wait()
            own = wgf[self.at, pl.ds(pl.multiple_of(core * half, 16), half), :]
            both = own + c_recv[self.at].astype(F32)
            s1_src[self.at] = both.astype(BF)
            for swap in self.first:
                swap.start()

        def to_second(self):
            for side, (swap, recv, pos, lanes, n) in enumerate(
                zip(self.first, (s1_ra, s1_rb), (y, z), (left, right), (ys, zs))
            ):
                swap.wait()
                span = pl.ds(pl.multiple_of(pos * first, 16), first)
                total = s1_src[self.at, span, lanes].astype(F32)
                for d in range(n - 1):
                    total = total + recv[self.at, d].astype(F32)
                s2_src[self.at, side] = total
                self.second[side].start()

        def to_third(self):
            for side, (swap, recv, pos, n) in enumerate(
                zip(self.second, (s2_ra, s2_rb), (z, y), (zs, ys))
            ):
                swap.wait()
                span = pl.ds(pl.multiple_of(second_at(pos), 16), second)
                total = s2_src[self.at, side, span, :]
                for d in range(n - 1):
                    total = total + recv[self.at, d]
                done = (total * scale).astype(BF)
                fin[self.at, side] = done
                chunk[self.at, side, pl.ds(pl.multiple_of(pos * second, 16), second), :] = done
                self.third[side].start()

        def to_fourth(self):
            for side, (swap, pos, lanes) in enumerate(zip(self.third, (y, z), (left, right))):
                swap.wait()
                self.fourth[side].start()
                span = pl.ds(pl.multiple_of(pos * first, 16), first)
                halves[self.at, span, lanes] = chunk[self.at, side, pl.ds(0, first), :]

        def to_last(self):
            for swap in self.fourth:
                swap.wait()
            self.last.start()

        def finish(self, ref):
            mine, theirs = halves[self.at], None
            self.last.wait()
            theirs = whole[self.at]
            upper = rows - half
            ref[0:half, :] = jnp.where(core == 0, mine, theirs)
            ref[half:rows, :] = jnp.where(core == 0, theirs, mine)[0:upper]

    total2, total1 = Total(0), Total(1)

    def own_rows(src, dst, index, size):
        span = pl.ds(pl.multiple_of(index * size, size), size)
        dst[span, :] = src[span, :]

    swap_a.start()
    own_rows(a_send, a_recv, y, ya)

    pr, pc = iota((prows, prows), 0), iota((prows, prows), 1)
    perm[...] = onehot(pc == (pr % ys) * ya + ((pr // ys) % 2) * qs + pr // qa)
    er, ec = iota((prows, slots), 0), iota((prows, slots), 1)
    em[...] = onehot(ec == 2 * ((er % ys) * qs + er // qa) + (er // ys) % 2)

    rim = 32

    def build(k):
        row = kmap[pl.ds(k, 1), :]
        inner = jnp.where(row < rim + slots, row - rim, row)
        column = jnp.where(row < rim, row + slots, jnp.where(row >= slots + 2 * rim, -1, inner))
        oh[k] = onehot(iota(oh.shape[1:], 0) == column)

    loop(0, koff // 3, build)

    swap_a.wait()
    b_send[...] = dot(perm[...], a_recv[...]).astype(BF)
    swap_b.start()
    own_rows(b_send, b_recv, q, qa)

    loop(koff // 3, koff, build)

    def turn(source, target):
        blocks = rows // LANE

        def step(j):
            at = pl.multiple_of(j * LANE, LANE)
            target[:, pl.ds(at, LANE)] = source[pl.ds(at, LANE), :].astype(F32).T.astype(BF)

        loop(0, blocks, step)
        if rows % LANE:
            tail = source[blocks * LANE : rows, :].astype(F32)
            tail = jnp.concatenate([tail, jnp.zeros((LANE - rows % LANE, tail.shape[1]), F32)], 0)
            target[:, blocks * LANE : (blocks + 1) * LANE] = tail.T.astype(BF)

    turn(w1, wt1)
    turn(w2, wt2)
    for gath in (gath1, gath2):
        gath[rows:padded, :] = jnp.zeros((padded - rows, slots), BF)

    lent = iota((slots, LANE), 0) == aux[1:2, :]
    side = iota((slots, LANE), 1) < rim
    lend_next, lend_prev = onehot(lent & side), onehot(lent & ~side)
    has_prev = (b > 0).astype(F32)
    has_next = (b < bricks - 1).astype(F32)

    swap_b.wait()
    arrived = dot(b_recv[...].astype(F32).T.astype(BF), em[...])
    occupied = arrived[chans : chans + 1, :]
    voxels = arrived[0:chans, :].astype(BF)
    keep1 = occupied * drop1[...].astype(F32) / KEEP_RATE
    keep2 = occupied * drop2[...].astype(F32) / KEEP_RATE

    def lend(field, halo, at):
        hs[at, 0] = dot(field, lend_next).astype(BF)
        hs[at, 1] = dot(field, lend_prev).astype(BF)
        halo.start()
        tab[:, 0:slots] = field

    def convolve(halo, at, gath, wt, summing):
        halo.wait()
        edge = hr[at, 0].astype(F32) * has_prev + hr[at, 1].astype(F32) * has_next
        tab[:, slots : slots + LANE] = edge.astype(BF)
        table = tab[...]

        def step(k):
            gath[pl.ds(pl.multiple_of(k * chans, 16), chans), :] = dot(table, oh[k]).astype(BF)

        loop(0, koff, step)
        rs_send[at] = dot(wt[...], gath[...])
        summing.start()
        own = rs_send[at, pl.ds(pl.multiple_of(x * chans, 16), chans), :]
        summing.wait()
        for d in range(chs - 1):
            own = own + rs_recv[at, d]
        return own

    lend(voxels, halo1, 0)
    conv1 = convolve(halo1, 0, gath1, wt1, sum1)
    hidden = (conv1 * jax.nn.sigmoid(conv1) * keep1).astype(BF)
    lend(hidden, halo2, 1)
    conv2 = convolve(halo2, 1, gath2, wt2, sum2)
    summed = voxels.astype(F32) + keep2 * conv2
    grad_pre = cot[...].astype(F32) * slope_silu(summed)
    mine = pl.ds(pl.multiple_of(x * chans, 16), chans)
    full_g[0, mine, :] = (grad_pre * keep2).astype(BF)
    share2.start()
    out_ref[...] = (summed * jax.nn.sigmoid(summed)).astype(BF)

    def push(weight, grads, fold, at):
        g = grads[...]

        def ahead(j):
            span = pl.ds(pl.multiple_of(j * 3 * chans, 16), 3 * chans)
            high, low = split(dot(weight[span, :], g))
            for i in range(3):
                part = slice(i * chans, (i + 1) * chans)
                pushed[3 * j + i, 0:chans, :] = high[part]
                pushed[3 * j + i, chans : 2 * chans, :] = low[part]

        loop(0, koff // 3, ahead)
        ret[...] = jnp.zeros_like(ret)

        def step(k):
            ret[...] += dot_nt(pushed[k], oh[k])

        loop(0, koff, step)
        border = ret[0:chans, slots : slots + LANE] + ret[chans : 2 * chans, slots : slots + LANE]
        fs[at, 0] = border
        fs[at, 1] = border
        fold.start()

    def folded(fold, at):
        own = ret[0:chans, 0:slots] + ret[chans : 2 * chans, 0:slots]
        fold.wait()
        for part in split(fr[at, 0] * has_prev):
            own = own + dot_nt(part, lend_prev)
        for part in split(fr[at, 1] * has_next):
            own = own + dot_nt(part, lend_next)
        return own

    share2.wait()
    push(w2, full_g.at[0], fold2, 0)
    total2.compute(gath2, full_g.at[0])
    grad_hidden = folded(fold2, 0)
    full_g[1, mine, :] = (grad_hidden * keep1 * slope_silu(conv1)).astype(BF)
    share1.start()
    total2.to_first()
    share1.wait()
    push(w1, full_g.at[1], fold1, 1)
    total1.compute(gath1, full_g.at[1])
    grad_voxels = (grad_pre + folded(fold1, 1)).astype(BF)
    wide = jnp.concatenate([grad_voxels, jnp.zeros((LANE - chans, slots), BF)], axis=0)
    bb_send[...] = dot_nt(em[...], wide).astype(BF)
    back_b.start()
    own_rows(bb_send, bb_recv, q, qa)
    total1.to_first()
    back_b.wait()
    perm_back = onehot(pc == (pr % qs) * qa + ((pr // qs) % 2) * ys + pr // ya)
    ba_send[...] = dot(perm_back, bb_recv[...]).astype(BF)
    back_a.start()
    own_rows(ba_send, ba_recv, y, ya)
    total2.to_second()
    back_a.wait()
    gf = dot(ba_recv[...].astype(F32).T.astype(BF), pm[...])
    gf_ref[...] = gf[0:chans, :].astype(BF)
    total1.to_second()
    total2.to_third()
    total1.to_third()
    total2.to_fourth()
    total1.to_fourth()
    total2.to_last()
    total1.to_last()
    total2.finish(wg2_ref)
    total1.finish(wg1_ref)

    for swap in (
        swap_a,
        swap_b,
        back_b,
        back_a,
        halo1,
        halo2,
        fold2,
        fold1,
        sum1,
        sum2,
        share2,
        share1,
        *total2.all,
        *total1.all,
    ):
        swap.done()


def local(ys, features, owner_map, kernel_map, send_lists, drop1, drop2, w1, w2, cotangent):
    bricks, chs = lax.axis_size("brick"), lax.axis_size("ch")
    chans, scan = features.shape
    koff, slots = kernel_map.shape
    outs = w1.shape[2]
    zs, rows, padded, half, first, second = sizes(bricks, ys, koff, chans, outs)
    qs = zs * CORES
    rim = send_lists.shape[1]
    dims = (
        bricks, ys, zs, chs, koff, chans, rows, padded, half, first, second,
        float(bricks * slots) ** -0.5,
    )
    lists = jnp.concatenate(
        [send_lists[1:2], send_lists[0:1], jnp.full((1, LANE - 2 * rim), -1, I32)], axis=1
    )
    aux = jnp.concatenate([owner_map.reshape(1, scan), lists], axis=0)
    prows = 2 * bricks
    vm = pltpu.VMEM
    table = slots + LANE
    scratch = [
        vm((koff, table, slots), BF),
        vm((outs, padded), BF),
        vm((outs, padded), BF),
        vm((chans, table), BF),
        vm((padded, slots), BF),
        vm((padded, slots), BF),
        vm((koff, 2 * chans, slots), BF),
        vm((2 * chans, table), F32),
        vm((prows, scan), BF),
        vm((prows, slots), BF),
        vm((prows, prows), BF),
        *[vm((prows, LANE), BF)] * 8,
        vm((2, 2, chans, LANE), BF),
        vm((2, 2, chans, LANE), BF),
        vm((2, 2, chans, LANE), F32),
        vm((2, 2, chans, LANE), F32),
        vm((2, outs, slots), F32),
        vm((2, chs - 1, chans, slots), F32),
        vm((2, outs, slots), BF),
        vm((2, padded, outs), F32),
        vm((2, padded, outs), BF),
        vm((2, half, outs), BF),
        vm((2, half, outs), BF),
        vm((2, ys - 1, first, LANE), BF),
        vm((2, zs - 1, first, LANE), BF),
        vm((2, 2, first, LANE), F32),
        vm((2, zs - 1, second, LANE), F32),
        vm((2, ys - 1, second, LANE), F32),
        vm((2, 2, second, LANE), BF),
        vm((2, 2, max(ys, zs) * second, LANE), BF),
        vm((2, half, outs), BF),
        vm((2, half, outs), BF),
    ]
    weight_sums = [1, ys - 1, zs - 1, zs - 1, ys - 1, zs - 1, ys - 1, ys - 1, zs - 1, 1]
    copies = [ys - 1, qs - 1, qs - 1, ys - 1, 2, 2, 2, 2] + [chs - 1] * 4 + weight_sums * 2
    for n in copies:
        scratch += [pltpu.SemaphoreType.DMA((n,))] * 2
    shape = jax.ShapeDtypeStruct
    spec = pl.BlockSpec(memory_space=pltpu.VMEM)
    block_out, grad_features, wg1, wg2 = pl.pallas_call(
        functools.partial(kernel, dims),
        out_shape=(
            shape((chans, slots), BF),
            shape((chans, scan), BF),
            shape((rows, outs), BF),
            shape((rows, outs), BF),
        ),
        in_specs=[spec] * 9,
        out_specs=(spec,) * 4,
        scratch_shapes=scratch,
        compiler_params=pltpu.CompilerParams(
            collective_id=0, has_side_effects=True, vmem_limit_bytes=56 * 2**20
        ),
        name="block",
    )(
        features, owner_map, aux, kernel_map, drop1, drop2,
        w1.reshape(rows, outs), w2.reshape(rows, outs), cotangent,
    )
    return block_out, grad_features, wg1.reshape(w1.shape), wg2.reshape(w2.shape)


def rows_of_chips(bricks):
    ys = 1
    while ys * ys * CORES < bricks:
        ys *= 2
    return ys


def solution(mesh):
    return jax.shard_map(
        functools.partial(local, rows_of_chips(mesh.shape["brick"])),
        mesh=mesh,
        in_specs=(
            P("ch", "brick"),
            P("brick", None),
            P(None, "brick"),
            P(None, "brick"),
            P("ch", "brick"),
            P("ch", "brick"),
            P(None, "ch", None),
            P(None, "ch", None),
            P("ch", "brick"),
        ),
        out_specs=(P("ch", "brick"), P("ch", "brick"), P(None, "ch", None), P(None, "ch", None)),
        check_vma=False,
    )
```

```python
import functools

import jax
import jax.numpy as jnp
from jax import lax
from jax.experimental import pallas as pl
from jax.experimental.pallas import tpu as pltpu
from jax.sharding import PartitionSpec as P

KEEP_RATE = 0.9
MESH = pl.DeviceIdType.MESH
BF = jnp.bfloat16
F32 = jnp.float32
I32 = jnp.int32
CORES = 2
LANE = 128


def dot(a, b):
    return jnp.dot(a, b, preferred_element_type=F32)


def dot_nt(a, b):
    return lax.dot_general(a, b, (((1,), (1,)), ((), ())), preferred_element_type=F32)


def onehot(mask):
    return jnp.where(mask, 1.0, 0.0).astype(BF)


def iota(shape, dim):
    return lax.broadcasted_iota(I32, shape, dim)


def split(value):
    high = value.astype(BF)
    return high, (value - high.astype(F32)).astype(BF)


def slope_silu(value):
    sig = jax.nn.sigmoid(value)
    return sig * (1.0 + value * (1.0 - sig))


def loop(low, high, body):
    def step(index, carry):
        body(index)
        return carry

    lax.fori_loop(low, high, step, 0)


def unrolled(low, high, body):
    for index in range(low, high):
        body(index)


class Swap:
    def __init__(self, n, peer, src, dst, land, sems):
        self.n, self.peer, self.src, self.dst, self.land = n, peer, src, dst, land
        self.ss, self.rs = sems

    def _copy(self, d, src, dst):
        return pltpu.make_async_remote_copy(
            src_ref=src,
            dst_ref=dst,
            send_sem=self.ss.at[d - 1],
            recv_sem=self.rs.at[d - 1],
            device_id=self.peer(d),
            device_id_type=MESH,
        )

    def start_one(self, d):
        self._copy(d, self.src(d), self.dst(d)).start()

    def wait_one(self, d):
        self._copy(d, self.land(d), self.land(d)).wait_recv()

    def start(self):
        loop(1, self.n, self.start_one)

    def wait(self):
        loop(1, self.n, self.wait_one)

    def done(self):
        loop(1, self.n, lambda d: self._copy(d, self.src(d), self.dst(d)).wait_send())


def sizes(bricks, ys, koff, chans, outs):
    zs = bricks // CORES // ys
    rows = koff * chans
    unit = CORES * ys * 16
    padded = -(-rows // unit) * unit
    padded = -(-padded // LANE) * LANE
    half = padded // CORES
    first = half // ys
    second = -(-first // zs // 16) * 16 if first % zs == 0 else -(-first // (16 * zs)) * 16
    return zs, rows, padded, half, first, second


def kernel(
    dims,
    feat,
    owner,
    lists,
    kmap,
    drop1,
    drop2,
    w1,
    w2,
    cot,
    out_ref,
    gf_ref,
    wg1_ref,
    wg2_ref,
    oh,
    wt1,
    wt2,
    tab,
    gath1,
    gath2,
    pushed,
    ret,
    pm,
    em,
    perm,
    a_send,
    a_recv,
    b_send,
    b_recv,
    bb_send,
    bb_recv,
    ba_send,
    ba_recv,
    hs,
    hr,
    fs,
    fr,
    rs_send,
    rs_recv,
    full_g,
    wgf,
    wgb,
    c_recv,
    s1_src,
    s1_ra,
    s1_rb,
    s2_src,
    s2_ra,
    s2_rb,
    fin,
    chunk,
    *sems,
):
    bricks, ys, zs, chs, koff, chans, rows, padded, half, first, second, scale = dims
    qs = zs * CORES
    b, x = lax.axis_index("brick"), lax.axis_index("ch")
    y, q = b // qs, b % qs
    z, core = q // CORES, q % CORES
    slots = kmap.shape[1]
    sem_at = iter([(sems[i], sems[i + 1]) for i in range(0, len(sems), 2)])

    def ring(count, at, step):
        return lax.rem(at + step, count)

    to_y = lambda d: (ring(ys, y, d) * qs + q, x)
    to_q = lambda d: (y * qs + ring(qs, q, d), x)
    to_z = lambda d: (y * qs + ring(zs, z, d) * CORES + core, x)
    to_core = lambda d: (y * qs + z * CORES + (1 - core), x)
    to_ch = lambda d: (b, ring(chs, x, d))
    to_brick = lambda d: (lax.rem(b + 1 + (d - 1) * (bricks - 2), bricks), x)

    barrier = pltpu.get_barrier_semaphore()
    groups = ((to_y, ys), (to_q, qs), (to_ch, chs), (to_brick, 3))
    for peer, n in groups:
        loop(
            1,
            n,
            lambda d, peer=peer: pl.semaphore_signal(
                barrier, inc=1, device_id=peer(d), device_id_type=MESH
            ),
        )

    prows = 2 * bricks
    t_row = owner[...]
    scan = t_row.shape[1]
    t_col = jnp.broadcast_to(t_row.astype(F32), (scan, scan)).T.astype(I32)
    earlier = (t_col == t_row) & (iota((scan, scan), 0) < iota((scan, scan), 1))
    ordinal = jnp.sum(jnp.where(earlier, 1.0, 0.0), axis=0, keepdims=True)
    code = (t_row // qs) * (2 * qs) + ordinal.astype(I32) * qs + t_row % qs
    pm[...] = onehot(iota((prows, scan), 0) == code)
    carried = jnp.concatenate(
        [feat[...], jnp.where(iota((LANE - chans, scan), 0) == 0, 1.0, 0.0).astype(BF)], axis=0
    )
    a_send[...] = dot_nt(pm[...], carried).astype(BF)

    pl.semaphore_wait(barrier, sum(n - 1 for _, n in groups))

    def chunk_of(ref, index, size):
        return ref.at[pl.ds(pl.multiple_of(index * size, size), size)]

    ya, qa = 2 * qs, 2 * ys
    swap_a = Swap(
        ys,
        to_y,
        lambda d: chunk_of(a_send, ring(ys, y, d), ya),
        lambda d: chunk_of(a_recv, y, ya),
        lambda d: chunk_of(a_recv, ring(ys, y, ys - d), ya),
        next(sem_at),
    )
    swap_b = Swap(
        qs,
        to_q,
        lambda d: chunk_of(b_send, ring(qs, q, d), qa),
        lambda d: chunk_of(b_recv, q, qa),
        lambda d: chunk_of(b_recv, ring(qs, q, qs - d), qa),
        next(sem_at),
    )
    back_b = Swap(
        qs,
        to_q,
        lambda d: chunk_of(bb_send, ring(qs, q, d), qa),
        lambda d: chunk_of(bb_recv, q, qa),
        lambda d: chunk_of(bb_recv, ring(qs, q, qs - d), qa),
        next(sem_at),
    )
    back_a = Swap(
        ys,
        to_y,
        lambda d: chunk_of(ba_send, ring(ys, y, d), ya),
        lambda d: chunk_of(ba_recv, y, ya),
        lambda d: chunk_of(ba_recv, ring(ys, y, ys - d), ya),
        next(sem_at),
    )

    def neighbours(send, recv, at):
        return Swap(
            3,
            to_brick,
            lambda d: send.at[at, d - 1],
            lambda d: recv.at[at, d - 1],
            lambda d: recv.at[at, d - 1],
            next(sem_at),
        )

    halo1, halo2 = neighbours(hs, hr, 0), neighbours(hs, hr, 1)
    fold2, fold1 = neighbours(fs, fr, 0), neighbours(fs, fr, 1)

    def scatter_sum(at):
        return Swap(
            chs,
            to_ch,
            lambda d: chunk_of(rs_send.at[at], ring(chs, x, d), chans),
            lambda d: rs_recv.at[at, d - 1],
            lambda d: rs_recv.at[at, d - 1],
            next(sem_at),
        )

    sum1, sum2 = scatter_sum(0), scatter_sum(1)

    def share(at):
        return Swap(
            chs,
            to_ch,
            lambda d: chunk_of(full_g.at[at], x, chans),
            lambda d: chunk_of(full_g.at[at], x, chans),
            lambda d: chunk_of(full_g.at[at], ring(chs, x, chs - d), chans),
            next(sem_at),
        )

    share2, share1 = share(0), share(1)

    left, right = pl.ds(0, LANE), pl.ds(LANE, LANE)

    def rows_of(ref, start, size, lanes):
        return ref.at[pl.ds(pl.multiple_of(start, 16), size), lanes]

    def second_at(index):
        return jnp.minimum(index * second, first - second)

    class Total:
        def __init__(self, at, ref):
            self.at, self.ref = at, ref
            self.cores = Swap(
                2,
                to_core,
                lambda d: wgb.at[at],
                lambda d: c_recv.at[at],
                lambda d: c_recv.at[at],
                next(sem_at),
            )
            src = s1_src.at[at]
            self.first = (
                Swap(
                    ys,
                    to_y,
                    lambda d: rows_of(src, ring(ys, y, d) * first, first, left),
                    lambda d: s1_ra.at[at, d - 1],
                    lambda d: s1_ra.at[at, d - 1],
                    next(sem_at),
                ),
                Swap(
                    zs,
                    to_z,
                    lambda d: rows_of(src, ring(zs, z, d) * first, first, right),
                    lambda d: s1_rb.at[at, d - 1],
                    lambda d: s1_rb.at[at, d - 1],
                    next(sem_at),
                ),
            )
            self.second = (
                Swap(
                    zs,
                    to_z,
                    lambda d: s2_src.at[at, 0, pl.ds(pl.multiple_of(second_at(ring(zs, z, d)), 16), second)],
                    lambda d: s2_ra.at[at, d - 1],
                    lambda d: s2_ra.at[at, d - 1],
                    next(sem_at),
                ),
                Swap(
                    ys,
                    to_y,
                    lambda d: s2_src.at[at, 1, pl.ds(pl.multiple_of(second_at(ring(ys, y, d)), 16), second)],
                    lambda d: s2_rb.at[at, d - 1],
                    lambda d: s2_rb.at[at, d - 1],
                    next(sem_at),
                ),
            )
            self.third = (
                Swap(
                    zs,
                    to_z,
                    lambda d: fin.at[at, 0],
                    lambda d: chunk_of(chunk.at[at, 0], z, second),
                    lambda d: chunk_of(chunk.at[at, 0], ring(zs, z, zs - d), second),
                    next(sem_at),
                ),
                Swap(
                    ys,
                    to_y,
                    lambda d: fin.at[at, 1],
                    lambda d: chunk_of(chunk.at[at, 1], y, second),
                    lambda d: chunk_of(chunk.at[at, 1], ring(ys, y, ys - d), second),
                    next(sem_at),
                ),
            )
            self.fourth = (
                Swap(
                    ys,
                    to_y,
                    lambda d: chunk.at[at, 0, pl.ds(0, first)],
                    lambda d: rows_of(ref, core * half + y * first, first, left),
                    lambda d: rows_of(ref, core * half + ring(ys, y, ys - d) * first, first, left),
                    next(sem_at),
                ),
                Swap(
                    zs,
                    to_z,
                    lambda d: chunk.at[at, 1, pl.ds(0, first)],
                    lambda d: rows_of(ref, core * half + z * first, first, right),
                    lambda d: rows_of(ref, core * half + ring(zs, z, zs - d) * first, first, right),
                    next(sem_at),
                ),
            )
            self.last = tuple(
                Swap(
                    n + 1,
                    lambda d: to_core(1),
                    lambda d, n=n, pos=pos, lanes=lanes: rows_of(
                        ref, core * half + ring(n, pos, n + 1 - d) * first, first, lanes
                    ),
                    lambda d, n=n, pos=pos, lanes=lanes: rows_of(
                        ref, core * half + ring(n, pos, n + 1 - d) * first, first, lanes
                    ),
                    lambda d, n=n, pos=pos, lanes=lanes: rows_of(
                        ref, (1 - core) * half + ring(n, pos, n + 1 - d) * first, first, lanes
                    ),
                    next(sem_at),
                )
                for n, pos, lanes in ((ys, y, left), (zs, z, right))
            )
            self.all = (
                self.cores, *self.first, *self.second, *self.third, *self.fourth, *self.last
            )

        def compute(self, gath, grads):
            at, g, block = self.at, grads[...], half // 2

            def step(start, keep):
                span = pl.ds(pl.multiple_of(start, 16), block)
                part = dot_nt(gath[span, :], g)
                if keep:
                    wgf[at, pl.ds(pl.multiple_of(start - core * half, 16), block), :] = part
                else:
                    at_b = pl.ds(pl.multiple_of(start - (1 - core) * half, 16), block)
                    wgb[at, at_b, :] = part.astype(BF)

            for i in range(2):
                step((1 - core) * half + i * block, False)
            self.cores.start()
            for i in range(2):
                step(core * half + i * block, True)

        def to_first(self):
            self.cores.wait()
            both = wgf[self.at] + c_recv[self.at].astype(F32)
            s1_src[self.at] = both.astype(BF)
            for swap in self.first:
                swap.start()

        def to_second(self):
            for side, (swap, recv, pos, lanes, n) in enumerate(
                zip(self.first, (s1_ra, s1_rb), (y, z), (left, right), (ys, zs))
            ):
                swap.wait()
                span = pl.ds(pl.multiple_of(pos * first, 16), first)
                total = s1_src[self.at, span, lanes].astype(F32)
                for d in range(n - 1):
                    total = total + recv[self.at, d].astype(F32)
                s2_src[self.at, side] = total
                self.second[side].start()

        def to_third(self):
            for side, (swap, recv, pos, n) in enumerate(
                zip(self.second, (s2_ra, s2_rb), (z, y), (zs, ys))
            ):
                swap.wait()
                span = pl.ds(pl.multiple_of(second_at(pos), 16), second)
                total = s2_src[self.at, side, span, :]
                for d in range(n - 1):
                    total = total + recv[self.at, d]
                done = (total * scale).astype(BF)
                fin[self.at, side] = done
                chunk[self.at, side, pl.ds(pl.multiple_of(pos * second, 16), second), :] = done
                self.third[side].start()

        def to_fourth(self):
            for side, (swap, pos, lanes) in enumerate(zip(self.third, (y, z), (left, right))):
                swap.wait()
                self.fourth[side].start()
                span = pl.ds(pl.multiple_of(core * half + pos * first, 16), first)
                self.ref[span, lanes] = chunk[self.at, side, pl.ds(0, first), :]
                self.last[side].start_one(1)

        def to_last(self):
            for side, swap in enumerate(self.fourth):

                def forward(d, swap=swap, side=side):
                    swap.wait_one(d)
                    self.last[side].start_one(d + 1)

                loop(1, swap.n, forward)

        def finish(self):
            for swap in self.last:
                swap.wait()

    total2, total1 = Total(0, wg2_ref), Total(1, wg1_ref)

    def own_rows(src, dst, index, size):
        span = pl.ds(pl.multiple_of(index * size, size), size)
        dst[span, :] = src[span, :]

    swap_a.start()
    own_rows(a_send, a_recv, y, ya)

    pr, pc = iota((prows, prows), 0), iota((prows, prows), 1)
    perm[...] = onehot(pc == (pr % ys) * ya + ((pr // ys) % 2) * qs + pr // qa)
    er, ec = iota((prows, slots), 0), iota((prows, slots), 1)
    em[...] = onehot(ec == 2 * ((er % ys) * qs + er // qa) + (er // ys) % 2)

    rim = 32

    def build(k):
        row = kmap[pl.ds(k, 1), :]
        inner = jnp.where(row < rim + slots, row - rim, row)
        column = jnp.where(row < rim, row + slots, jnp.where(row >= slots + 2 * rim, -1, inner))
        oh[k] = onehot(iota(oh.shape[1:], 0) == column)

    unrolled(0, koff // 3, build)

    swap_a.wait()
    b_send[...] = dot(perm[...], a_recv[...]).astype(BF)
    swap_b.start()
    own_rows(b_send, b_recv, q, qa)

    unrolled(koff // 3, koff, build)

    def turn(source, target):
        blocks = rows // LANE

        def step(j):
            at = pl.multiple_of(j * LANE, LANE)
            target[:, pl.ds(at, LANE)] = source[pl.ds(at, LANE), :].astype(F32).T.astype(BF)

        unrolled(0, blocks, step)
        if rows % LANE:
            tail = source[blocks * LANE : rows, :].astype(F32)
            tail = jnp.concatenate([tail, jnp.zeros((LANE - rows % LANE, tail.shape[1]), F32)], 0)
            target[:, blocks * LANE : (blocks + 1) * LANE] = tail.T.astype(BF)

    turn(w1, wt1)
    turn(w2, wt2)
    for gath in (gath1, gath2):
        gath[rows:padded, :] = jnp.zeros((padded - rows, slots), BF)

    both = jnp.concatenate(
        [lists[1:2, :], lists[0:1, :], jnp.full((1, LANE - 2 * rim), -1, I32)], axis=1
    )
    lent = iota((slots, LANE), 0) == both
    side = iota((slots, LANE), 1) < rim
    lend_next, lend_prev = onehot(lent & side), onehot(lent & ~side)
    has_prev = (b > 0).astype(F32)
    has_next = (b < bricks - 1).astype(F32)

    swap_b.wait()
    arrived = dot(b_recv[...].astype(F32).T.astype(BF), em[...])
    occupied = arrived[chans : chans + 1, :]
    voxels = arrived[0:chans, :].astype(BF)
    keep1 = occupied * drop1[...].astype(F32) / KEEP_RATE
    keep2 = occupied * drop2[...].astype(F32) / KEEP_RATE

    def lend(field, halo, at):
        hs[at, 0] = dot(field, lend_next).astype(BF)
        hs[at, 1] = dot(field, lend_prev).astype(BF)
        halo.start()
        tab[:, 0:slots] = field

    def convolve(halo, at, gath, wt, summing):
        halo.wait()
        edge = hr[at, 0].astype(F32) * has_prev + hr[at, 1].astype(F32) * has_next
        tab[:, slots : slots + LANE] = edge.astype(BF)
        table = tab[...]

        def step(k):
            gath[pl.ds(pl.multiple_of(k * chans, 16), chans), :] = dot(table, oh[k]).astype(BF)

        unrolled(0, koff, step)
        rs_send[at] = dot(wt[...], gath[...])
        summing.start()
        own = rs_send[at, pl.ds(pl.multiple_of(x * chans, 16), chans), :]
        summing.wait()
        for d in range(chs - 1):
            own = own + rs_recv[at, d]
        return own

    lend(voxels, halo1, 0)
    conv1 = convolve(halo1, 0, gath1, wt1, sum1)
    hidden = (conv1 * jax.nn.sigmoid(conv1) * keep1).astype(BF)
    lend(hidden, halo2, 1)
    conv2 = convolve(halo2, 1, gath2, wt2, sum2)
    summed = voxels.astype(F32) + keep2 * conv2
    grad_pre = cot[...].astype(F32) * slope_silu(summed)
    mine = pl.ds(pl.multiple_of(x * chans, 16), chans)
    full_g[0, mine, :] = (grad_pre * keep2).astype(BF)
    share2.start()
    out_ref[...] = (summed * jax.nn.sigmoid(summed)).astype(BF)

    def push(weight, grads, fold, at):
        g = grads[...]

        def ahead(j):
            span = pl.ds(pl.multiple_of(j * 3 * chans, 16), 3 * chans)
            high, low = split(dot(weight[span, :], g))
            for i in range(3):
                part = slice(i * chans, (i + 1) * chans)
                pushed[3 * j + i, 0:chans, :] = high[part]
                pushed[3 * j + i, chans : 2 * chans, :] = low[part]

        unrolled(0, koff // 3, ahead)
        ret[...] = jnp.zeros_like(ret)

        def step(k):
            part = dot_nt(pushed[9 * k], oh[9 * k])
            for i in range(9 * k + 1, 9 * k + 9):
                part = part + dot_nt(pushed[i], oh[i])
            ret[...] += part

        unrolled(0, koff // 9, step)
        border = ret[0:chans, slots : slots + LANE] + ret[chans : 2 * chans, slots : slots + LANE]
        fs[at, 0] = border
        fs[at, 1] = border
        fold.start()

    def folded(fold, at):
        own = ret[0:chans, 0:slots] + ret[chans : 2 * chans, 0:slots]
        fold.wait()
        for part in split(fr[at, 0] * has_prev):
            own = own + dot_nt(part, lend_prev)
        for part in split(fr[at, 1] * has_next):
            own = own + dot_nt(part, lend_next)
        return own

    share2.wait()
    push(w2, full_g.at[0], fold2, 0)
    total2.compute(gath2, full_g.at[0])
    grad_hidden = folded(fold2, 0)
    full_g[1, mine, :] = (grad_hidden * keep1 * slope_silu(conv1)).astype(BF)
    share1.start()
    total2.to_first()
    share1.wait()
    total1.compute(gath1, full_g.at[1])
    push(w1, full_g.at[1], fold1, 1)
    grad_voxels = (grad_pre + folded(fold1, 1)).astype(BF)
    wide = jnp.concatenate([grad_voxels, jnp.zeros((LANE - chans, slots), BF)], axis=0)
    bb_send[...] = dot_nt(em[...], wide).astype(BF)
    back_b.start()
    own_rows(bb_send, bb_recv, q, qa)
    total1.to_first()
    back_b.wait()
    perm_back = onehot(pc == (pr % qs) * qa + ((pr // qs) % 2) * ys + pr // ya)
    ba_send[...] = dot(perm_back, bb_recv[...]).astype(BF)
    back_a.start()
    own_rows(ba_send, ba_recv, y, ya)
    total2.to_second()
    back_a.wait()
    gf = dot(ba_recv[...].astype(F32).T.astype(BF), pm[...])
    gf_ref[...] = gf[0:chans, :].astype(BF)
    total1.to_second()
    total2.to_third()
    total1.to_third()
    total2.to_fourth()
    total1.to_fourth()
    total2.to_last()
    total1.to_last()
    total2.finish()
    total1.finish()

    for swap in (
        swap_a,
        swap_b,
        back_b,
        back_a,
        halo1,
        halo2,
        fold2,
        fold1,
        sum1,
        sum2,
        share2,
        share1,
        *total2.all,
        *total1.all,
    ):
        swap.done()


def store(*refs):
    sources, targets, sem = refs[0:4], refs[4:8], refs[8]
    copies = [
        pltpu.make_async_copy(source.at[pl.ds(0, target.shape[0])], target, sem.at[i])
        for i, (source, target) in enumerate(zip(sources, targets))
    ]
    for copy in copies:
        copy.start()
    for copy in copies:
        copy.wait()


def local(ys, features, owner_map, kernel_map, send_lists, drop1, drop2, w1, w2, cotangent):
    bricks, chs = lax.axis_size("brick"), lax.axis_size("ch")
    chans, scan = features.shape
    koff, slots = kernel_map.shape
    outs = w1.shape[2]
    zs, rows, padded, half, first, second = sizes(bricks, ys, koff, chans, outs)
    qs = zs * CORES
    rim = send_lists.shape[1]
    dims = (
        bricks, ys, zs, chs, koff, chans, rows, padded, half, first, second,
        float(bricks * slots) ** -0.5,
    )
    prows = 2 * bricks
    vm = pltpu.VMEM
    table = slots + LANE
    scratch = [
        vm((koff, table, slots), BF),
        vm((outs, padded), BF),
        vm((outs, padded), BF),
        vm((chans, table), BF),
        vm((padded, slots), BF),
        vm((padded, slots), BF),
        vm((koff, 2 * chans, slots), BF),
        vm((2 * chans, table), F32),
        vm((prows, scan), BF),
        vm((prows, slots), BF),
        vm((prows, prows), BF),
        *[vm((prows, LANE), BF)] * 8,
        vm((2, 2, chans, LANE), BF),
        vm((2, 2, chans, LANE), BF),
        vm((2, 2, chans, LANE), F32),
        vm((2, 2, chans, LANE), F32),
        vm((2, outs, slots), F32),
        vm((2, chs - 1, chans, slots), F32),
        vm((2, outs, slots), BF),
        vm((2, half, outs), F32),
        vm((2, half, outs), BF),
        vm((2, half, outs), BF),
        vm((2, half, outs), BF),
        vm((2, ys - 1, first, LANE), BF),
        vm((2, zs - 1, first, LANE), BF),
        vm((2, 2, first, LANE), F32),
        vm((2, zs - 1, second, LANE), F32),
        vm((2, ys - 1, second, LANE), F32),
        vm((2, 2, second, LANE), BF),
        vm((2, 2, max(ys, zs) * second, LANE), BF),
    ]
    weight_sums = [1, ys - 1, zs - 1, zs - 1, ys - 1, zs - 1, ys - 1, ys - 1, zs - 1, ys, zs]
    copies = [ys - 1, qs - 1, qs - 1, ys - 1, 2, 2, 2, 2] + [chs - 1] * 4 + weight_sums * 2
    for n in copies:
        scratch += [pltpu.SemaphoreType.DMA((n,))] * 2
    shape = jax.ShapeDtypeStruct
    spec = pl.BlockSpec(memory_space=pltpu.VMEM)
    results = pl.pallas_call(
        functools.partial(kernel, dims),
        out_shape=(
            shape((chans, slots), BF),
            shape((chans, scan), BF),
            shape((padded, outs), BF),
            shape((padded, outs), BF),
        ),
        in_specs=[spec] * 9,
        out_specs=(spec,) * 4,
        scratch_shapes=scratch,
        compiler_params=pltpu.CompilerParams(
            collective_id=0, has_side_effects=True, vmem_limit_bytes=56 * 2**20
        ),
        name="block",
    )(
        features, owner_map.reshape(1, scan), send_lists, kernel_map, drop1, drop2,
        w1.reshape(rows, outs), w2.reshape(rows, outs), cotangent,
    )
    anywhere = pl.BlockSpec(memory_space=pl.ANY)
    block_out, grad_features, wg1, wg2 = pl.pallas_call(
        store,
        out_shape=(
            shape((chans, slots), BF),
            shape((chans, scan), BF),
            shape((rows, outs), BF),
            shape((rows, outs), BF),
        ),
        in_specs=[spec] * 4,
        out_specs=(anywhere,) * 4,
        scratch_shapes=[pltpu.SemaphoreType.DMA((4,))],
        name="store",
    )(*results)
    return block_out, grad_features, wg1.reshape(w1.shape), wg2.reshape(w2.shape)


def rows_of_chips(bricks):
    ys = 1
    while ys * ys * CORES < bricks:
        ys *= 2
    return ys


def solution(mesh):
    return jax.shard_map(
        functools.partial(local, rows_of_chips(mesh.shape["brick"])),
        mesh=mesh,
        in_specs=(
            P("ch", "brick"),
            P("brick", None),
            P(None, "brick"),
            P(None, "brick"),
            P("ch", "brick"),
            P("ch", "brick"),
            P(None, "ch", None),
            P(None, "ch", None),
            P("ch", "brick"),
        ),
        out_specs=(P("ch", "brick"), P("ch", "brick"), P(None, "ch", None), P(None, "ch", None)),
        check_vma=False,
    )
```

```python
import functools

import jax
import jax.numpy as jnp
from jax import lax
from jax.experimental import pallas as pl
from jax.experimental.pallas import tpu as pltpu
from jax.sharding import PartitionSpec as P

KEEP_RATE = 0.9
MESH = pl.DeviceIdType.MESH
BF = jnp.bfloat16
F32 = jnp.float32
I32 = jnp.int32
CORES = 2
LANE = 128


def dot(a, b):
    return jnp.dot(a, b, preferred_element_type=F32)


def dot_nt(a, b):
    return lax.dot_general(a, b, (((1,), (1,)), ((), ())), preferred_element_type=F32)


def onehot(mask):
    return jnp.where(mask, 1.0, 0.0).astype(BF)


def iota(shape, dim):
    return lax.broadcasted_iota(I32, shape, dim)


def split(value):
    high = value.astype(BF)
    return high, (value - high.astype(F32)).astype(BF)


def slope_silu(value):
    sig = jax.nn.sigmoid(value)
    return sig * (1.0 + value * (1.0 - sig))


def loop(low, high, body):
    def step(index, carry):
        body(index)
        return carry

    lax.fori_loop(low, high, step, 0)


def unrolled(low, high, body):
    for index in range(low, high):
        body(index)


class Swap:
    def __init__(self, n, peer, src, dst, land, sems):
        self.n, self.peer, self.src, self.dst, self.land = n, peer, src, dst, land
        self.ss, self.rs = sems

    def _copy(self, d, src, dst):
        return pltpu.make_async_remote_copy(
            src_ref=src,
            dst_ref=dst,
            send_sem=self.ss.at[d - 1],
            recv_sem=self.rs.at[d - 1],
            device_id=self.peer(d),
            device_id_type=MESH,
        )

    def start_one(self, d):
        self._copy(d, self.src(d), self.dst(d)).start()

    def wait_one(self, d):
        self._copy(d, self.land(d), self.land(d)).wait_recv()

    def start(self):
        unrolled(1, self.n, self.start_one)

    def wait(self):
        unrolled(1, self.n, self.wait_one)

    def done(self):
        loop(1, self.n, lambda d: self._copy(d, self.src(d), self.dst(d)).wait_send())


def sizes(bricks, ys, koff, chans, outs):
    zs = bricks // CORES // ys
    rows = koff * chans
    unit = CORES * ys * 16
    padded = -(-rows // unit) * unit
    padded = -(-padded // LANE) * LANE
    half = padded // CORES
    first = half // ys
    second = -(-first // zs // 16) * 16 if first % zs == 0 else -(-first // (16 * zs)) * 16
    return zs, rows, padded, half, first, second


def kernel(
    dims,
    feat,
    owner,
    lists,
    kmap,
    drop1,
    drop2,
    w1,
    w2,
    cot,
    out_ref,
    gf_ref,
    wg1_ref,
    wg2_ref,
    oh,
    wt1,
    wt2,
    gath1,
    gath2,
    pushed,
    ret,
    pm,
    em,
    perm,
    a_send,
    a_recv,
    b_send,
    b_recv,
    bb_send,
    bb_recv,
    ba_send,
    ba_recv,
    hs,
    hr,
    fs,
    fr,
    rs_send,
    rs_recv,
    full_g,
    wgf,
    wgb,
    c_recv,
    s1_src,
    s1_ra,
    s1_rb,
    s2_src,
    s2_ra,
    s2_rb,
    fin,
    chunk,
    *sems,
):
    bricks, ys, zs, chs, koff, chans, rows, padded, half, first, second, scale = dims
    qs = zs * CORES
    b, x = lax.axis_index("brick"), lax.axis_index("ch")
    y, q = b // qs, b % qs
    z, core = q // CORES, q % CORES
    slots = kmap.shape[1]
    sem_at = iter([(sems[i], sems[i + 1]) for i in range(0, len(sems), 2)])

    def ring(count, at, step):
        return lax.rem(at + step, count)

    to_y = lambda d: (ring(ys, y, d) * qs + q, x)
    to_q = lambda d: (y * qs + ring(qs, q, d), x)
    to_z = lambda d: (y * qs + ring(zs, z, d) * CORES + core, x)
    to_core = lambda d: (y * qs + z * CORES + (1 - core), x)
    to_ch = lambda d: (b, ring(chs, x, d))
    to_brick = lambda d: (lax.rem(b + 1 + (d - 1) * (bricks - 2), bricks), x)

    barrier = pltpu.get_barrier_semaphore()
    groups = ((to_y, ys), (to_q, qs), (to_ch, chs), (to_brick, 3))
    for peer, n in groups:
        loop(
            1,
            n,
            lambda d, peer=peer: pl.semaphore_signal(
                barrier, inc=1, device_id=peer(d), device_id_type=MESH
            ),
        )

    prows = 2 * bricks
    t_row = owner[...]
    scan = t_row.shape[1]
    t_col = jnp.broadcast_to(t_row.astype(F32), (scan, scan)).T.astype(I32)
    earlier = (t_col == t_row) & (iota((scan, scan), 0) < iota((scan, scan), 1))
    ordinal = jnp.sum(jnp.where(earlier, 1.0, 0.0), axis=0, keepdims=True)
    code = (t_row // qs) * (2 * qs) + ordinal.astype(I32) * qs + t_row % qs
    pm[...] = onehot(iota((prows, scan), 0) == code)
    carried = jnp.concatenate(
        [feat[...], jnp.where(iota((LANE - chans, scan), 0) == 0, 1.0, 0.0).astype(BF)], axis=0
    )
    a_send[...] = dot_nt(pm[...], carried).astype(BF)

    pl.semaphore_wait(barrier, sum(n - 1 for _, n in groups))

    def chunk_of(ref, index, size):
        return ref.at[pl.ds(pl.multiple_of(index * size, size), size)]

    ya, qa = 2 * qs, 2 * ys
    swap_a = Swap(
        ys,
        to_y,
        lambda d: chunk_of(a_send, ring(ys, y, d), ya),
        lambda d: chunk_of(a_recv, y, ya),
        lambda d: chunk_of(a_recv, ring(ys, y, ys - d), ya),
        next(sem_at),
    )
    swap_b = Swap(
        qs,
        to_q,
        lambda d: chunk_of(b_send, ring(qs, q, d), qa),
        lambda d: chunk_of(b_recv, q, qa),
        lambda d: chunk_of(b_recv, ring(qs, q, qs - d), qa),
        next(sem_at),
    )
    back_b = Swap(
        qs,
        to_q,
        lambda d: chunk_of(bb_send, ring(qs, q, d), qa),
        lambda d: chunk_of(bb_recv, q, qa),
        lambda d: chunk_of(bb_recv, ring(qs, q, qs - d), qa),
        next(sem_at),
    )
    back_a = Swap(
        ys,
        to_y,
        lambda d: chunk_of(ba_send, ring(ys, y, d), ya),
        lambda d: chunk_of(ba_recv, y, ya),
        lambda d: chunk_of(ba_recv, ring(ys, y, ys - d), ya),
        next(sem_at),
    )

    def neighbours(send, recv, at):
        return Swap(
            3,
            to_brick,
            lambda d: send.at[at, d - 1],
            lambda d: recv.at[at, d - 1],
            lambda d: recv.at[at, d - 1],
            next(sem_at),
        )

    halo1, halo2 = neighbours(hs, hr, 0), neighbours(hs, hr, 1)
    fold2, fold1 = neighbours(fs, fr, 0), neighbours(fs, fr, 1)

    def scatter_sum(at):
        return Swap(
            chs,
            to_ch,
            lambda d: chunk_of(rs_send.at[at], ring(chs, x, d), chans),
            lambda d: rs_recv.at[at, d - 1],
            lambda d: rs_recv.at[at, d - 1],
            next(sem_at),
        )

    sum1, sum2 = scatter_sum(0), scatter_sum(1)

    def share(at):
        return Swap(
            chs,
            to_ch,
            lambda d: chunk_of(full_g.at[at], x, chans),
            lambda d: chunk_of(full_g.at[at], x, chans),
            lambda d: chunk_of(full_g.at[at], ring(chs, x, chs - d), chans),
            next(sem_at),
        )

    share2, share1 = share(0), share(1)

    left, right = pl.ds(0, LANE), pl.ds(LANE, LANE)

    def rows_of(ref, start, size, lanes):
        return ref.at[pl.ds(pl.multiple_of(start, 16), size), lanes]

    def second_at(index):
        return jnp.minimum(index * second, first - second)

    class Total:
        def __init__(self, at, ref):
            self.at, self.ref = at, ref
            self.cores = Swap(
                2,
                to_core,
                lambda d: wgb.at[at],
                lambda d: c_recv.at[at],
                lambda d: c_recv.at[at],
                next(sem_at),
            )
            src = s1_src.at[at]
            self.first = (
                Swap(
                    ys,
                    to_y,
                    lambda d: rows_of(src, ring(ys, y, d) * first, first, left),
                    lambda d: s1_ra.at[at, d - 1],
                    lambda d: s1_ra.at[at, d - 1],
                    next(sem_at),
                ),
                Swap(
                    zs,
                    to_z,
                    lambda d: rows_of(src, ring(zs, z, d) * first, first, right),
                    lambda d: s1_rb.at[at, d - 1],
                    lambda d: s1_rb.at[at, d - 1],
                    next(sem_at),
                ),
            )
            self.second = (
                Swap(
                    zs,
                    to_z,
                    lambda d: s2_src.at[at, 0, pl.ds(pl.multiple_of(second_at(ring(zs, z, d)), 16), second)],
                    lambda d: s2_ra.at[at, d - 1],
                    lambda d: s2_ra.at[at, d - 1],
                    next(sem_at),
                ),
                Swap(
                    ys,
                    to_y,
                    lambda d: s2_src.at[at, 1, pl.ds(pl.multiple_of(second_at(ring(ys, y, d)), 16), second)],
                    lambda d: s2_rb.at[at, d - 1],
                    lambda d: s2_rb.at[at, d - 1],
                    next(sem_at),
                ),
            )
            self.third = (
                Swap(
                    zs,
                    to_z,
                    lambda d: fin.at[at, 0],
                    lambda d: chunk_of(chunk.at[at, 0], z, second),
                    lambda d: chunk_of(chunk.at[at, 0], ring(zs, z, zs - d), second),
                    next(sem_at),
                ),
                Swap(
                    ys,
                    to_y,
                    lambda d: fin.at[at, 1],
                    lambda d: chunk_of(chunk.at[at, 1], y, second),
                    lambda d: chunk_of(chunk.at[at, 1], ring(ys, y, ys - d), second),
                    next(sem_at),
                ),
            )
            self.fourth = (
                Swap(
                    ys,
                    to_y,
                    lambda d: chunk.at[at, 0, pl.ds(0, first)],
                    lambda d: rows_of(ref, core * half + y * first, first, left),
                    lambda d: rows_of(ref, core * half + ring(ys, y, ys - d) * first, first, left),
                    next(sem_at),
                ),
                Swap(
                    zs,
                    to_z,
                    lambda d: chunk.at[at, 1, pl.ds(0, first)],
                    lambda d: rows_of(ref, core * half + z * first, first, right),
                    lambda d: rows_of(ref, core * half + ring(zs, z, zs - d) * first, first, right),
                    next(sem_at),
                ),
            )
            self.last = tuple(
                Swap(
                    n + 1,
                    lambda d: to_core(1),
                    lambda d, n=n, pos=pos, lanes=lanes: rows_of(
                        ref, core * half + ring(n, pos, n + 1 - d) * first, first, lanes
                    ),
                    lambda d, n=n, pos=pos, lanes=lanes: rows_of(
                        ref, core * half + ring(n, pos, n + 1 - d) * first, first, lanes
                    ),
                    lambda d, n=n, pos=pos, lanes=lanes: rows_of(
                        ref, (1 - core) * half + ring(n, pos, n + 1 - d) * first, first, lanes
                    ),
                    next(sem_at),
                )
                for n, pos, lanes in ((ys, y, left), (zs, z, right))
            )
            self.all = (
                self.cores, *self.first, *self.second, *self.third, *self.fourth, *self.last
            )

        def compute(self, gath, grads, which):
            g, block = grads[...], half // 2
            for i in range(2):
                start = which * half + i * block
                yield pl.ds(i * block, block), dot_nt(
                    gath[pl.ds(pl.multiple_of(start, 16), block), :], g
                )

        def give(self, gath, grads):
            for span, part in self.compute(gath, grads, 1 - core):
                wgb[self.at, span, :] = part.astype(BF)
            self.cores.start()

        def keep(self, gath, grads):
            for span, part in self.compute(gath, grads, core):
                wgf[self.at, span, :] = part

        def to_first(self):
            self.cores.wait()
            both = wgf[self.at] + c_recv[self.at].astype(F32)
            s1_src[self.at] = both.astype(BF)
            for swap in self.first:
                swap.start()

        def to_second(self):
            for side, (swap, recv, pos, lanes, n) in enumerate(
                zip(self.first, (s1_ra, s1_rb), (y, z), (left, right), (ys, zs))
            ):
                swap.wait()
                span = pl.ds(pl.multiple_of(pos * first, 16), first)
                total = s1_src[self.at, span, lanes].astype(F32)
                for d in range(n - 1):
                    total = total + recv[self.at, d].astype(F32)
                s2_src[self.at, side] = total
                self.second[side].start()

        def to_third(self):
            for side, (swap, recv, pos, n) in enumerate(
                zip(self.second, (s2_ra, s2_rb), (z, y), (zs, ys))
            ):
                swap.wait()
                span = pl.ds(pl.multiple_of(second_at(pos), 16), second)
                total = s2_src[self.at, side, span, :]
                for d in range(n - 1):
                    total = total + recv[self.at, d]
                done = (total * scale).astype(BF)
                fin[self.at, side] = done
                chunk[self.at, side, pl.ds(pl.multiple_of(pos * second, 16), second), :] = done
                self.third[side].start()

        def to_fourth(self):
            for side, (swap, pos, lanes) in enumerate(zip(self.third, (y, z), (left, right))):
                swap.wait()
                self.fourth[side].start()
                span = pl.ds(pl.multiple_of(core * half + pos * first, 16), first)
                self.ref[span, lanes] = chunk[self.at, side, pl.ds(0, first), :]
                self.last[side].start_one(1)

        def to_last(self):
            for side, swap in enumerate(self.fourth):

                def forward(d, swap=swap, side=side):
                    swap.wait_one(d)
                    self.last[side].start_one(d + 1)

                loop(1, swap.n, forward)

        def finish(self):
            for swap in self.last:
                swap.wait()

    total2, total1 = Total(0, wg2_ref), Total(1, wg1_ref)

    def own_rows(src, dst, index, size):
        span = pl.ds(pl.multiple_of(index * size, size), size)
        dst[span, :] = src[span, :]

    swap_a.start()
    own_rows(a_send, a_recv, y, ya)

    pr, pc = iota((prows, prows), 0), iota((prows, prows), 1)
    perm[...] = onehot(pc == (pr % ys) * ya + ((pr // ys) % 2) * qs + pr // qa)
    er, ec = iota((prows, slots), 0), iota((prows, slots), 1)
    em[...] = onehot(ec == 2 * ((er % ys) * qs + er // qa) + (er // ys) % 2)

    rim = 32

    def build(k):
        row = kmap[pl.ds(k, 1), :]
        inner = jnp.where(row < rim + slots, row - rim, row)
        column = jnp.where(row < rim, row + slots, jnp.where(row >= slots + 2 * rim, -1, inner))
        oh[k] = onehot(iota(oh.shape[1:], 0) == column)

    unrolled(0, koff // 3, build)

    swap_a.wait()
    b_send[...] = dot(perm[...], a_recv[...]).astype(BF)
    swap_b.start()
    own_rows(b_send, b_recv, q, qa)

    unrolled(koff // 3, koff, build)

    def turn(source, target):
        blocks = rows // LANE

        def step(j):
            at = pl.multiple_of(j * LANE, LANE)
            target[:, pl.ds(at, LANE)] = source[pl.ds(at, LANE), :].astype(F32).T.astype(BF)

        unrolled(0, blocks, step)
        if rows % LANE:
            tail = source[blocks * LANE : rows, :].astype(F32)
            tail = jnp.concatenate([tail, jnp.zeros((LANE - rows % LANE, tail.shape[1]), F32)], 0)
            target[:, blocks * LANE : (blocks + 1) * LANE] = tail.T.astype(BF)

    turn(w1, wt1)
    turn(w2, wt2)
    for gath in (gath1, gath2):
        gath[rows:padded, :] = jnp.zeros((padded - rows, slots), BF)

    both = jnp.concatenate(
        [lists[1:2, :], lists[0:1, :], jnp.full((1, LANE - 2 * rim), -1, I32)], axis=1
    )
    lent = iota((slots, LANE), 0) == both
    side = iota((slots, LANE), 1) < rim
    lend_next, lend_prev = onehot(lent & side), onehot(lent & ~side)
    has_prev = (b > 0).astype(F32)
    has_next = (b < bricks - 1).astype(F32)

    swap_b.wait()
    arrived = dot(b_recv[...].astype(F32).T.astype(BF), em[...])
    occupied = arrived[chans : chans + 1, :]
    voxels = arrived[0:chans, :].astype(BF)
    keep1 = occupied * drop1[...].astype(F32) / KEEP_RATE
    keep2 = occupied * drop2[...].astype(F32) / KEEP_RATE

    def lend(field, halo, at):
        hs[at, 0] = dot(field, lend_next).astype(BF)
        hs[at, 1] = dot(field, lend_prev).astype(BF)
        halo.start()

    def convolve(field, halo, at, gath, wt, summing):
        def inner(k):
            gath[k * chans : (k + 1) * chans, :] = dot(field, oh[k, 0:slots, :]).astype(BF)

        unrolled(0, koff, inner)
        halo.wait()
        edge = hr[at, 0].astype(F32) * has_prev + hr[at, 1].astype(F32) * has_next
        edge = edge.astype(BF)

        def outer(k):
            part = dot(edge, oh[k, slots : slots + LANE, :]).astype(BF)
            gath[k * chans : (k + 1) * chans, :] += part

        unrolled(0, koff, outer)
        rs_send[at] = dot(wt[...], gath[...])
        summing.start()
        own = rs_send[at, pl.ds(pl.multiple_of(x * chans, 16), chans), :]
        summing.wait()
        for d in range(chs - 1):
            own = own + rs_recv[at, d]
        return own

    lend(voxels, halo1, 0)
    conv1 = convolve(voxels, halo1, 0, gath1, wt1, sum1)
    hidden = (conv1 * jax.nn.sigmoid(conv1) * keep1).astype(BF)
    lend(hidden, halo2, 1)
    conv2 = convolve(hidden, halo2, 1, gath2, wt2, sum2)
    summed = voxels.astype(F32) + keep2 * conv2
    grad_pre = cot[...].astype(F32) * slope_silu(summed)
    mine = pl.ds(pl.multiple_of(x * chans, 16), chans)
    full_g[0, mine, :] = (grad_pre * keep2).astype(BF)
    share2.start()
    out_ref[...] = (summed * jax.nn.sigmoid(summed)).astype(BF)

    def push(weight, grads, fold, at):
        g = grads[...]

        def ahead(j):
            span = pl.ds(pl.multiple_of(j * 3 * chans, 16), 3 * chans)
            high, low = split(dot(weight[span, :], g))
            for i in range(3):
                part = slice(i * chans, (i + 1) * chans)
                pushed[3 * j + i, 0:chans, :] = high[part]
                pushed[3 * j + i, chans : 2 * chans, :] = low[part]

        unrolled(0, koff // 3, ahead)
        both = returned(slots, slots + LANE)
        border = both[0:chans] + both[chans : 2 * chans]
        fs[at, 0] = border
        fs[at, 1] = border
        fold.start()

    def returned(low, high):
        part = dot_nt(pushed[0], oh[0, low:high, :])
        for k in range(1, koff):
            part = part + dot_nt(pushed[k], oh[k, low:high, :])
        return part

    def own_columns():
        ret[...] = returned(0, slots)

    def folded(fold, at):
        own = ret[0:chans, :] + ret[chans : 2 * chans, :]
        fold.wait()
        for part in split(fr[at, 0] * has_prev):
            own = own + dot_nt(part, lend_prev)
        for part in split(fr[at, 1] * has_next):
            own = own + dot_nt(part, lend_next)
        return own

    share2.wait()
    push(w2, full_g.at[0], fold2, 0)
    own_columns()
    total2.give(gath2, full_g.at[0])
    grad_hidden = folded(fold2, 0)
    full_g[1, mine, :] = (grad_hidden * keep1 * slope_silu(conv1)).astype(BF)
    share1.start()
    total2.keep(gath2, full_g.at[0])
    total2.to_first()
    share1.wait()
    total1.give(gath1, full_g.at[1])
    push(w1, full_g.at[1], fold1, 1)
    own_columns()
    total1.keep(gath1, full_g.at[1])
    grad_voxels = (grad_pre + folded(fold1, 1)).astype(BF)
    wide = jnp.concatenate([grad_voxels, jnp.zeros((LANE - chans, slots), BF)], axis=0)
    bb_send[...] = dot_nt(em[...], wide).astype(BF)
    back_b.start()
    own_rows(bb_send, bb_recv, q, qa)
    total1.to_first()
    total2.to_second()
    back_b.wait()
    perm_back = onehot(pc == (pr % qs) * qa + ((pr // qs) % 2) * ys + pr // ya)
    ba_send[...] = dot(perm_back, bb_recv[...]).astype(BF)
    back_a.start()
    own_rows(ba_send, ba_recv, y, ya)
    total2.to_third()
    total1.to_second()
    back_a.wait()
    gf = dot(ba_recv[...].astype(F32).T.astype(BF), pm[...])
    gf_ref[...] = gf[0:chans, :].astype(BF)
    total2.to_fourth()
    total1.to_third()
    total1.to_fourth()
    total2.to_last()
    total1.to_last()
    total2.finish()
    total1.finish()

    for swap in (
        swap_a,
        swap_b,
        back_b,
        back_a,
        halo1,
        halo2,
        fold2,
        fold1,
        sum1,
        sum2,
        share2,
        share1,
        *total2.all,
        *total1.all,
    ):
        swap.done()


def store(*refs):
    sources, targets, sem = refs[0:4], refs[4:8], refs[8]
    copies = [
        pltpu.make_async_copy(source.at[pl.ds(0, target.shape[0])], target, sem.at[i])
        for i, (source, target) in enumerate(zip(sources, targets))
    ]
    for copy in copies:
        copy.start()
    for copy in copies:
        copy.wait()


def local(ys, features, owner_map, kernel_map, send_lists, drop1, drop2, w1, w2, cotangent):
    bricks, chs = lax.axis_size("brick"), lax.axis_size("ch")
    chans, scan = features.shape
    koff, slots = kernel_map.shape
    outs = w1.shape[2]
    zs, rows, padded, half, first, second = sizes(bricks, ys, koff, chans, outs)
    qs = zs * CORES
    rim = send_lists.shape[1]
    dims = (
        bricks, ys, zs, chs, koff, chans, rows, padded, half, first, second,
        float(bricks * slots) ** -0.5,
    )
    prows = 2 * bricks
    vm = pltpu.VMEM
    table = slots + LANE
    scratch = [
        vm((koff, table, slots), BF),
        vm((outs, padded), BF),
        vm((outs, padded), BF),
        vm((padded, slots), BF),
        vm((padded, slots), BF),
        vm((koff, 2 * chans, slots), BF),
        vm((2 * chans, slots), F32),
        vm((prows, scan), BF),
        vm((prows, slots), BF),
        vm((prows, prows), BF),
        *[vm((prows, LANE), BF)] * 8,
        vm((2, 2, chans, LANE), BF),
        vm((2, 2, chans, LANE), BF),
        vm((2, 2, chans, LANE), F32),
        vm((2, 2, chans, LANE), F32),
        vm((2, outs, slots), F32),
        vm((2, chs - 1, chans, slots), F32),
        vm((2, outs, slots), BF),
        vm((2, half, outs), F32),
        vm((2, half, outs), BF),
        vm((2, half, outs), BF),
        vm((2, half, outs), BF),
        vm((2, ys - 1, first, LANE), BF),
        vm((2, zs - 1, first, LANE), BF),
        vm((2, 2, first, LANE), F32),
        vm((2, zs - 1, second, LANE), F32),
        vm((2, ys - 1, second, LANE), F32),
        vm((2, 2, second, LANE), BF),
        vm((2, 2, max(ys, zs) * second, LANE), BF),
    ]
    weight_sums = [1, ys - 1, zs - 1, zs - 1, ys - 1, zs - 1, ys - 1, ys - 1, zs - 1, ys, zs]
    copies = [ys - 1, qs - 1, qs - 1, ys - 1, 2, 2, 2, 2] + [chs - 1] * 4 + weight_sums * 2
    for n in copies:
        scratch += [pltpu.SemaphoreType.DMA((n,))] * 2
    shape = jax.ShapeDtypeStruct
    spec = pl.BlockSpec(memory_space=pltpu.VMEM)
    results = pl.pallas_call(
        functools.partial(kernel, dims),
        out_shape=(
            shape((chans, slots), BF),
            shape((chans, scan), BF),
            shape((padded, outs), BF),
            shape((padded, outs), BF),
        ),
        in_specs=[spec] * 9,
        out_specs=(spec,) * 4,
        scratch_shapes=scratch,
        compiler_params=pltpu.CompilerParams(
            collective_id=0, has_side_effects=True, vmem_limit_bytes=56 * 2**20
        ),
        name="block",
    )(
        features, owner_map.reshape(1, scan), send_lists, kernel_map, drop1, drop2,
        w1.reshape(rows, outs), w2.reshape(rows, outs), cotangent,
    )
    anywhere = pl.BlockSpec(memory_space=pl.ANY)
    block_out, grad_features, wg1, wg2 = pl.pallas_call(
        store,
        out_shape=(
            shape((chans, slots), BF),
            shape((chans, scan), BF),
            shape((rows, outs), BF),
            shape((rows, outs), BF),
        ),
        in_specs=[spec] * 4,
        out_specs=(anywhere,) * 4,
        scratch_shapes=[pltpu.SemaphoreType.DMA((4,))],
        name="store",
    )(*results)
    return block_out, grad_features, wg1.reshape(w1.shape), wg2.reshape(w2.shape)


def rows_of_chips(bricks):
    ys = 1
    while ys * ys * CORES < bricks:
        ys *= 2
    return ys


def solution(mesh):
    return jax.shard_map(
        functools.partial(local, rows_of_chips(mesh.shape["brick"])),
        mesh=mesh,
        in_specs=(
            P("ch", "brick"),
            P("brick", None),
            P(None, "brick"),
            P(None, "brick"),
            P("ch", "brick"),
            P("ch", "brick"),
            P(None, "ch", None),
            P(None, "ch", None),
            P("ch", "brick"),
        ),
        out_specs=(P("ch", "brick"), P("ch", "brick"), P(None, "ch", None), P(None, "ch", None)),
        check_vma=False,
    )
```

```python
import functools

import jax
import jax.numpy as jnp
from jax import lax
from jax.experimental import pallas as pl
from jax.experimental.pallas import tpu as pltpu
from jax.sharding import PartitionSpec as P

KEEP_RATE = 0.9
MESH = pl.DeviceIdType.MESH
BF = jnp.bfloat16
F32 = jnp.float32
I32 = jnp.int32
CORES = 2
LANE = 128


def dot(a, b):
    return jnp.dot(a, b, preferred_element_type=F32)


def dot_nt(a, b):
    return lax.dot_general(a, b, (((1,), (1,)), ((), ())), preferred_element_type=F32)


def onehot(mask):
    return jnp.where(mask, 1.0, 0.0).astype(BF)


def iota(shape, dim):
    return lax.broadcasted_iota(I32, shape, dim)


def split(value):
    high = value.astype(BF)
    return high, (value - high.astype(F32)).astype(BF)


def slope_silu(value):
    sig = jax.nn.sigmoid(value)
    return sig * (1.0 + value * (1.0 - sig))


def loop(low, high, body):
    def step(index, carry):
        body(index)
        return carry

    lax.fori_loop(low, high, step, 0)


def unrolled(low, high, body):
    for index in range(low, high):
        body(index)


class Swap:
    def __init__(self, n, peer, src, dst, land, sems):
        self.n, self.peer, self.src, self.dst, self.land = n, peer, src, dst, land
        self.ss, self.rs = sems

    def _copy(self, d, src, dst):
        return pltpu.make_async_remote_copy(
            src_ref=src,
            dst_ref=dst,
            send_sem=self.ss.at[d - 1],
            recv_sem=self.rs.at[d - 1],
            device_id=self.peer(d),
            device_id_type=MESH,
        )

    def start_one(self, d):
        self._copy(d, self.src(d), self.dst(d)).start()

    def wait_one(self, d):
        self._copy(d, self.land(d), self.land(d)).wait_recv()

    def start(self):
        unrolled(1, self.n, self.start_one)

    def wait(self):
        unrolled(1, self.n, self.wait_one)

    def done(self):
        loop(1, self.n, lambda d: self._copy(d, self.src(d), self.dst(d)).wait_send())


def sizes(bricks, ys, koff, chans, outs):
    zs = bricks // CORES // ys
    rows = koff * chans
    unit = CORES * ys * 16
    padded = -(-rows // unit) * unit
    padded = -(-padded // LANE) * LANE
    half = padded // CORES
    first = half // ys
    second = -(-first // zs // 16) * 16 if first % zs == 0 else -(-first // (16 * zs)) * 16
    return zs, rows, padded, half, first, second


def kernel(
    dims,
    feat,
    owner,
    lists,
    kmap,
    drop1,
    drop2,
    w1,
    w2,
    cot,
    out_ref,
    gf_ref,
    wg1_ref,
    wg2_ref,
    oh,
    wt1,
    wt2,
    gath1,
    gath2,
    pushed,
    ret,
    pm,
    em,
    perm,
    a_send,
    a_recv,
    b_send,
    b_recv,
    bb_send,
    bb_recv,
    ba_send,
    ba_recv,
    hs,
    hr,
    fs,
    fr,
    rs_send,
    rs_recv,
    full_g,
    wgf,
    wgb,
    c_recv,
    s1_src,
    s1_ra,
    s1_rb,
    s2_src,
    s2_ra,
    s2_rb,
    fin,
    chunk,
    *sems,
):
    bricks, ys, zs, chs, koff, chans, rows, padded, half, first, second, scale = dims
    qs = zs * CORES
    b, x = lax.axis_index("brick"), lax.axis_index("ch")
    y, q = b // qs, b % qs
    z, core = q // CORES, q % CORES
    slots = kmap.shape[1]
    sem_at = iter([(sems[i], sems[i + 1]) for i in range(0, len(sems), 2)])

    def ring(count, at, step):
        return lax.rem(at + step, count)

    to_y = lambda d: (ring(ys, y, d) * qs + q, x)
    to_q = lambda d: (y * qs + ring(qs, q, d), x)
    to_z = lambda d: (y * qs + ring(zs, z, d) * CORES + core, x)
    to_core = lambda d: (y * qs + z * CORES + (1 - core), x)
    to_ch = lambda d: (b, ring(chs, x, d))
    to_brick = lambda d: (lax.rem(b + 1 + (d - 1) * (bricks - 2), bricks), x)

    barrier = pltpu.get_barrier_semaphore()
    groups = ((to_y, ys), (to_q, qs), (to_ch, chs), (to_brick, 3))
    for peer, n in groups:
        loop(
            1,
            n,
            lambda d, peer=peer: pl.semaphore_signal(
                barrier, inc=1, device_id=peer(d), device_id_type=MESH
            ),
        )

    prows = 2 * bricks
    t_row = owner[...]
    scan = t_row.shape[1]
    t_col = jnp.broadcast_to(t_row.astype(F32), (scan, scan)).T.astype(I32)
    earlier = (t_col == t_row) & (iota((scan, scan), 0) < iota((scan, scan), 1))
    ordinal = jnp.sum(jnp.where(earlier, 1.0, 0.0), axis=0, keepdims=True)
    code = (t_row // qs) * (2 * qs) + ordinal.astype(I32) * qs + t_row % qs
    pm[...] = onehot(iota((prows, scan), 0) == code)
    carried = jnp.concatenate(
        [feat[...], jnp.where(iota((LANE - chans, scan), 0) == 0, 1.0, 0.0).astype(BF)], axis=0
    )
    a_send[...] = dot_nt(pm[...], carried).astype(BF)

    pl.semaphore_wait(barrier, sum(n - 1 for _, n in groups))

    def chunk_of(ref, index, size):
        return ref.at[pl.ds(pl.multiple_of(index * size, size), size)]

    ya, qa = 2 * qs, 2 * ys
    swap_a = Swap(
        ys,
        to_y,
        lambda d: chunk_of(a_send, ring(ys, y, d), ya),
        lambda d: chunk_of(a_recv, y, ya),
        lambda d: chunk_of(a_recv, ring(ys, y, ys - d), ya),
        next(sem_at),
    )
    swap_b = Swap(
        qs,
        to_q,
        lambda d: chunk_of(b_send, ring(qs, q, d), qa),
        lambda d: chunk_of(b_recv, q, qa),
        lambda d: chunk_of(b_recv, ring(qs, q, qs - d), qa),
        next(sem_at),
    )
    back_b = Swap(
        qs,
        to_q,
        lambda d: chunk_of(bb_send, ring(qs, q, d), qa),
        lambda d: chunk_of(bb_recv, q, qa),
        lambda d: chunk_of(bb_recv, ring(qs, q, qs - d), qa),
        next(sem_at),
    )
    back_a = Swap(
        ys,
        to_y,
        lambda d: chunk_of(ba_send, ring(ys, y, d), ya),
        lambda d: chunk_of(ba_recv, y, ya),
        lambda d: chunk_of(ba_recv, ring(ys, y, ys - d), ya),
        next(sem_at),
    )

    def neighbours(send, recv, at):
        return Swap(
            3,
            to_brick,
            lambda d: send.at[at, d - 1],
            lambda d: recv.at[at, d - 1],
            lambda d: recv.at[at, d - 1],
            next(sem_at),
        )

    halo1, halo2 = neighbours(hs, hr, 0), neighbours(hs, hr, 1)
    fold2, fold1 = neighbours(fs, fr, 0), neighbours(fs, fr, 1)

    def scatter_sum(at):
        return Swap(
            chs,
            to_ch,
            lambda d: chunk_of(rs_send.at[at], ring(chs, x, d), chans),
            lambda d: rs_recv.at[at, d - 1],
            lambda d: rs_recv.at[at, d - 1],
            next(sem_at),
        )

    sum1, sum2 = scatter_sum(0), scatter_sum(1)

    def share(at):
        return Swap(
            chs,
            to_ch,
            lambda d: chunk_of(full_g.at[at], x, chans),
            lambda d: chunk_of(full_g.at[at], x, chans),
            lambda d: chunk_of(full_g.at[at], ring(chs, x, chs - d), chans),
            next(sem_at),
        )

    share2, share1 = share(0), share(1)

    left, right = pl.ds(0, LANE), pl.ds(LANE, LANE)

    def rows_of(ref, start, size, lanes):
        return ref.at[pl.ds(pl.multiple_of(start, 16), size), lanes]

    def second_at(index):
        return jnp.minimum(index * second, first - second)

    class Total:
        def __init__(self, at, ref):
            self.at, self.ref = at, ref
            self.cores = Swap(
                2,
                to_core,
                lambda d: wgb.at[at],
                lambda d: c_recv.at[at],
                lambda d: c_recv.at[at],
                next(sem_at),
            )
            src = s1_src.at[at]
            self.first = (
                Swap(
                    ys,
                    to_y,
                    lambda d: rows_of(src, ring(ys, y, d) * first, first, left),
                    lambda d: s1_ra.at[at, d - 1],
                    lambda d: s1_ra.at[at, d - 1],
                    next(sem_at),
                ),
                Swap(
                    zs,
                    to_z,
                    lambda d: rows_of(src, ring(zs, z, d) * first, first, right),
                    lambda d: s1_rb.at[at, d - 1],
                    lambda d: s1_rb.at[at, d - 1],
                    next(sem_at),
                ),
            )
            self.second = (
                Swap(
                    zs,
                    to_z,
                    lambda d: s2_src.at[at, 0, pl.ds(pl.multiple_of(second_at(ring(zs, z, d)), 16), second)],
                    lambda d: s2_ra.at[at, d - 1],
                    lambda d: s2_ra.at[at, d - 1],
                    next(sem_at),
                ),
                Swap(
                    ys,
                    to_y,
                    lambda d: s2_src.at[at, 1, pl.ds(pl.multiple_of(second_at(ring(ys, y, d)), 16), second)],
                    lambda d: s2_rb.at[at, d - 1],
                    lambda d: s2_rb.at[at, d - 1],
                    next(sem_at),
                ),
            )
            self.third = (
                Swap(
                    zs,
                    to_z,
                    lambda d: fin.at[at, 0],
                    lambda d: chunk_of(chunk.at[at, 0], z, second),
                    lambda d: chunk_of(chunk.at[at, 0], ring(zs, z, zs - d), second),
                    next(sem_at),
                ),
                Swap(
                    ys,
                    to_y,
                    lambda d: fin.at[at, 1],
                    lambda d: chunk_of(chunk.at[at, 1], y, second),
                    lambda d: chunk_of(chunk.at[at, 1], ring(ys, y, ys - d), second),
                    next(sem_at),
                ),
            )
            self.fourth = (
                Swap(
                    ys,
                    to_y,
                    lambda d: chunk.at[at, 0, pl.ds(0, first)],
                    lambda d: rows_of(ref, core * half + y * first, first, left),
                    lambda d: rows_of(ref, core * half + ring(ys, y, ys - d) * first, first, left),
                    next(sem_at),
                ),
                Swap(
                    zs,
                    to_z,
                    lambda d: chunk.at[at, 1, pl.ds(0, first)],
                    lambda d: rows_of(ref, core * half + z * first, first, right),
                    lambda d: rows_of(ref, core * half + ring(zs, z, zs - d) * first, first, right),
                    next(sem_at),
                ),
            )
            self.last = tuple(
                Swap(
                    n + 1,
                    lambda d: to_core(1),
                    lambda d, n=n, pos=pos, lanes=lanes: rows_of(
                        ref, core * half + ring(n, pos, n + 1 - d) * first, first, lanes
                    ),
                    lambda d, n=n, pos=pos, lanes=lanes: rows_of(
                        ref, core * half + ring(n, pos, n + 1 - d) * first, first, lanes
                    ),
                    lambda d, n=n, pos=pos, lanes=lanes: rows_of(
                        ref, (1 - core) * half + ring(n, pos, n + 1 - d) * first, first, lanes
                    ),
                    next(sem_at),
                )
                for n, pos, lanes in ((ys, y, left), (zs, z, right))
            )
            self.all = (
                self.cores, *self.first, *self.second, *self.third, *self.fourth, *self.last
            )

        def compute(self, gath, grads, which):
            g, block = grads[...], half // 2
            for i in range(2):
                start = which * half + i * block
                yield pl.ds(i * block, block), dot_nt(
                    gath[pl.ds(pl.multiple_of(start, 16), block), :], g
                )

        def give(self, gath, grads):
            for span, part in self.compute(gath, grads, 1 - core):
                wgb[self.at, span, :] = part.astype(BF)
            self.cores.start()

        def keep(self, gath, grads):
            for span, part in self.compute(gath, grads, core):
                wgf[self.at, span, :] = part

        def to_first(self):
            self.cores.wait()
            both = wgf[self.at] + c_recv[self.at].astype(F32)
            s1_src[self.at] = both.astype(BF)
            for swap in self.first:
                swap.start()

        def to_second(self):
            for side, (swap, recv, pos, lanes, n) in enumerate(
                zip(self.first, (s1_ra, s1_rb), (y, z), (left, right), (ys, zs))
            ):
                swap.wait()
                span = pl.ds(pl.multiple_of(pos * first, 16), first)
                total = s1_src[self.at, span, lanes].astype(F32)
                for d in range(n - 1):
                    total = total + recv[self.at, d].astype(F32)
                s2_src[self.at, side] = total
                self.second[side].start()

        def to_third(self):
            for side, (swap, recv, pos, n) in enumerate(
                zip(self.second, (s2_ra, s2_rb), (z, y), (zs, ys))
            ):
                swap.wait()
                span = pl.ds(pl.multiple_of(second_at(pos), 16), second)
                total = s2_src[self.at, side, span, :]
                for d in range(n - 1):
                    total = total + recv[self.at, d]
                done = (total * scale).astype(BF)
                fin[self.at, side] = done
                chunk[self.at, side, pl.ds(pl.multiple_of(pos * second, 16), second), :] = done
                self.third[side].start()

        def to_fourth(self):
            for side, (swap, pos, lanes) in enumerate(zip(self.third, (y, z), (left, right))):
                swap.wait()
                self.fourth[side].start()
                span = pl.ds(pl.multiple_of(core * half + pos * first, 16), first)
                self.ref[span, lanes] = chunk[self.at, side, pl.ds(0, first), :]
                self.last[side].start_one(1)

        def to_last(self):
            for i in range(max(ys, zs) - 1):
                for side, swap in enumerate(self.fourth):
                    if i < swap.n - 1:
                        d = 1 + i // 2 if i % 2 == 0 else swap.n - 1 - i // 2
                        swap.wait_one(d)
                        self.last[side].start_one(d + 1)

        def finish(self):
            for swap in self.last:
                swap.wait()

    total2, total1 = Total(0, wg2_ref), Total(1, wg1_ref)

    def own_rows(src, dst, index, size):
        span = pl.ds(pl.multiple_of(index * size, size), size)
        dst[span, :] = src[span, :]

    swap_a.start()
    own_rows(a_send, a_recv, y, ya)

    pr, pc = iota((prows, prows), 0), iota((prows, prows), 1)
    perm[...] = onehot(pc == (pr % ys) * ya + ((pr // ys) % 2) * qs + pr // qa)
    er, ec = iota((prows, slots), 0), iota((prows, slots), 1)
    em[...] = onehot(ec == 2 * ((er % ys) * qs + er // qa) + (er // ys) % 2)

    rim = 32

    def build(k):
        row = kmap[pl.ds(k, 1), :]
        inner = jnp.where(row < rim + slots, row - rim, row)
        column = jnp.where(row < rim, row + slots, jnp.where(row >= slots + 2 * rim, -1, inner))
        oh[k] = onehot(iota(oh.shape[1:], 0) == column)

    unrolled(0, koff // 3, build)

    swap_a.wait()
    b_send[...] = dot(perm[...], a_recv[...]).astype(BF)
    swap_b.start()
    own_rows(b_send, b_recv, q, qa)

    unrolled(koff // 3, koff, build)

    def turn(source, target):
        blocks = rows // LANE

        def step(j):
            at = pl.multiple_of(j * LANE, LANE)
            target[:, pl.ds(at, LANE)] = source[pl.ds(at, LANE), :].astype(F32).T.astype(BF)

        unrolled(0, blocks, step)
        if rows % LANE:
            tail = source[blocks * LANE : rows, :].astype(F32)
            tail = jnp.concatenate([tail, jnp.zeros((LANE - rows % LANE, tail.shape[1]), F32)], 0)
            target[:, blocks * LANE : (blocks + 1) * LANE] = tail.T.astype(BF)

    turn(w1, wt1)
    turn(w2, wt2)
    for gath in (gath1, gath2):
        gath[rows:padded, :] = jnp.zeros((padded - rows, slots), BF)

    both = jnp.concatenate(
        [lists[1:2, :], lists[0:1, :], jnp.full((1, LANE - 2 * rim), -1, I32)], axis=1
    )
    lent = iota((slots, LANE), 0) == both
    side = iota((slots, LANE), 1) < rim
    lend_next, lend_prev = onehot(lent & side), onehot(lent & ~side)
    has_prev = (b > 0).astype(F32)
    has_next = (b < bricks - 1).astype(F32)

    swap_b.wait()
    arrived = dot(b_recv[...].astype(F32).T.astype(BF), em[...])
    occupied = arrived[chans : chans + 1, :]
    voxels = arrived[0:chans, :].astype(BF)
    keep1 = occupied * drop1[...].astype(F32) / KEEP_RATE
    keep2 = occupied * drop2[...].astype(F32) / KEEP_RATE

    def lend(field, halo, at):
        hs[at, 0] = dot(field, lend_next).astype(BF)
        hs[at, 1] = dot(field, lend_prev).astype(BF)
        halo.start()

    def convolve(field, halo, at, gath, wt, summing):
        def inner(k):
            gath[k * chans : (k + 1) * chans, :] = dot(field, oh[k, 0:slots, :]).astype(BF)

        unrolled(0, koff, inner)
        halo.wait()
        edge = hr[at, 0].astype(F32) * has_prev + hr[at, 1].astype(F32) * has_next
        edge = edge.astype(BF)

        def outer(k):
            part = dot(edge, oh[k, slots : slots + LANE, :]).astype(BF)
            gath[k * chans : (k + 1) * chans, :] += part

        unrolled(0, koff, outer)
        rs_send[at] = dot(wt[...], gath[...])
        summing.start()
        own = rs_send[at, pl.ds(pl.multiple_of(x * chans, 16), chans), :]
        summing.wait()
        for d in range(chs - 1):
            own = own + rs_recv[at, d]
        return own

    lend(voxels, halo1, 0)
    conv1 = convolve(voxels, halo1, 0, gath1, wt1, sum1)
    hidden = (conv1 * jax.nn.sigmoid(conv1) * keep1).astype(BF)
    lend(hidden, halo2, 1)
    conv2 = convolve(hidden, halo2, 1, gath2, wt2, sum2)
    summed = voxels.astype(F32) + keep2 * conv2
    grad_pre = cot[...].astype(F32) * slope_silu(summed)
    mine = pl.ds(pl.multiple_of(x * chans, 16), chans)
    full_g[0, mine, :] = (grad_pre * keep2).astype(BF)
    share2.start()
    out_ref[...] = (summed * jax.nn.sigmoid(summed)).astype(BF)

    def push(weight, grads, fold, at):
        g = grads[...]

        def ahead(j):
            span = pl.ds(pl.multiple_of(j * 3 * chans, 16), 3 * chans)
            high, low = split(dot(weight[span, :], g))
            for i in range(3):
                part = slice(i * chans, (i + 1) * chans)
                pushed[3 * j + i, 0:chans, :] = high[part]
                pushed[3 * j + i, chans : 2 * chans, :] = low[part]

        unrolled(0, koff // 3, ahead)
        both = returned(slots, slots + LANE)
        border = both[0:chans] + both[chans : 2 * chans]
        fs[at, 0] = border
        fs[at, 1] = border
        fold.start()

    def returned(low, high):
        part = dot_nt(pushed[0], oh[0, low:high, :])
        for k in range(1, koff):
            part = part + dot_nt(pushed[k], oh[k, low:high, :])
        return part

    def own_columns():
        ret[...] = returned(0, slots)

    def folded(fold, at):
        own = ret[0:chans, :] + ret[chans : 2 * chans, :]
        fold.wait()
        for part in split(fr[at, 0] * has_prev):
            own = own + dot_nt(part, lend_prev)
        for part in split(fr[at, 1] * has_next):
            own = own + dot_nt(part, lend_next)
        return own

    share2.wait()
    push(w2, full_g.at[0], fold2, 0)
    own_columns()
    total2.give(gath2, full_g.at[0])
    grad_hidden = folded(fold2, 0)
    full_g[1, mine, :] = (grad_hidden * keep1 * slope_silu(conv1)).astype(BF)
    share1.start()
    total2.keep(gath2, full_g.at[0])
    total2.to_first()
    share1.wait()
    total1.give(gath1, full_g.at[1])
    push(w1, full_g.at[1], fold1, 1)
    total1.keep(gath1, full_g.at[1])
    total1.to_first()
    own_columns()
    total2.to_second()
    grad_voxels = (grad_pre + folded(fold1, 1)).astype(BF)
    wide = jnp.concatenate([grad_voxels, jnp.zeros((LANE - chans, slots), BF)], axis=0)
    bb_send[...] = dot_nt(em[...], wide).astype(BF)
    back_b.start()
    own_rows(bb_send, bb_recv, q, qa)
    perm_back = onehot(pc == (pr % qs) * qa + ((pr // qs) % 2) * ys + pr // ya)
    total1.to_second()
    total2.to_third()
    back_b.wait()
    ba_send[...] = dot(perm_back, bb_recv[...]).astype(BF)
    back_a.start()
    own_rows(ba_send, ba_recv, y, ya)
    total1.to_third()
    total2.to_fourth()
    total1.to_fourth()
    back_a.wait()
    gf = dot(ba_recv[...].astype(F32).T.astype(BF), pm[...])
    gf_ref[...] = gf[0:chans, :].astype(BF)
    total2.to_last()
    total1.to_last()
    total2.finish()
    total1.finish()

    for swap in (
        swap_a,
        swap_b,
        back_b,
        back_a,
        halo1,
        halo2,
        fold2,
        fold1,
        sum1,
        sum2,
        share2,
        share1,
        *total2.all,
        *total1.all,
    ):
        swap.done()


def store(*refs):
    sources, targets, sem = refs[0:4], refs[4:8], refs[8]
    copies = [
        pltpu.make_async_copy(source.at[pl.ds(0, target.shape[0])], target, sem.at[i])
        for i, (source, target) in enumerate(zip(sources, targets))
    ]
    for copy in copies:
        copy.start()
    for copy in copies:
        copy.wait()


def local(ys, features, owner_map, kernel_map, send_lists, drop1, drop2, w1, w2, cotangent):
    bricks, chs = lax.axis_size("brick"), lax.axis_size("ch")
    chans, scan = features.shape
    koff, slots = kernel_map.shape
    outs = w1.shape[2]
    zs, rows, padded, half, first, second = sizes(bricks, ys, koff, chans, outs)
    qs = zs * CORES
    rim = send_lists.shape[1]
    dims = (
        bricks, ys, zs, chs, koff, chans, rows, padded, half, first, second,
        float(bricks * slots) ** -0.5,
    )
    prows = 2 * bricks
    vm = pltpu.VMEM
    table = slots + LANE
    scratch = [
        vm((koff, table, slots), BF),
        vm((outs, padded), BF),
        vm((outs, padded), BF),
        vm((padded, slots), BF),
        vm((padded, slots), BF),
        vm((koff, 2 * chans, slots), BF),
        vm((2 * chans, slots), F32),
        vm((prows, scan), BF),
        vm((prows, slots), BF),
        vm((prows, prows), BF),
        *[vm((prows, LANE), BF)] * 8,
        vm((2, 2, chans, LANE), BF),
        vm((2, 2, chans, LANE), BF),
        vm((2, 2, chans, LANE), F32),
        vm((2, 2, chans, LANE), F32),
        vm((2, outs, slots), F32),
        vm((2, chs - 1, chans, slots), F32),
        vm((2, outs, slots), BF),
        vm((2, half, outs), F32),
        vm((2, half, outs), BF),
        vm((2, half, outs), BF),
        vm((2, half, outs), BF),
        vm((2, ys - 1, first, LANE), BF),
        vm((2, zs - 1, first, LANE), BF),
        vm((2, 2, first, LANE), F32),
        vm((2, zs - 1, second, LANE), F32),
        vm((2, ys - 1, second, LANE), F32),
        vm((2, 2, second, LANE), BF),
        vm((2, 2, max(ys, zs) * second, LANE), BF),
    ]
    weight_sums = [1, ys - 1, zs - 1, zs - 1, ys - 1, zs - 1, ys - 1, ys - 1, zs - 1, ys, zs]
    copies = [ys - 1, qs - 1, qs - 1, ys - 1, 2, 2, 2, 2] + [chs - 1] * 4 + weight_sums * 2
    for n in copies:
        scratch += [pltpu.SemaphoreType.DMA((n,))] * 2
    shape = jax.ShapeDtypeStruct
    spec = pl.BlockSpec(memory_space=pltpu.VMEM)
    results = pl.pallas_call(
        functools.partial(kernel, dims),
        out_shape=(
            shape((chans, slots), BF),
            shape((chans, scan), BF),
            shape((padded, outs), BF),
            shape((padded, outs), BF),
        ),
        in_specs=[spec] * 9,
        out_specs=(spec,) * 4,
        scratch_shapes=scratch,
        compiler_params=pltpu.CompilerParams(
            collective_id=0, has_side_effects=True, vmem_limit_bytes=56 * 2**20
        ),
        name="block",
    )(
        features, owner_map.reshape(1, scan), send_lists, kernel_map, drop1, drop2,
        w1.reshape(rows, outs), w2.reshape(rows, outs), cotangent,
    )
    anywhere = pl.BlockSpec(memory_space=pl.ANY)
    block_out, grad_features, wg1, wg2 = pl.pallas_call(
        store,
        out_shape=(
            shape((chans, slots), BF),
            shape((chans, scan), BF),
            shape((rows, outs), BF),
            shape((rows, outs), BF),
        ),
        in_specs=[spec] * 4,
        out_specs=(anywhere,) * 4,
        scratch_shapes=[pltpu.SemaphoreType.DMA((4,))],
        name="store",
    )(*results)
    return block_out, grad_features, wg1.reshape(w1.shape), wg2.reshape(w2.shape)


def rows_of_chips(bricks):
    ys = 1
    while ys * ys * CORES < bricks:
        ys *= 2
    return ys


def solution(mesh):
    return jax.shard_map(
        functools.partial(local, rows_of_chips(mesh.shape["brick"])),
        mesh=mesh,
        in_specs=(
            P("ch", "brick"),
            P("brick", None),
            P(None, "brick"),
            P(None, "brick"),
            P("ch", "brick"),
            P("ch", "brick"),
            P(None, "ch", None),
            P(None, "ch", None),
            P("ch", "brick"),
        ),
        out_specs=(P("ch", "brick"), P("ch", "brick"), P(None, "ch", None), P(None, "ch", None)),
        check_vma=False,
    )
```

```python
import functools

import jax
import jax.numpy as jnp
from jax import lax
from jax.experimental import pallas as pl
from jax.experimental.pallas import tpu as pltpu
from jax.sharding import PartitionSpec as P

KEEP_RATE = 0.9
MESH = pl.DeviceIdType.MESH
BF = jnp.bfloat16
F32 = jnp.float32
I32 = jnp.int32
CORES = 2
LANE = 128


def dot(a, b):
    return jnp.dot(a, b, preferred_element_type=F32)


def dot_nt(a, b):
    return lax.dot_general(a, b, (((1,), (1,)), ((), ())), preferred_element_type=F32)


def onehot(mask):
    return jnp.where(mask, 1.0, 0.0).astype(BF)


def iota(shape, dim):
    return lax.broadcasted_iota(I32, shape, dim)


def split(value):
    high = value.astype(BF)
    return high, (value - high.astype(F32)).astype(BF)


def slope_silu(value):
    sig = jax.nn.sigmoid(value)
    return sig * (1.0 + value * (1.0 - sig))


def loop(low, high, body):
    def step(index, carry):
        body(index)
        return carry

    lax.fori_loop(low, high, step, 0)


def unrolled(low, high, body):
    for index in range(low, high):
        body(index)


class Swap:
    def __init__(self, n, peer, src, dst, land, sems):
        self.n, self.peer, self.src, self.dst, self.land = n, peer, src, dst, land
        self.ss, self.rs = sems

    def _copy(self, d, src, dst):
        return pltpu.make_async_remote_copy(
            src_ref=src,
            dst_ref=dst,
            send_sem=self.ss.at[d - 1],
            recv_sem=self.rs.at[d - 1],
            device_id=self.peer(d),
            device_id_type=MESH,
        )

    def start_one(self, d):
        self._copy(d, self.src(d), self.dst(d)).start()

    def wait_one(self, d):
        self._copy(d, self.land(d), self.land(d)).wait_recv()

    def start(self):
        unrolled(1, self.n, self.start_one)

    def wait(self):
        unrolled(1, self.n, self.wait_one)

    def done(self):
        unrolled(1, self.n, lambda d: self._copy(d, self.src(d), self.dst(d)).wait_send())


def sizes(bricks, ys, koff, chans, outs):
    zs = bricks // CORES // ys
    rows = koff * chans
    unit = CORES * ys * 16
    padded = -(-rows // unit) * unit
    padded = -(-padded // LANE) * LANE
    half = padded // CORES
    first = half // ys
    second = -(-first // zs // 16) * 16 if first % zs == 0 else -(-first // (16 * zs)) * 16
    return zs, rows, padded, half, first, second


def kernel(
    dims,
    feat,
    owner,
    lists,
    kmap,
    drop1,
    drop2,
    w1_hbm,
    w2_hbm,
    cot,
    out_ref,
    gf_ref,
    wg1_hbm,
    wg2_hbm,
    w1,
    w2,
    wg1_ref,
    wg2_ref,
    rs_low,
    io_sem,
    oh,
    wt1,
    wt2,
    gath1,
    gath2,
    pushed,
    ret,
    pm,
    em,
    perm,
    a_send,
    a_recv,
    b_send,
    b_recv,
    bb_send,
    bb_recv,
    ba_send,
    ba_recv,
    hs,
    hr,
    fs,
    fr,
    rs_send,
    rs_recv,
    full_g,
    wgf,
    wgb,
    c_recv,
    s1_src,
    s1_ra,
    s1_rb,
    s2_src,
    s2_ra,
    s2_rb,
    fin,
    chunk,
    *sems,
):
    bricks, ys, zs, chs, koff, chans, rows, padded, half, first, second, scale = dims
    qs = zs * CORES
    b, x = lax.axis_index("brick"), lax.axis_index("ch")
    y, q = b // qs, b % qs
    z, core = q // CORES, q % CORES
    slots = kmap.shape[1]
    sem_at = iter([(sems[i], sems[i + 1]) for i in range(0, len(sems), 2)])

    def ring(count, at, step):
        return lax.rem(at + step, count)

    to_y = lambda d: (ring(ys, y, d) * qs + q, x)
    to_q = lambda d: (y * qs + ring(qs, q, d), x)
    to_z = lambda d: (y * qs + ring(zs, z, d) * CORES + core, x)
    to_core = lambda d: (y * qs + z * CORES + (1 - core), x)
    to_ch = lambda d: (b, ring(chs, x, d))
    to_brick = lambda d: (lax.rem(b + 1 + (d - 1) * (bricks - 2), bricks), x)

    fetches = [
        pltpu.make_async_copy(source, target, io_sem.at[i])
        for i, (source, target) in enumerate(((w1_hbm, w1), (w2_hbm, w2)))
    ]
    for fetch in fetches:
        fetch.start()
    results = [
        pltpu.make_async_copy(source.at[pl.ds(0, rows)], target, io_sem.at[2 + i])
        for i, (source, target) in enumerate(((wg1_ref, wg1_hbm), (wg2_ref, wg2_hbm)))
    ]

    barrier = pltpu.get_barrier_semaphore()
    groups = ((to_y, ys), (to_q, qs), (to_ch, chs), (to_brick, 3))
    for peer, n in groups:
        unrolled(
            1,
            n,
            lambda d, peer=peer: pl.semaphore_signal(
                barrier, inc=1, device_id=peer(d), device_id_type=MESH
            ),
        )

    prows = 2 * bricks
    t_row = owner[...]
    scan = t_row.shape[1]
    t_col = jnp.broadcast_to(t_row.astype(F32), (scan, scan)).T.astype(I32)
    earlier = (t_col == t_row) & (iota((scan, scan), 0) < iota((scan, scan), 1))
    ordinal = jnp.sum(jnp.where(earlier, 1.0, 0.0), axis=0, keepdims=True)
    code = (t_row // qs) * (2 * qs) + ordinal.astype(I32) * qs + t_row % qs
    pm[...] = onehot(iota((prows, scan), 0) == code)
    carried = jnp.concatenate(
        [feat[...], jnp.where(iota((LANE - chans, scan), 0) == 0, 1.0, 0.0).astype(BF)], axis=0
    )
    a_send[...] = dot_nt(pm[...], carried).astype(BF)

    pl.semaphore_wait(barrier, sum(n - 1 for _, n in groups))

    def chunk_of(ref, index, size):
        return ref.at[pl.ds(pl.multiple_of(index * size, size), size)]

    ya, qa = 2 * qs, 2 * ys
    swap_a = Swap(
        ys,
        to_y,
        lambda d: chunk_of(a_send, ring(ys, y, d), ya),
        lambda d: chunk_of(a_recv, y, ya),
        lambda d: chunk_of(a_recv, ring(ys, y, ys - d), ya),
        next(sem_at),
    )
    swap_b = Swap(
        qs,
        to_q,
        lambda d: chunk_of(b_send, ring(qs, q, d), qa),
        lambda d: chunk_of(b_recv, q, qa),
        lambda d: chunk_of(b_recv, ring(qs, q, qs - d), qa),
        next(sem_at),
    )
    back_b = Swap(
        qs,
        to_q,
        lambda d: chunk_of(bb_send, ring(qs, q, d), qa),
        lambda d: chunk_of(bb_recv, q, qa),
        lambda d: chunk_of(bb_recv, ring(qs, q, qs - d), qa),
        next(sem_at),
    )
    back_a = Swap(
        ys,
        to_y,
        lambda d: chunk_of(ba_send, ring(ys, y, d), ya),
        lambda d: chunk_of(ba_recv, y, ya),
        lambda d: chunk_of(ba_recv, ring(ys, y, ys - d), ya),
        next(sem_at),
    )

    def neighbours(send, recv, at):
        return Swap(
            3,
            to_brick,
            lambda d: send.at[at, d - 1],
            lambda d: recv.at[at, d - 1],
            lambda d: recv.at[at, d - 1],
            next(sem_at),
        )

    halo1, halo2 = neighbours(hs, hr, 0), neighbours(hs, hr, 1)
    fold2, fold1 = neighbours(fs, fr, 0), neighbours(fs, fr, 1)

    def scatter_sum(at):
        return Swap(
            chs,
            to_ch,
            lambda d: chunk_of(rs_low.at[at], ring(chs, x, d), chans),
            lambda d: rs_recv.at[at, d - 1],
            lambda d: rs_recv.at[at, d - 1],
            next(sem_at),
        )

    sum1, sum2 = scatter_sum(0), scatter_sum(1)

    def share(at):
        return Swap(
            chs,
            to_ch,
            lambda d: chunk_of(full_g.at[at], x, chans),
            lambda d: chunk_of(full_g.at[at], x, chans),
            lambda d: chunk_of(full_g.at[at], ring(chs, x, chs - d), chans),
            next(sem_at),
        )

    share2, share1 = share(0), share(1)

    left, right = pl.ds(0, LANE), pl.ds(LANE, LANE)

    def rows_of(ref, start, size, lanes):
        return ref.at[pl.ds(pl.multiple_of(start, 16), size), lanes]

    def second_at(index):
        return jnp.minimum(index * second, first - second)

    class Total:
        def __init__(self, at, ref):
            self.at, self.ref = at, ref
            self.cores = Swap(
                2,
                to_core,
                lambda d: wgb.at[at],
                lambda d: c_recv.at[at],
                lambda d: c_recv.at[at],
                next(sem_at),
            )
            src = s1_src.at[at]
            self.first = (
                Swap(
                    ys,
                    to_y,
                    lambda d: rows_of(src, ring(ys, y, d) * first, first, left),
                    lambda d: s1_ra.at[at, d - 1],
                    lambda d: s1_ra.at[at, d - 1],
                    next(sem_at),
                ),
                Swap(
                    zs,
                    to_z,
                    lambda d: rows_of(src, ring(zs, z, d) * first, first, right),
                    lambda d: s1_rb.at[at, d - 1],
                    lambda d: s1_rb.at[at, d - 1],
                    next(sem_at),
                ),
            )
            self.second = (
                Swap(
                    zs,
                    to_z,
                    lambda d: s2_src.at[at, 0, pl.ds(pl.multiple_of(second_at(ring(zs, z, d)), 16), second)],
                    lambda d: s2_ra.at[at, d - 1],
                    lambda d: s2_ra.at[at, d - 1],
                    next(sem_at),
                ),
                Swap(
                    ys,
                    to_y,
                    lambda d: s2_src.at[at, 1, pl.ds(pl.multiple_of(second_at(ring(ys, y, d)), 16), second)],
                    lambda d: s2_rb.at[at, d - 1],
                    lambda d: s2_rb.at[at, d - 1],
                    next(sem_at),
                ),
            )
            self.third = (
                Swap(
                    zs,
                    to_z,
                    lambda d: fin.at[at, 0],
                    lambda d: chunk_of(chunk.at[at, 0], z, second),
                    lambda d: chunk_of(chunk.at[at, 0], ring(zs, z, zs - d), second),
                    next(sem_at),
                ),
                Swap(
                    ys,
                    to_y,
                    lambda d: fin.at[at, 1],
                    lambda d: chunk_of(chunk.at[at, 1], y, second),
                    lambda d: chunk_of(chunk.at[at, 1], ring(ys, y, ys - d), second),
                    next(sem_at),
                ),
            )
            self.fourth = (
                Swap(
                    ys,
                    to_y,
                    lambda d: chunk.at[at, 0, pl.ds(0, first)],
                    lambda d: rows_of(ref, core * half + y * first, first, left),
                    lambda d: rows_of(ref, core * half + ring(ys, y, ys - d) * first, first, left),
                    next(sem_at),
                ),
                Swap(
                    zs,
                    to_z,
                    lambda d: chunk.at[at, 1, pl.ds(0, first)],
                    lambda d: rows_of(ref, core * half + z * first, first, right),
                    lambda d: rows_of(ref, core * half + ring(zs, z, zs - d) * first, first, right),
                    next(sem_at),
                ),
            )
            self.last = tuple(
                Swap(
                    n + 1,
                    lambda d: to_core(1),
                    lambda d, n=n, pos=pos, lanes=lanes: rows_of(
                        ref, core * half + ring(n, pos, n + 1 - d) * first, first, lanes
                    ),
                    lambda d, n=n, pos=pos, lanes=lanes: rows_of(
                        ref, core * half + ring(n, pos, n + 1 - d) * first, first, lanes
                    ),
                    lambda d, n=n, pos=pos, lanes=lanes: rows_of(
                        ref, (1 - core) * half + ring(n, pos, n + 1 - d) * first, first, lanes
                    ),
                    next(sem_at),
                )
                for n, pos, lanes in ((ys, y, left), (zs, z, right))
            )
            self.all = (
                self.cores, *self.first, *self.second, *self.third, *self.fourth, *self.last
            )

        def compute(self, gath, grads, which):
            g, block = grads[...], half // 2
            for i in range(2):
                start = which * half + i * block
                yield pl.ds(i * block, block), dot_nt(
                    gath[pl.ds(pl.multiple_of(start, 16), block), :], g
                )

        def give(self, gath, grads):
            for span, part in self.compute(gath, grads, 1 - core):
                wgb[self.at, span, :] = part.astype(BF)
            self.cores.start()

        def keep(self, gath, grads):
            for span, part in self.compute(gath, grads, core):
                wgf[self.at, span, :] = part

        def to_first(self):
            self.cores.wait()
            both = wgf[self.at] + c_recv[self.at].astype(F32)
            s1_src[self.at] = both.astype(BF)
            for swap in self.first:
                swap.start()

        def to_second(self):
            for side, (swap, recv, pos, lanes, n) in enumerate(
                zip(self.first, (s1_ra, s1_rb), (y, z), (left, right), (ys, zs))
            ):
                swap.wait()
                span = pl.ds(pl.multiple_of(pos * first, 16), first)
                total = s1_src[self.at, span, lanes].astype(F32)
                for d in range(n - 1):
                    total = total + recv[self.at, d].astype(F32)
                s2_src[self.at, side] = total
                self.second[side].start()

        def to_third(self):
            for side, (swap, recv, pos, n) in enumerate(
                zip(self.second, (s2_ra, s2_rb), (z, y), (zs, ys))
            ):
                swap.wait()
                span = pl.ds(pl.multiple_of(second_at(pos), 16), second)
                total = s2_src[self.at, side, span, :]
                for d in range(n - 1):
                    total = total + recv[self.at, d]
                done = (total * scale).astype(BF)
                fin[self.at, side] = done
                chunk[self.at, side, pl.ds(pl.multiple_of(pos * second, 16), second), :] = done
                self.third[side].start()

        def to_fourth(self):
            for side, (swap, pos, lanes) in enumerate(zip(self.third, (y, z), (left, right))):
                swap.wait()
                self.fourth[side].start()
                span = pl.ds(pl.multiple_of(core * half + pos * first, 16), first)
                self.ref[span, lanes] = chunk[self.at, side, pl.ds(0, first), :]
                self.last[side].start_one(1)

        def to_last(self):
            for i in range(max(ys, zs) - 1):
                for side, swap in enumerate(self.fourth):
                    if i < swap.n - 1:
                        d = 1 + i // 2 if i % 2 == 0 else swap.n - 1 - i // 2
                        swap.wait_one(d)
                        self.last[side].start_one(d + 1)

        def finish(self):
            for swap in self.last:
                swap.wait()

    total2, total1 = Total(0, wg2_ref), Total(1, wg1_ref)

    def own_rows(src, dst, index, size):
        span = pl.ds(pl.multiple_of(index * size, size), size)
        dst[span, :] = src[span, :]

    swap_a.start()
    own_rows(a_send, a_recv, y, ya)

    pr, pc = iota((prows, prows), 0), iota((prows, prows), 1)
    perm[...] = onehot(pc == (pr % ys) * ya + ((pr // ys) % 2) * qs + pr // qa)
    er, ec = iota((prows, slots), 0), iota((prows, slots), 1)
    em[...] = onehot(ec == 2 * ((er % ys) * qs + er // qa) + (er // ys) % 2)

    rim = 32

    def build(k):
        row = kmap[pl.ds(k, 1), :]
        inner = jnp.where(row < rim + slots, row - rim, row)
        column = jnp.where(row < rim, row + slots, jnp.where(row >= slots + 2 * rim, -1, inner))
        oh[k] = onehot(iota(oh.shape[1:], 0) == column)

    unrolled(0, koff // 3, build)

    swap_a.wait()
    b_send[...] = dot(perm[...], a_recv[...]).astype(BF)
    swap_b.start()
    own_rows(b_send, b_recv, q, qa)

    unrolled(koff // 3, koff, build)

    def turn(source, target):
        blocks = rows // LANE

        def step(j):
            at = pl.multiple_of(j * LANE, LANE)
            target[:, pl.ds(at, LANE)] = source[pl.ds(at, LANE), :].astype(F32).T.astype(BF)

        unrolled(0, blocks, step)
        if rows % LANE:
            tail = source[blocks * LANE : rows, :].astype(F32)
            tail = jnp.concatenate([tail, jnp.zeros((LANE - rows % LANE, tail.shape[1]), F32)], 0)
            target[:, blocks * LANE : (blocks + 1) * LANE] = tail.T.astype(BF)

    for fetch in fetches:
        fetch.wait()
    turn(w1, wt1)
    turn(w2, wt2)
    for gath in (gath1, gath2):
        gath[rows:padded, :] = jnp.zeros((padded - rows, slots), BF)

    both = jnp.concatenate(
        [lists[1:2, :], lists[0:1, :], jnp.full((1, LANE - 2 * rim), -1, I32)], axis=1
    )
    lent = iota((slots, LANE), 0) == both
    side = iota((slots, LANE), 1) < rim
    lend_next, lend_prev = onehot(lent & side), onehot(lent & ~side)
    has_prev = (b > 0).astype(F32)
    has_next = (b < bricks - 1).astype(F32)

    swap_b.wait()
    arrived = dot(b_recv[...].astype(F32).T.astype(BF), em[...])
    occupied = arrived[chans : chans + 1, :]
    voxels = arrived[0:chans, :].astype(BF)
    keep1 = occupied * drop1[...].astype(F32) / KEEP_RATE
    keep2 = occupied * drop2[...].astype(F32) / KEEP_RATE

    def lend(field, halo, at):
        hs[at, 0] = dot(field, lend_next).astype(BF)
        hs[at, 1] = dot(field, lend_prev).astype(BF)
        halo.start()

    def convolve(field, halo, at, gath, wt, summing):
        def inner(k):
            gath[k * chans : (k + 1) * chans, :] = dot(field, oh[k, 0:slots, :]).astype(BF)

        unrolled(0, koff, inner)
        halo.wait()
        edge = hr[at, 0].astype(F32) * has_prev + hr[at, 1].astype(F32) * has_next
        edge = edge.astype(BF)

        def outer(k):
            part = dot(edge, oh[k, slots : slots + LANE, :]).astype(BF)
            gath[k * chans : (k + 1) * chans, :] += part

        unrolled(0, koff, outer)
        partial = dot(wt[...], gath[...])
        rs_low[at] = partial.astype(BF)
        summing.start()
        rs_send[at] = partial
        own = rs_send[at, pl.ds(pl.multiple_of(x * chans, 16), chans), :]
        summing.wait()
        for d in range(chs - 1):
            own = own + rs_recv[at, d].astype(F32)
        return own

    lend(voxels, halo1, 0)
    conv1 = convolve(voxels, halo1, 0, gath1, wt1, sum1)
    hidden = (conv1 * jax.nn.sigmoid(conv1) * keep1).astype(BF)
    lend(hidden, halo2, 1)
    conv2 = convolve(hidden, halo2, 1, gath2, wt2, sum2)
    summed = voxels.astype(F32) + keep2 * conv2
    grad_pre = cot[...].astype(F32) * slope_silu(summed)
    mine = pl.ds(pl.multiple_of(x * chans, 16), chans)
    full_g[0, mine, :] = (grad_pre * keep2).astype(BF)
    share2.start()
    out_ref[...] = (summed * jax.nn.sigmoid(summed)).astype(BF)

    def push(weight, grads, fold, at):
        g = grads[...]

        def ahead(j):
            span = pl.ds(pl.multiple_of(j * 3 * chans, 16), 3 * chans)
            high, low = split(dot(weight[span, :], g))
            for i in range(3):
                part = slice(i * chans, (i + 1) * chans)
                pushed[3 * j + i, 0:chans, :] = high[part]
                pushed[3 * j + i, chans : 2 * chans, :] = low[part]

        unrolled(0, koff // 3, ahead)
        both = returned(slots, slots + LANE)
        border = both[0:chans] + both[chans : 2 * chans]
        fs[at, 0] = border
        fs[at, 1] = border
        fold.start()

    def returned(low, high):
        part = dot_nt(pushed[0], oh[0, low:high, :])
        for k in range(1, koff):
            part = part + dot_nt(pushed[k], oh[k, low:high, :])
        return part

    def own_columns():
        ret[...] = returned(0, slots)

    def folded(fold, at):
        own = ret[0:chans, :] + ret[chans : 2 * chans, :]
        fold.wait()
        for part in split(fr[at, 0] * has_prev):
            own = own + dot_nt(part, lend_prev)
        for part in split(fr[at, 1] * has_next):
            own = own + dot_nt(part, lend_next)
        return own

    share2.wait()
    push(w2, full_g.at[0], fold2, 0)
    own_columns()
    total2.give(gath2, full_g.at[0])
    grad_hidden = folded(fold2, 0)
    full_g[1, mine, :] = (grad_hidden * keep1 * slope_silu(conv1)).astype(BF)
    share1.start()
    total2.keep(gath2, full_g.at[0])
    total2.to_first()
    share1.wait()
    total1.give(gath1, full_g.at[1])
    push(w1, full_g.at[1], fold1, 1)
    total1.keep(gath1, full_g.at[1])
    total1.to_first()
    own_columns()
    total2.to_second()
    grad_voxels = (grad_pre + folded(fold1, 1)).astype(BF)
    wide = jnp.concatenate([grad_voxels, jnp.zeros((LANE - chans, slots), BF)], axis=0)
    bb_send[...] = dot_nt(em[...], wide).astype(BF)
    back_b.start()
    own_rows(bb_send, bb_recv, q, qa)
    perm_back = onehot(pc == (pr % qs) * qa + ((pr // qs) % 2) * ys + pr // ya)
    total1.to_second()
    total2.to_third()
    back_b.wait()
    ba_send[...] = dot(perm_back, bb_recv[...]).astype(BF)
    back_a.start()
    own_rows(ba_send, ba_recv, y, ya)
    total1.to_third()
    total2.to_fourth()
    total1.to_fourth()
    back_a.wait()
    gf = dot(ba_recv[...].astype(F32).T.astype(BF), pm[...])
    gf_ref[...] = gf[0:chans, :].astype(BF)
    total2.to_last()
    for swap in (
        swap_a,
        swap_b,
        back_b,
        back_a,
        halo1,
        halo2,
        fold2,
        fold1,
        sum1,
        sum2,
        share2,
        share1,
        *total2.all[:-2],
        *total1.all[:-4],
    ):
        swap.done()
    total2.finish()
    results[1].start()
    total1.to_last()
    for swap in (*total2.last, *total1.fourth):
        swap.done()
    total1.finish()
    results[0].start()
    for swap in total1.last:
        swap.done()
    for result in results:
        result.wait()


def store(*refs):
    sources, targets, sem = refs[0:4], refs[4:8], refs[8]
    copies = [
        pltpu.make_async_copy(source.at[pl.ds(0, target.shape[0])], target, sem.at[i])
        for i, (source, target) in enumerate(zip(sources, targets))
    ]
    for copy in copies:
        copy.start()
    for copy in copies:
        copy.wait()


def local(ys, features, owner_map, kernel_map, send_lists, drop1, drop2, w1, w2, cotangent):
    bricks, chs = lax.axis_size("brick"), lax.axis_size("ch")
    chans, scan = features.shape
    koff, slots = kernel_map.shape
    outs = w1.shape[2]
    zs, rows, padded, half, first, second = sizes(bricks, ys, koff, chans, outs)
    qs = zs * CORES
    rim = send_lists.shape[1]
    dims = (
        bricks, ys, zs, chs, koff, chans, rows, padded, half, first, second,
        float(bricks * slots) ** -0.5,
    )
    prows = 2 * bricks
    vm = pltpu.VMEM
    table = slots + LANE
    scratch = [
        vm((rows, outs), BF),
        vm((rows, outs), BF),
        vm((padded, outs), BF),
        vm((padded, outs), BF),
        vm((2, outs, slots), BF),
        pltpu.SemaphoreType.DMA((4,)),
        vm((koff, table, slots), BF),
        vm((outs, padded), BF),
        vm((outs, padded), BF),
        vm((padded, slots), BF),
        vm((padded, slots), BF),
        vm((koff, 2 * chans, slots), BF),
        vm((2 * chans, slots), F32),
        vm((prows, scan), BF),
        vm((prows, slots), BF),
        vm((prows, prows), BF),
        *[vm((prows, LANE), BF)] * 8,
        vm((2, 2, chans, LANE), BF),
        vm((2, 2, chans, LANE), BF),
        vm((2, 2, chans, LANE), F32),
        vm((2, 2, chans, LANE), F32),
        vm((2, outs, slots), F32),
        vm((2, chs - 1, chans, slots), BF),
        vm((2, outs, slots), BF),
        vm((2, half, outs), F32),
        vm((2, half, outs), BF),
        vm((2, half, outs), BF),
        vm((2, half, outs), BF),
        vm((2, ys - 1, first, LANE), BF),
        vm((2, zs - 1, first, LANE), BF),
        vm((2, 2, first, LANE), F32),
        vm((2, zs - 1, second, LANE), F32),
        vm((2, ys - 1, second, LANE), F32),
        vm((2, 2, second, LANE), BF),
        vm((2, 2, max(ys, zs) * second, LANE), BF),
    ]
    weight_sums = [1, ys - 1, zs - 1, zs - 1, ys - 1, zs - 1, ys - 1, ys - 1, zs - 1, ys, zs]
    copies = [ys - 1, qs - 1, qs - 1, ys - 1, 2, 2, 2, 2] + [chs - 1] * 4 + weight_sums * 2
    for n in copies:
        scratch += [pltpu.SemaphoreType.DMA((n,))] * 2
    shape = jax.ShapeDtypeStruct
    spec = pl.BlockSpec(memory_space=pltpu.VMEM)
    anywhere = pl.BlockSpec(memory_space=pl.ANY)
    results = pl.pallas_call(
        functools.partial(kernel, dims),
        out_shape=(
            shape((chans, slots), BF),
            shape((chans, scan), BF),
            shape((rows, outs), BF),
            shape((rows, outs), BF),
        ),
        in_specs=[spec] * 6 + [anywhere] * 2 + [spec],
        out_specs=(spec, spec, anywhere, anywhere),
        scratch_shapes=scratch,
        compiler_params=pltpu.CompilerParams(
            collective_id=0, has_side_effects=True, vmem_limit_bytes=56 * 2**20
        ),
        name="block",
    )(
        features, owner_map.reshape(1, scan), send_lists, kernel_map, drop1, drop2,
        w1.reshape(rows, outs), w2.reshape(rows, outs), cotangent,
    )
    block_out, grad_features, wg1, wg2 = pl.pallas_call(
        store,
        out_shape=(
            shape((chans, slots), BF),
            shape((chans, scan), BF),
            shape((rows, outs), BF),
            shape((rows, outs), BF),
        ),
        in_specs=[spec] * 4,
        out_specs=(anywhere,) * 4,
        scratch_shapes=[pltpu.SemaphoreType.DMA((4,))],
        name="store",
    )(*results)
    return block_out, grad_features, wg1.reshape(w1.shape), wg2.reshape(w2.shape)


def rows_of_chips(bricks):
    ys = 1
    while ys * ys * CORES < bricks:
        ys *= 2
    return ys


def solution(mesh):
    return jax.shard_map(
        functools.partial(local, rows_of_chips(mesh.shape["brick"])),
        mesh=mesh,
        in_specs=(
            P("ch", "brick"),
            P("brick", None),
            P(None, "brick"),
            P(None, "brick"),
            P("ch", "brick"),
            P("ch", "brick"),
            P(None, "ch", None),
            P(None, "ch", None),
            P("ch", "brick"),
        ),
        out_specs=(P("ch", "brick"), P("ch", "brick"), P(None, "ch", None), P(None, "ch", None)),
        check_vma=False,
    )
```

```python
import functools

import jax
import jax.numpy as jnp
from jax import lax
from jax.experimental import pallas as pl
from jax.experimental.pallas import tpu as pltpu
from jax.sharding import PartitionSpec as P

KEEP_RATE = 0.9
MESH = pl.DeviceIdType.MESH
BF = jnp.bfloat16
F32 = jnp.float32
I32 = jnp.int32
CORES = 2
LANE = 128


def dot(a, b):
    return jnp.dot(a, b, preferred_element_type=F32)


def dot_nt(a, b):
    return lax.dot_general(a, b, (((1,), (1,)), ((), ())), preferred_element_type=F32)


def onehot(mask):
    return jnp.where(mask, 1.0, 0.0).astype(BF)


def iota(shape, dim):
    return lax.broadcasted_iota(I32, shape, dim)


def split(value):
    high = value.astype(BF)
    return high, (value - high.astype(F32)).astype(BF)


def slope_silu(value):
    sig = jax.nn.sigmoid(value)
    return sig * (1.0 + value * (1.0 - sig))


def loop(low, high, body):
    def step(index, carry):
        body(index)
        return carry

    lax.fori_loop(low, high, step, 0)


def unrolled(low, high, body):
    for index in range(low, high):
        body(index)


class Swap:
    def __init__(self, n, peer, src, dst, land, sems):
        self.n, self.peer, self.src, self.dst, self.land = n, peer, src, dst, land
        self.ss, self.rs = sems

    def _copy(self, d, src, dst):
        return pltpu.make_async_remote_copy(
            src_ref=src,
            dst_ref=dst,
            send_sem=self.ss.at[d - 1],
            recv_sem=self.rs.at[d - 1],
            device_id=self.peer(d),
            device_id_type=MESH,
        )

    def start_one(self, d):
        self._copy(d, self.src(d), self.dst(d)).start()

    def wait_one(self, d):
        self._copy(d, self.land(d), self.land(d)).wait_recv()

    def start(self):
        unrolled(1, self.n, self.start_one)

    def wait(self):
        unrolled(1, self.n, self.wait_one)

    def done(self):
        unrolled(1, self.n, lambda d: self._copy(d, self.src(d), self.dst(d)).wait_send())


def sizes(bricks, ys, koff, chans, outs):
    zs = bricks // CORES // ys
    rows = koff * chans
    unit = CORES * ys * 16
    padded = -(-rows // unit) * unit
    padded = -(-padded // LANE) * LANE
    half = padded // CORES
    first = half // ys
    second = -(-first // zs // 16) * 16 if first % zs == 0 else -(-first // (16 * zs)) * 16
    return zs, rows, padded, half, first, second


def kernel(
    dims,
    *refs,
):
    sources, targets, held = refs[0:9], refs[9:13], refs[13:24]
    feat, owner, lists, kmap, drop1, drop2, w1, w2, cot, out_ref, gf_ref = held
    body(dims, sources, targets, feat, owner, lists, kmap, drop1, drop2, w1, w2, cot, out_ref, gf_ref, *refs[24:])


def body(
    dims,
    sources,
    targets,
    feat,
    owner,
    lists,
    kmap,
    drop1,
    drop2,
    w1,
    w2,
    cot,
    out_ref,
    gf_ref,
    wg1_ref,
    wg2_ref,
    rs_low,
    io_sem,
    oh,
    wt1,
    wt2,
    gath1,
    gath2,
    pushed,
    ret,
    pm,
    em,
    perm,
    a_send,
    a_recv,
    b_send,
    b_recv,
    bb_send,
    bb_recv,
    ba_send,
    ba_recv,
    hs,
    hr,
    fs,
    fr,
    rs_send,
    rs_recv,
    full_g,
    wgf,
    wgb,
    c_recv,
    s1_src,
    s1_ra,
    s1_rb,
    s2_src,
    s2_ra,
    s2_rb,
    fin,
    chunk,
    *sems,
):
    bricks, ys, zs, chs, koff, chans, rows, padded, half, first, second, scale = dims
    qs = zs * CORES
    b, x = lax.axis_index("brick"), lax.axis_index("ch")
    y, q = b // qs, b % qs
    z, core = q // CORES, q % CORES
    slots = kmap.shape[1]
    sem_at = iter([(sems[i], sems[i + 1]) for i in range(0, len(sems), 2)])

    def ring(count, at, step):
        return lax.rem(at + step, count)

    to_y = lambda d: (ring(ys, y, d) * qs + q, x)
    to_q = lambda d: (y * qs + ring(qs, q, d), x)
    to_z = lambda d: (y * qs + ring(zs, z, d) * CORES + core, x)
    to_core = lambda d: (y * qs + z * CORES + (1 - core), x)
    to_ch = lambda d: (b, ring(chs, x, d))
    to_brick = lambda d: (lax.rem(b + 1 + (d - 1) * (bricks - 2), bricks), x)

    barrier = pltpu.get_barrier_semaphore()
    groups = ((to_y, ys), (to_q, qs), (to_ch, chs), (to_brick, 3))
    for peer, n in groups:
        unrolled(
            1,
            n,
            lambda d, peer=peer: pl.semaphore_signal(
                barrier, inc=1, device_id=peer(d), device_id_type=MESH
            ),
        )

    inputs = (feat, owner, lists, kmap, drop1, drop2, w1, w2, cot)
    fetches = [
        pltpu.make_async_copy(source, target, io_sem.at[i])
        for i, (source, target) in enumerate(zip(sources, inputs))
    ]
    for fetch in fetches:
        fetch.start()
    lower, upper = pl.ds(0, half), pl.ds(half, rows - half)
    leaving = (
        (out_ref, targets[0]),
        (gf_ref, targets[1]),
        (wg2_ref.at[pl.ds(0, rows)], targets[3]),
        (wg1_ref.at[lower], targets[2].at[lower]),
        (wg1_ref.at[upper], targets[2].at[upper]),
    )
    results = [
        pltpu.make_async_copy(source, target, io_sem.at[9 + i])
        for i, (source, target) in enumerate(leaving)
    ]
    for fetch in fetches[0:2]:
        fetch.wait()

    prows = 2 * bricks
    t_row = owner[...]
    scan = t_row.shape[1]
    t_col = jnp.broadcast_to(t_row.astype(F32), (scan, scan)).T.astype(I32)
    earlier = (t_col == t_row) & (iota((scan, scan), 0) < iota((scan, scan), 1))
    ordinal = jnp.sum(jnp.where(earlier, 1.0, 0.0), axis=0, keepdims=True)
    code = (t_row // qs) * (2 * qs) + ordinal.astype(I32) * qs + t_row % qs
    pm[...] = onehot(iota((prows, scan), 0) == code)
    carried = jnp.concatenate(
        [feat[...], jnp.where(iota((LANE - chans, scan), 0) == 0, 1.0, 0.0).astype(BF)], axis=0
    )
    a_send[...] = dot_nt(pm[...], carried).astype(BF)

    pl.semaphore_wait(barrier, sum(n - 1 for _, n in groups))

    def chunk_of(ref, index, size):
        return ref.at[pl.ds(pl.multiple_of(index * size, size), size)]

    ya, qa = 2 * qs, 2 * ys
    swap_a = Swap(
        ys,
        to_y,
        lambda d: chunk_of(a_send, ring(ys, y, d), ya),
        lambda d: chunk_of(a_recv, y, ya),
        lambda d: chunk_of(a_recv, ring(ys, y, ys - d), ya),
        next(sem_at),
    )
    swap_b = Swap(
        qs,
        to_q,
        lambda d: chunk_of(b_send, ring(qs, q, d), qa),
        lambda d: chunk_of(b_recv, q, qa),
        lambda d: chunk_of(b_recv, ring(qs, q, qs - d), qa),
        next(sem_at),
    )
    back_b = Swap(
        qs,
        to_q,
        lambda d: chunk_of(bb_send, ring(qs, q, d), qa),
        lambda d: chunk_of(bb_recv, q, qa),
        lambda d: chunk_of(bb_recv, ring(qs, q, qs - d), qa),
        next(sem_at),
    )
    back_a = Swap(
        ys,
        to_y,
        lambda d: chunk_of(ba_send, ring(ys, y, d), ya),
        lambda d: chunk_of(ba_recv, y, ya),
        lambda d: chunk_of(ba_recv, ring(ys, y, ys - d), ya),
        next(sem_at),
    )

    def neighbours(send, recv, at):
        return Swap(
            3,
            to_brick,
            lambda d: send.at[at, d - 1],
            lambda d: recv.at[at, d - 1],
            lambda d: recv.at[at, d - 1],
            next(sem_at),
        )

    halo1, halo2 = neighbours(hs, hr, 0), neighbours(hs, hr, 1)
    fold2, fold1 = neighbours(fs, fr, 0), neighbours(fs, fr, 1)

    def scatter_sum(at):
        return Swap(
            chs,
            to_ch,
            lambda d: chunk_of(rs_low.at[at], ring(chs, x, d), chans),
            lambda d: rs_recv.at[at, d - 1],
            lambda d: rs_recv.at[at, d - 1],
            next(sem_at),
        )

    sum1, sum2 = scatter_sum(0), scatter_sum(1)

    def share(at):
        return Swap(
            chs,
            to_ch,
            lambda d: chunk_of(full_g.at[at], x, chans),
            lambda d: chunk_of(full_g.at[at], x, chans),
            lambda d: chunk_of(full_g.at[at], ring(chs, x, chs - d), chans),
            next(sem_at),
        )

    share2, share1 = share(0), share(1)

    left, right = pl.ds(0, LANE), pl.ds(LANE, LANE)

    def rows_of(ref, start, size, lanes):
        return ref.at[pl.ds(pl.multiple_of(start, 16), size), lanes]

    def second_at(index):
        return jnp.minimum(index * second, first - second)

    class Total:
        def __init__(self, at, ref):
            self.at, self.ref = at, ref
            self.cores = Swap(
                2,
                to_core,
                lambda d: wgb.at[at],
                lambda d: c_recv.at[at],
                lambda d: c_recv.at[at],
                next(sem_at),
            )
            src = s1_src.at[at]
            self.first = (
                Swap(
                    ys,
                    to_y,
                    lambda d: rows_of(src, ring(ys, y, d) * first, first, left),
                    lambda d: s1_ra.at[at, d - 1],
                    lambda d: s1_ra.at[at, d - 1],
                    next(sem_at),
                ),
                Swap(
                    zs,
                    to_z,
                    lambda d: rows_of(src, ring(zs, z, d) * first, first, right),
                    lambda d: s1_rb.at[at, d - 1],
                    lambda d: s1_rb.at[at, d - 1],
                    next(sem_at),
                ),
            )
            self.second = (
                Swap(
                    zs,
                    to_z,
                    lambda d: s2_src.at[at, 0, pl.ds(pl.multiple_of(second_at(ring(zs, z, d)), 16), second)],
                    lambda d: s2_ra.at[at, d - 1],
                    lambda d: s2_ra.at[at, d - 1],
                    next(sem_at),
                ),
                Swap(
                    ys,
                    to_y,
                    lambda d: s2_src.at[at, 1, pl.ds(pl.multiple_of(second_at(ring(ys, y, d)), 16), second)],
                    lambda d: s2_rb.at[at, d - 1],
                    lambda d: s2_rb.at[at, d - 1],
                    next(sem_at),
                ),
            )
            self.third = (
                Swap(
                    zs,
                    to_z,
                    lambda d: fin.at[at, 0],
                    lambda d: chunk_of(chunk.at[at, 0], z, second),
                    lambda d: chunk_of(chunk.at[at, 0], ring(zs, z, zs - d), second),
                    next(sem_at),
                ),
                Swap(
                    ys,
                    to_y,
                    lambda d: fin.at[at, 1],
                    lambda d: chunk_of(chunk.at[at, 1], y, second),
                    lambda d: chunk_of(chunk.at[at, 1], ring(ys, y, ys - d), second),
                    next(sem_at),
                ),
            )
            self.fourth = (
                Swap(
                    ys,
                    to_y,
                    lambda d: chunk.at[at, 0, pl.ds(0, first)],
                    lambda d: rows_of(ref, core * half + y * first, first, left),
                    lambda d: rows_of(ref, core * half + ring(ys, y, ys - d) * first, first, left),
                    next(sem_at),
                ),
                Swap(
                    zs,
                    to_z,
                    lambda d: chunk.at[at, 1, pl.ds(0, first)],
                    lambda d: rows_of(ref, core * half + z * first, first, right),
                    lambda d: rows_of(ref, core * half + ring(zs, z, zs - d) * first, first, right),
                    next(sem_at),
                ),
            )
            self.last = tuple(
                Swap(
                    n + 1,
                    lambda d: to_core(1),
                    lambda d, n=n, pos=pos, lanes=lanes: rows_of(
                        ref, core * half + ring(n, pos, n + 1 - d) * first, first, lanes
                    ),
                    lambda d, n=n, pos=pos, lanes=lanes: rows_of(
                        ref, core * half + ring(n, pos, n + 1 - d) * first, first, lanes
                    ),
                    lambda d, n=n, pos=pos, lanes=lanes: rows_of(
                        ref, (1 - core) * half + ring(n, pos, n + 1 - d) * first, first, lanes
                    ),
                    next(sem_at),
                )
                for n, pos, lanes in ((ys, y, left), (zs, z, right))
            )
            self.all = (
                self.cores, *self.first, *self.second, *self.third, *self.fourth, *self.last
            )

        def compute(self, gath, grads, which):
            g, block = grads[...], half // 2
            for i in range(2):
                start = which * half + i * block
                yield pl.ds(i * block, block), dot_nt(
                    gath[pl.ds(pl.multiple_of(start, 16), block), :], g
                )

        def give(self, gath, grads):
            for span, part in self.compute(gath, grads, 1 - core):
                wgb[self.at, span, :] = part.astype(BF)
            self.cores.start()

        def keep(self, gath, grads):
            for span, part in self.compute(gath, grads, core):
                wgf[self.at, span, :] = part

        def to_first(self):
            self.cores.wait()
            for swap, lanes in zip(self.first, (left, right)):
                both = wgf[self.at, :, lanes] + c_recv[self.at, :, lanes].astype(F32)
                s1_src[self.at, :, lanes] = both.astype(BF)
                swap.start()

        def to_second(self):
            for side, (swap, recv, pos, lanes, n) in enumerate(
                zip(self.first, (s1_ra, s1_rb), (y, z), (left, right), (ys, zs))
            ):
                swap.wait()
                span = pl.ds(pl.multiple_of(pos * first, 16), first)
                total = s1_src[self.at, span, lanes].astype(F32)
                for d in range(n - 1):
                    total = total + recv[self.at, d].astype(F32)
                s2_src[self.at, side] = total
                self.second[side].start()

        def to_third(self):
            for side, (swap, recv, pos, n) in enumerate(
                zip(self.second, (s2_ra, s2_rb), (z, y), (zs, ys))
            ):
                swap.wait()
                span = pl.ds(pl.multiple_of(second_at(pos), 16), second)
                total = s2_src[self.at, side, span, :]
                for d in range(n - 1):
                    total = total + recv[self.at, d]
                done = (total * scale).astype(BF)
                fin[self.at, side] = done
                chunk[self.at, side, pl.ds(pl.multiple_of(pos * second, 16), second), :] = done
                self.third[side].start()

        def to_fourth(self):
            for side, (swap, pos, lanes) in enumerate(zip(self.third, (y, z), (left, right))):
                swap.wait()
                self.fourth[side].start()
                span = pl.ds(pl.multiple_of(core * half + pos * first, 16), first)
                self.ref[span, lanes] = chunk[self.at, side, pl.ds(0, first), :]
                self.last[side].start_one(1)

        def to_last(self):
            for i in range(max(ys, zs) - 1):
                for side, swap in enumerate(self.fourth):
                    if i < swap.n - 1:
                        d = 1 + i // 2 if i % 2 == 0 else swap.n - 1 - i // 2
                        swap.wait_one(d)
                        self.last[side].start_one(d + 1)

        def finish(self):
            for swap in self.last:
                swap.wait()

    total2, total1 = Total(0, wg2_ref), Total(1, wg1_ref)

    def own_rows(src, dst, index, size):
        span = pl.ds(pl.multiple_of(index * size, size), size)
        dst[span, :] = src[span, :]

    swap_a.start()
    own_rows(a_send, a_recv, y, ya)

    pr, pc = iota((prows, prows), 0), iota((prows, prows), 1)
    perm[...] = onehot(pc == (pr % ys) * ya + ((pr // ys) % 2) * qs + pr // qa)
    er, ec = iota((prows, slots), 0), iota((prows, slots), 1)
    em[...] = onehot(ec == 2 * ((er % ys) * qs + er // qa) + (er // ys) % 2)

    rim = 32

    def build(k):
        row = kmap[pl.ds(k, 1), :]
        inner = jnp.where(row < rim + slots, row - rim, row)
        column = jnp.where(row < rim, row + slots, jnp.where(row >= slots + 2 * rim, -1, inner))
        oh[k] = onehot(iota(oh.shape[1:], 0) == column)

    for fetch in fetches[2:4]:
        fetch.wait()
    unrolled(0, koff // 3, build)

    swap_a.wait()
    b_send[...] = dot(perm[...], a_recv[...]).astype(BF)
    swap_b.start()
    own_rows(b_send, b_recv, q, qa)

    unrolled(koff // 3, koff, build)

    def turn(source, target):
        blocks = rows // LANE

        def step(j):
            at = pl.multiple_of(j * LANE, LANE)
            target[:, pl.ds(at, LANE)] = source[pl.ds(at, LANE), :].astype(F32).T.astype(BF)

        unrolled(0, blocks, step)
        if rows % LANE:
            tail = source[blocks * LANE : rows, :].astype(F32)
            tail = jnp.concatenate([tail, jnp.zeros((LANE - rows % LANE, tail.shape[1]), F32)], 0)
            target[:, blocks * LANE : (blocks + 1) * LANE] = tail.T.astype(BF)

    for fetch in fetches[4:9]:
        fetch.wait()
    turn(w1, wt1)
    turn(w2, wt2)
    for gath in (gath1, gath2):
        gath[rows:padded, :] = jnp.zeros((padded - rows, slots), BF)

    both = jnp.concatenate(
        [lists[1:2, :], lists[0:1, :], jnp.full((1, LANE - 2 * rim), -1, I32)], axis=1
    )
    lent = iota((slots, LANE), 0) == both
    side = iota((slots, LANE), 1) < rim
    lend_next, lend_prev = onehot(lent & side), onehot(lent & ~side)
    has_prev = (b > 0).astype(F32)
    has_next = (b < bricks - 1).astype(F32)

    swap_b.wait()
    arrived = dot(b_recv[...].astype(F32).T.astype(BF), em[...])
    occupied = arrived[chans : chans + 1, :]
    voxels = arrived[0:chans, :].astype(BF)
    keep1 = occupied * drop1[...].astype(F32) / KEEP_RATE
    keep2 = occupied * drop2[...].astype(F32) / KEEP_RATE

    def lend(field, halo, at):
        hs[at, 0] = dot(field, lend_next).astype(BF)
        hs[at, 1] = dot(field, lend_prev).astype(BF)
        halo.start()

    def convolve(field, halo, at, gath, wt, summing):
        def inner(k):
            gath[k * chans : (k + 1) * chans, :] = dot(field, oh[k, 0:slots, :]).astype(BF)

        unrolled(0, koff, inner)
        halo.wait()
        edge = hr[at, 0].astype(F32) * has_prev + hr[at, 1].astype(F32) * has_next
        edge = edge.astype(BF)

        def outer(k):
            part = dot(edge, oh[k, slots : slots + LANE, :]).astype(BF)
            gath[k * chans : (k + 1) * chans, :] += part

        unrolled(0, koff, outer)
        partial = dot(wt[...], gath[...])
        rs_low[at] = partial.astype(BF)
        summing.start()
        rs_send[at] = partial
        own = rs_send[at, pl.ds(pl.multiple_of(x * chans, 16), chans), :]
        summing.wait()
        for d in range(chs - 1):
            own = own + rs_recv[at, d].astype(F32)
        return own

    lend(voxels, halo1, 0)
    conv1 = convolve(voxels, halo1, 0, gath1, wt1, sum1)
    hidden = (conv1 * jax.nn.sigmoid(conv1) * keep1).astype(BF)
    lend(hidden, halo2, 1)
    conv2 = convolve(hidden, halo2, 1, gath2, wt2, sum2)
    summed = voxels.astype(F32) + keep2 * conv2
    grad_pre = cot[...].astype(F32) * slope_silu(summed)
    mine = pl.ds(pl.multiple_of(x * chans, 16), chans)
    full_g[0, mine, :] = (grad_pre * keep2).astype(BF)
    share2.start()
    out_ref[...] = (summed * jax.nn.sigmoid(summed)).astype(BF)
    results[0].start()

    def push(weight, grads, fold, at):
        g = grads[...]

        def ahead(j):
            span = pl.ds(pl.multiple_of(j * 3 * chans, 16), 3 * chans)
            high, low = split(dot(weight[span, :], g))
            for i in range(3):
                part = slice(i * chans, (i + 1) * chans)
                pushed[3 * j + i, 0:chans, :] = high[part]
                pushed[3 * j + i, chans : 2 * chans, :] = low[part]

        unrolled(0, koff // 3, ahead)
        both = returned(slots, slots + LANE)
        border = both[0:chans] + both[chans : 2 * chans]
        fs[at, 0] = border
        fs[at, 1] = border
        fold.start()

    def returned(low, high):
        part = dot_nt(pushed[0], oh[0, low:high, :])
        for k in range(1, koff):
            part = part + dot_nt(pushed[k], oh[k, low:high, :])
        return part

    def own_columns():
        ret[...] = returned(0, slots)

    def folded(fold, at):
        own = ret[0:chans, :] + ret[chans : 2 * chans, :]
        fold.wait()
        for part in split(fr[at, 0] * has_prev):
            own = own + dot_nt(part, lend_prev)
        for part in split(fr[at, 1] * has_next):
            own = own + dot_nt(part, lend_next)
        return own

    share2.wait()
    push(w2, full_g.at[0], fold2, 0)
    own_columns()
    total2.give(gath2, full_g.at[0])
    grad_hidden = folded(fold2, 0)
    full_g[1, mine, :] = (grad_hidden * keep1 * slope_silu(conv1)).astype(BF)
    share1.start()
    total2.keep(gath2, full_g.at[0])
    total2.to_first()
    share1.wait()
    total1.give(gath1, full_g.at[1])
    push(w1, full_g.at[1], fold1, 1)
    total1.keep(gath1, full_g.at[1])
    total1.to_first()
    own_columns()
    total2.to_second()
    grad_voxels = (grad_pre + folded(fold1, 1)).astype(BF)
    wide = jnp.concatenate([grad_voxels, jnp.zeros((LANE - chans, slots), BF)], axis=0)
    bb_send[...] = dot_nt(em[...], wide).astype(BF)
    back_b.start()
    own_rows(bb_send, bb_recv, q, qa)
    perm_back = onehot(pc == (pr % qs) * qa + ((pr // qs) % 2) * ys + pr // ya)
    total1.to_second()
    total2.to_third()
    back_b.wait()
    ba_send[...] = dot(perm_back, bb_recv[...]).astype(BF)
    back_a.start()
    own_rows(ba_send, ba_recv, y, ya)
    total1.to_third()
    total2.to_fourth()
    total1.to_fourth()
    back_a.wait()
    gf = dot(ba_recv[...].astype(F32).T.astype(BF), pm[...])
    gf_ref[...] = gf[0:chans, :].astype(BF)
    results[1].start()
    total2.to_last()
    for swap in (
        swap_a,
        swap_b,
        back_b,
        back_a,
        halo1,
        halo2,
        fold2,
        fold1,
        sum1,
        sum2,
        share2,
        share1,
        *total2.all[:-2],
        *total1.all[:-4],
    ):
        swap.done()
    total2.finish()
    results[2].start()
    total1.to_last()

    @pl.when(core == 0)
    def _():
        results[3].start()

    @pl.when(core == 1)
    def _():
        results[4].start()

    for swap in (*total2.last, *total1.fourth):
        swap.done()
    total1.finish()

    @pl.when(core == 1)
    def _():
        results[3].start()

    @pl.when(core == 0)
    def _():
        results[4].start()

    for swap in total1.last:
        swap.done()
    for result in results:
        result.wait()


def store(*refs):
    sources, targets, sem = refs[0:4], refs[4:8], refs[8]
    copies = [
        pltpu.make_async_copy(source.at[pl.ds(0, target.shape[0])], target, sem.at[i])
        for i, (source, target) in enumerate(zip(sources, targets))
    ]
    for copy in copies:
        copy.start()
    for copy in copies:
        copy.wait()


def local(ys, features, owner_map, kernel_map, send_lists, drop1, drop2, w1, w2, cotangent):
    bricks, chs = lax.axis_size("brick"), lax.axis_size("ch")
    chans, scan = features.shape
    koff, slots = kernel_map.shape
    outs = w1.shape[2]
    zs, rows, padded, half, first, second = sizes(bricks, ys, koff, chans, outs)
    qs = zs * CORES
    rim = send_lists.shape[1]
    dims = (
        bricks, ys, zs, chs, koff, chans, rows, padded, half, first, second,
        float(bricks * slots) ** -0.5,
    )
    prows = 2 * bricks
    vm = pltpu.VMEM
    table = slots + LANE
    scratch = [
        vm((chans, scan), BF),
        vm((1, scan), I32),
        vm(send_lists.shape, I32),
        vm((koff, slots), I32),
        vm((chans, slots), I32),
        vm((chans, slots), I32),
        vm((rows, outs), BF),
        vm((rows, outs), BF),
        vm((chans, slots), BF),
        vm((chans, slots), BF),
        vm((chans, scan), BF),
        vm((padded, outs), BF),
        vm((padded, outs), BF),
        vm((2, outs, slots), BF),
        pltpu.SemaphoreType.DMA((14,)),
        vm((koff, table, slots), BF),
        vm((outs, padded), BF),
        vm((outs, padded), BF),
        vm((padded, slots), BF),
        vm((padded, slots), BF),
        vm((koff, 2 * chans, slots), BF),
        vm((2 * chans, slots), F32),
        vm((prows, scan), BF),
        vm((prows, slots), BF),
        vm((prows, prows), BF),
        *[vm((prows, LANE), BF)] * 8,
        vm((2, 2, chans, LANE), BF),
        vm((2, 2, chans, LANE), BF),
        vm((2, 2, chans, LANE), F32),
        vm((2, 2, chans, LANE), F32),
        vm((2, outs, slots), F32),
        vm((2, chs - 1, chans, slots), BF),
        vm((2, outs, slots), BF),
        vm((2, half, outs), F32),
        vm((2, half, outs), BF),
        vm((2, half, outs), BF),
        vm((2, half, outs), BF),
        vm((2, ys - 1, first, LANE), BF),
        vm((2, zs - 1, first, LANE), BF),
        vm((2, 2, first, LANE), F32),
        vm((2, zs - 1, second, LANE), F32),
        vm((2, ys - 1, second, LANE), F32),
        vm((2, 2, second, LANE), BF),
        vm((2, 2, max(ys, zs) * second, LANE), BF),
    ]
    weight_sums = [1, ys - 1, zs - 1, zs - 1, ys - 1, zs - 1, ys - 1, ys - 1, zs - 1, ys, zs]
    copies = [ys - 1, qs - 1, qs - 1, ys - 1, 2, 2, 2, 2] + [chs - 1] * 4 + weight_sums * 2
    for n in copies:
        scratch += [pltpu.SemaphoreType.DMA((n,))] * 2
    shape = jax.ShapeDtypeStruct
    spec = pl.BlockSpec(memory_space=pltpu.VMEM)
    anywhere = pl.BlockSpec(memory_space=pl.ANY)
    results = pl.pallas_call(
        functools.partial(kernel, dims),
        out_shape=(
            shape((chans, slots), BF),
            shape((chans, scan), BF),
            shape((rows, outs), BF),
            shape((rows, outs), BF),
        ),
        in_specs=[anywhere] * 9,
        out_specs=(anywhere,) * 4,
        scratch_shapes=scratch,
        compiler_params=pltpu.CompilerParams(
            collective_id=0, has_side_effects=True, vmem_limit_bytes=56 * 2**20
        ),
        name="block",
    )(
        features, owner_map.reshape(1, scan), send_lists, kernel_map, drop1, drop2,
        w1.reshape(rows, outs), w2.reshape(rows, outs), cotangent,
    )
    block_out, grad_features, wg1, wg2 = pl.pallas_call(
        store,
        out_shape=(
            shape((chans, slots), BF),
            shape((chans, scan), BF),
            shape((rows, outs), BF),
            shape((rows, outs), BF),
        ),
        in_specs=[spec] * 4,
        out_specs=(anywhere,) * 4,
        scratch_shapes=[pltpu.SemaphoreType.DMA((4,))],
        name="store",
    )(*results)
    return block_out, grad_features, wg1.reshape(w1.shape), wg2.reshape(w2.shape)


def rows_of_chips(bricks):
    ys = 1
    while ys * ys * CORES < bricks:
        ys *= 2
    return ys


def solution(mesh):
    return jax.shard_map(
        functools.partial(local, rows_of_chips(mesh.shape["brick"])),
        mesh=mesh,
        in_specs=(
            P("ch", "brick"),
            P("brick", None),
            P(None, "brick"),
            P(None, "brick"),
            P("ch", "brick"),
            P("ch", "brick"),
            P(None, "ch", None),
            P(None, "ch", None),
            P("ch", "brick"),
        ),
        out_specs=(P("ch", "brick"), P("ch", "brick"), P(None, "ch", None), P(None, "ch", None)),
        check_vma=False,
    )
```

```python
import functools

import jax
import jax.numpy as jnp
from jax import lax
from jax.experimental import pallas as pl
from jax.experimental.pallas import tpu as pltpu
from jax.sharding import PartitionSpec as P

KEEP_RATE = 0.9
MESH = pl.DeviceIdType.MESH
BF = jnp.bfloat16
F32 = jnp.float32
I32 = jnp.int32
CORES = 2
LANE = 128


def dot(a, b):
    return jnp.dot(a, b, preferred_element_type=F32)


def dot_nt(a, b):
    return lax.dot_general(a, b, (((1,), (1,)), ((), ())), preferred_element_type=F32)


def onehot(mask):
    return jnp.where(mask, 1.0, 0.0).astype(BF)


def iota(shape, dim):
    return lax.broadcasted_iota(I32, shape, dim)


def split(value):
    high = value.astype(BF)
    return high, (value - high.astype(F32)).astype(BF)


def slope_silu(value):
    sig = jax.nn.sigmoid(value)
    return sig * (1.0 + value * (1.0 - sig))


def loop(low, high, body):
    def step(index, carry):
        body(index)
        return carry

    lax.fori_loop(low, high, step, 0)


def unrolled(low, high, body):
    for index in range(low, high):
        body(index)


class Swap:
    def __init__(self, n, peer, src, dst, land, sems):
        self.n, self.peer, self.src, self.dst, self.land = n, peer, src, dst, land
        self.ss, self.rs = sems

    def _copy(self, d, src, dst):
        return pltpu.make_async_remote_copy(
            src_ref=src,
            dst_ref=dst,
            send_sem=self.ss.at[d - 1],
            recv_sem=self.rs.at[d - 1],
            device_id=self.peer(d),
            device_id_type=MESH,
        )

    def start_one(self, d):
        self._copy(d, self.src(d), self.dst(d)).start()

    def wait_one(self, d):
        self._copy(d, self.land(d), self.land(d)).wait_recv()

    def start(self):
        unrolled(1, self.n, self.start_one)

    def wait(self):
        unrolled(1, self.n, self.wait_one)

    def done(self):
        unrolled(1, self.n, lambda d: self._copy(d, self.src(d), self.dst(d)).wait_send())


def sizes(bricks, ys, koff, chans, outs):
    zs = bricks // CORES // ys
    rows = koff * chans
    unit = CORES * ys * 16
    padded = -(-rows // unit) * unit
    padded = -(-padded // LANE) * LANE
    half = padded // CORES
    first = half // ys
    second = -(-first // zs // 16) * 16 if first % zs == 0 else -(-first // (16 * zs)) * 16
    return zs, rows, padded, half, first, second


def kernel(
    dims,
    *refs,
):
    sources, targets, held = refs[0:9], refs[9:13], refs[13:24]
    feat, owner, lists, kmap, drop1, drop2, w1, w2, cot, out_ref, gf_ref = held
    body(dims, sources, targets, feat, owner, lists, kmap, drop1, drop2, w1, w2, cot, out_ref, gf_ref, *refs[24:])


def body(
    dims,
    sources,
    targets,
    feat,
    owner,
    lists,
    kmap,
    drop1,
    drop2,
    w1,
    w2,
    cot,
    out_ref,
    gf_ref,
    wg1_ref,
    wg2_ref,
    rs_low,
    io_sem,
    oh,
    wt1,
    wt2,
    gath1,
    gath2,
    pushed,
    ret,
    pm,
    em,
    perm,
    a_send,
    a_recv,
    b_send,
    b_recv,
    bb_send,
    bb_recv,
    ba_send,
    ba_recv,
    hs,
    hr,
    fs,
    fr,
    rs_send,
    rs_recv,
    full_g,
    wgf,
    wgb,
    c_recv,
    s1_src,
    s1_ra,
    s1_rb,
    s2_src,
    s2_ra,
    s2_rb,
    fin,
    chunk,
    *sems,
):
    bricks, ys, zs, chs, koff, chans, rows, padded, half, first, second, scale = dims
    qs = zs * CORES
    b, x = lax.axis_index("brick"), lax.axis_index("ch")
    y, q = b // qs, b % qs
    z, core = q // CORES, q % CORES
    slots = kmap.shape[1]
    sem_at = iter([(sems[i], sems[i + 1]) for i in range(0, len(sems), 2)])

    def ring(count, at, step):
        return lax.rem(at + step, count)

    to_y = lambda d: (ring(ys, y, d) * qs + q, x)
    to_q = lambda d: (y * qs + ring(qs, q, d), x)
    to_z = lambda d: (y * qs + ring(zs, z, d) * CORES + core, x)
    to_core = lambda d: (y * qs + z * CORES + (1 - core), x)
    to_ch = lambda d: (b, ring(chs, x, d))
    to_brick = lambda d: (lax.rem(b + 1 + (d - 1) * (bricks - 2), bricks), x)

    barrier = pltpu.get_barrier_semaphore()
    groups = ((to_y, ys), (to_q, qs), (to_ch, chs), (to_brick, 3))
    for peer, n in groups:
        unrolled(
            1,
            n,
            lambda d, peer=peer: pl.semaphore_signal(
                barrier, inc=1, device_id=peer(d), device_id_type=MESH
            ),
        )

    inputs = (feat, owner, lists, kmap, drop1, drop2, w1, w2, cot)
    fetches = [
        pltpu.make_async_copy(source, target, io_sem.at[i])
        for i, (source, target) in enumerate(zip(sources, inputs))
    ]
    for fetch in fetches:
        fetch.start()
    lower, upper = pl.ds(0, half), pl.ds(half, rows - half)
    leaving = (
        (out_ref, targets[0]),
        (gf_ref, targets[1]),
        (wg2_ref.at[pl.ds(0, rows)], targets[3]),
        (wg1_ref.at[lower], targets[2].at[lower]),
        (wg1_ref.at[upper], targets[2].at[upper]),
    )
    results = [
        pltpu.make_async_copy(source, target, io_sem.at[9 + i])
        for i, (source, target) in enumerate(leaving)
    ]
    for fetch in fetches[0:2]:
        fetch.wait()

    prows = 2 * bricks
    t_row = owner[...]
    scan = t_row.shape[1]
    t_col = jnp.broadcast_to(t_row.astype(F32), (scan, scan)).T.astype(I32)
    earlier = (t_col == t_row) & (iota((scan, scan), 0) < iota((scan, scan), 1))
    ordinal = jnp.sum(jnp.where(earlier, 1.0, 0.0), axis=0, keepdims=True)
    code = (t_row // qs) * (2 * qs) + ordinal.astype(I32) * qs + t_row % qs
    pm[...] = onehot(iota((prows, scan), 0) == code)
    carried = jnp.concatenate(
        [feat[...], jnp.where(iota((LANE - chans, scan), 0) == 0, 1.0, 0.0).astype(BF)], axis=0
    )
    a_send[...] = dot_nt(pm[...], carried).astype(BF)

    pl.semaphore_wait(barrier, sum(n - 1 for _, n in groups))

    def chunk_of(ref, index, size):
        return ref.at[pl.ds(pl.multiple_of(index * size, size), size)]

    ya, qa = 2 * qs, 2 * ys
    swap_a = Swap(
        ys,
        to_y,
        lambda d: chunk_of(a_send, ring(ys, y, d), ya),
        lambda d: chunk_of(a_recv, y, ya),
        lambda d: chunk_of(a_recv, ring(ys, y, ys - d), ya),
        next(sem_at),
    )
    swap_b = Swap(
        qs,
        to_q,
        lambda d: chunk_of(b_send, ring(qs, q, d), qa),
        lambda d: chunk_of(b_recv, q, qa),
        lambda d: chunk_of(b_recv, ring(qs, q, qs - d), qa),
        next(sem_at),
    )
    back_b = Swap(
        qs,
        to_q,
        lambda d: chunk_of(bb_send, ring(qs, q, d), qa),
        lambda d: chunk_of(bb_recv, q, qa),
        lambda d: chunk_of(bb_recv, ring(qs, q, qs - d), qa),
        next(sem_at),
    )
    back_a = Swap(
        ys,
        to_y,
        lambda d: chunk_of(ba_send, ring(ys, y, d), ya),
        lambda d: chunk_of(ba_recv, y, ya),
        lambda d: chunk_of(ba_recv, ring(ys, y, ys - d), ya),
        next(sem_at),
    )

    def neighbours(send, recv, at):
        return Swap(
            3,
            to_brick,
            lambda d: send.at[at, d - 1],
            lambda d: recv.at[at, d - 1],
            lambda d: recv.at[at, d - 1],
            next(sem_at),
        )

    halo1, halo2 = neighbours(hs, hr, 0), neighbours(hs, hr, 1)
    fold2, fold1 = neighbours(fs, fr, 0), neighbours(fs, fr, 1)

    def scatter_sum(at):
        return Swap(
            chs,
            to_ch,
            lambda d: chunk_of(rs_low.at[at], ring(chs, x, d), chans),
            lambda d: rs_recv.at[at, d - 1],
            lambda d: rs_recv.at[at, d - 1],
            next(sem_at),
        )

    sum1, sum2 = scatter_sum(0), scatter_sum(1)

    def share(at):
        return Swap(
            chs,
            to_ch,
            lambda d: chunk_of(full_g.at[at], x, chans),
            lambda d: chunk_of(full_g.at[at], x, chans),
            lambda d: chunk_of(full_g.at[at], ring(chs, x, chs - d), chans),
            next(sem_at),
        )

    share2, share1 = share(0), share(1)

    left, right = pl.ds(0, LANE), pl.ds(LANE, LANE)

    def rows_of(ref, start, size, lanes):
        return ref.at[pl.ds(pl.multiple_of(start, 16), size), lanes]

    def second_at(index):
        return jnp.minimum(index * second, first - second)

    class Total:
        def __init__(self, at, ref):
            self.at, self.ref = at, ref
            self.cores = Swap(
                3,
                lambda d: to_core(1),
                lambda d: wgb.at[at, pl.ds((d - 1) * (half // 2), half // 2)],
                lambda d: c_recv.at[at, pl.ds((d - 1) * (half // 2), half // 2)],
                lambda d: c_recv.at[at, pl.ds((d - 1) * (half // 2), half // 2)],
                next(sem_at),
            )
            src = s1_src.at[at]
            self.first = (
                Swap(
                    ys,
                    to_y,
                    lambda d: rows_of(src, ring(ys, y, d) * first, first, left),
                    lambda d: s1_ra.at[at, d - 1],
                    lambda d: s1_ra.at[at, d - 1],
                    next(sem_at),
                ),
                Swap(
                    zs,
                    to_z,
                    lambda d: rows_of(src, ring(zs, z, d) * first, first, right),
                    lambda d: s1_rb.at[at, d - 1],
                    lambda d: s1_rb.at[at, d - 1],
                    next(sem_at),
                ),
            )
            self.second = (
                Swap(
                    zs,
                    to_z,
                    lambda d: s2_src.at[at, 0, pl.ds(pl.multiple_of(second_at(ring(zs, z, d)), 16), second)],
                    lambda d: s2_ra.at[at, d - 1],
                    lambda d: s2_ra.at[at, d - 1],
                    next(sem_at),
                ),
                Swap(
                    ys,
                    to_y,
                    lambda d: s2_src.at[at, 1, pl.ds(pl.multiple_of(second_at(ring(ys, y, d)), 16), second)],
                    lambda d: s2_rb.at[at, d - 1],
                    lambda d: s2_rb.at[at, d - 1],
                    next(sem_at),
                ),
            )
            self.third = (
                Swap(
                    zs,
                    to_z,
                    lambda d: fin.at[at, 0],
                    lambda d: chunk_of(chunk.at[at, 0], z, second),
                    lambda d: chunk_of(chunk.at[at, 0], ring(zs, z, zs - d), second),
                    next(sem_at),
                ),
                Swap(
                    ys,
                    to_y,
                    lambda d: fin.at[at, 1],
                    lambda d: chunk_of(chunk.at[at, 1], y, second),
                    lambda d: chunk_of(chunk.at[at, 1], ring(ys, y, ys - d), second),
                    next(sem_at),
                ),
            )
            self.fourth = (
                Swap(
                    ys,
                    to_y,
                    lambda d: chunk.at[at, 0, pl.ds(0, first)],
                    lambda d: rows_of(ref, core * half + y * first, first, left),
                    lambda d: rows_of(ref, core * half + ring(ys, y, ys - d) * first, first, left),
                    next(sem_at),
                ),
                Swap(
                    zs,
                    to_z,
                    lambda d: chunk.at[at, 1, pl.ds(0, first)],
                    lambda d: rows_of(ref, core * half + z * first, first, right),
                    lambda d: rows_of(ref, core * half + ring(zs, z, zs - d) * first, first, right),
                    next(sem_at),
                ),
            )
            self.last = tuple(
                Swap(
                    n + 1,
                    lambda d: to_core(1),
                    lambda d, n=n, pos=pos, lanes=lanes: rows_of(
                        ref, core * half + ring(n, pos, n + 1 - d) * first, first, lanes
                    ),
                    lambda d, n=n, pos=pos, lanes=lanes: rows_of(
                        ref, core * half + ring(n, pos, n + 1 - d) * first, first, lanes
                    ),
                    lambda d, n=n, pos=pos, lanes=lanes: rows_of(
                        ref, (1 - core) * half + ring(n, pos, n + 1 - d) * first, first, lanes
                    ),
                    next(sem_at),
                )
                for n, pos, lanes in ((ys, y, left), (zs, z, right))
            )
            self.all = (
                self.cores, *self.first, *self.second, *self.third, *self.fourth, *self.last
            )

        def compute(self, gath, grads, which):
            g, block = grads[...], half // 2
            for i in range(2):
                start = which * half + i * block
                yield pl.ds(i * block, block), dot_nt(
                    gath[pl.ds(pl.multiple_of(start, 16), block), :], g
                )

        def give(self, gath, grads):
            for i, (span, part) in enumerate(self.compute(gath, grads, 1 - core)):
                wgb[self.at, span, :] = part.astype(BF)
                self.cores.start_one(i + 1)

        def keep(self, gath, grads):
            for span, part in self.compute(gath, grads, core):
                wgf[self.at, span, :] = part

        def to_first(self):
            self.cores.wait()
            for swap, lanes in zip(self.first, (left, right)):
                both = wgf[self.at, :, lanes] + c_recv[self.at, :, lanes].astype(F32)
                s1_src[self.at, :, lanes] = both.astype(BF)
                swap.start()

        def to_second(self):
            for side, (swap, recv, pos, lanes, n) in enumerate(
                zip(self.first, (s1_ra, s1_rb), (y, z), (left, right), (ys, zs))
            ):
                swap.wait()
                span = pl.ds(pl.multiple_of(pos * first, 16), first)
                total = s1_src[self.at, span, lanes].astype(F32)
                for d in range(n - 1):
                    total = total + recv[self.at, d].astype(F32)
                s2_src[self.at, side] = total
                self.second[side].start()

        def to_third(self):
            for side, (swap, recv, pos, n) in enumerate(
                zip(self.second, (s2_ra, s2_rb), (z, y), (zs, ys))
            ):
                swap.wait()
                span = pl.ds(pl.multiple_of(second_at(pos), 16), second)
                total = s2_src[self.at, side, span, :]
                for d in range(n - 1):
                    total = total + recv[self.at, d]
                done = (total * scale).astype(BF)
                fin[self.at, side] = done
                chunk[self.at, side, pl.ds(pl.multiple_of(pos * second, 16), second), :] = done
                self.third[side].start()

        def to_fourth(self):
            for side, (swap, pos, lanes) in enumerate(zip(self.third, (y, z), (left, right))):
                swap.wait()
                self.fourth[side].start()
                span = pl.ds(pl.multiple_of(core * half + pos * first, 16), first)
                self.ref[span, lanes] = chunk[self.at, side, pl.ds(0, first), :]
                self.last[side].start_one(1)

        def to_last(self):
            for i in range(max(ys, zs) - 1):
                for side, swap in enumerate(self.fourth):
                    if i < swap.n - 1:
                        d = 1 + i // 2 if i % 2 == 0 else swap.n - 1 - i // 2
                        swap.wait_one(d)
                        self.last[side].start_one(d + 1)

        def finish(self):
            for swap in self.last:
                swap.wait()

    total2, total1 = Total(0, wg2_ref), Total(1, wg1_ref)

    def own_rows(src, dst, index, size):
        span = pl.ds(pl.multiple_of(index * size, size), size)
        dst[span, :] = src[span, :]

    swap_a.start()
    own_rows(a_send, a_recv, y, ya)

    pr, pc = iota((prows, prows), 0), iota((prows, prows), 1)
    perm[...] = onehot(pc == (pr % ys) * ya + ((pr // ys) % 2) * qs + pr // qa)
    er, ec = iota((prows, slots), 0), iota((prows, slots), 1)
    em[...] = onehot(ec == 2 * ((er % ys) * qs + er // qa) + (er // ys) % 2)

    rim = 32

    def build(k):
        row = kmap[pl.ds(k, 1), :]
        inner = jnp.where(row < rim + slots, row - rim, row)
        column = jnp.where(row < rim, row + slots, jnp.where(row >= slots + 2 * rim, -1, inner))
        oh[k] = onehot(iota(oh.shape[1:], 0) == column)

    for fetch in fetches[2:4]:
        fetch.wait()
    unrolled(0, koff // 3, build)

    swap_a.wait()
    b_send[...] = dot(perm[...], a_recv[...]).astype(BF)
    swap_b.start()
    own_rows(b_send, b_recv, q, qa)

    unrolled(koff // 3, koff, build)

    def turn(source, target):
        blocks = rows // LANE

        def step(j):
            at = pl.multiple_of(j * LANE, LANE)
            target[:, pl.ds(at, LANE)] = source[pl.ds(at, LANE), :].astype(F32).T.astype(BF)

        unrolled(0, blocks, step)
        if rows % LANE:
            tail = source[blocks * LANE : rows, :].astype(F32)
            tail = jnp.concatenate([tail, jnp.zeros((LANE - rows % LANE, tail.shape[1]), F32)], 0)
            target[:, blocks * LANE : (blocks + 1) * LANE] = tail.T.astype(BF)

    for fetch in fetches[4:9]:
        fetch.wait()
    turn(w1, wt1)
    turn(w2, wt2)
    for gath in (gath1, gath2):
        gath[rows:padded, :] = jnp.zeros((padded - rows, slots), BF)

    both = jnp.concatenate(
        [lists[1:2, :], lists[0:1, :], jnp.full((1, LANE - 2 * rim), -1, I32)], axis=1
    )
    lent = iota((slots, LANE), 0) == both
    side = iota((slots, LANE), 1) < rim
    lend_next, lend_prev = onehot(lent & side), onehot(lent & ~side)
    has_prev = (b > 0).astype(F32)
    has_next = (b < bricks - 1).astype(F32)

    swap_b.wait()
    arrived = dot(b_recv[...].astype(F32).T.astype(BF), em[...])
    occupied = arrived[chans : chans + 1, :]
    voxels = arrived[0:chans, :].astype(BF)
    keep1 = occupied * drop1[...].astype(F32) / KEEP_RATE
    keep2 = occupied * drop2[...].astype(F32) / KEEP_RATE

    def lend(field, halo, at):
        hs[at, 0] = dot(field, lend_next).astype(BF)
        hs[at, 1] = dot(field, lend_prev).astype(BF)
        halo.start()

    def convolve(field, halo, at, gath, wt, summing):
        def inner(k):
            gath[k * chans : (k + 1) * chans, :] = dot(field, oh[k, 0:slots, :]).astype(BF)

        unrolled(0, koff, inner)
        halo.wait()
        edge = hr[at, 0].astype(F32) * has_prev + hr[at, 1].astype(F32) * has_next
        edge = edge.astype(BF)

        def outer(k):
            part = dot(edge, oh[k, slots : slots + LANE, :]).astype(BF)
            gath[k * chans : (k + 1) * chans, :] += part

        unrolled(0, koff, outer)
        partial = dot(wt[...], gath[...])
        rs_low[at] = partial.astype(BF)
        summing.start()
        rs_send[at] = partial
        own = rs_send[at, pl.ds(pl.multiple_of(x * chans, 16), chans), :]
        summing.wait()
        for d in range(chs - 1):
            own = own + rs_recv[at, d].astype(F32)
        return own

    lend(voxels, halo1, 0)
    conv1 = convolve(voxels, halo1, 0, gath1, wt1, sum1)
    hidden = (conv1 * jax.nn.sigmoid(conv1) * keep1).astype(BF)
    lend(hidden, halo2, 1)
    conv2 = convolve(hidden, halo2, 1, gath2, wt2, sum2)
    summed = voxels.astype(F32) + keep2 * conv2
    grad_pre = cot[...].astype(F32) * slope_silu(summed)
    mine = pl.ds(pl.multiple_of(x * chans, 16), chans)
    full_g[0, mine, :] = (grad_pre * keep2).astype(BF)
    share2.start()
    out_ref[...] = (summed * jax.nn.sigmoid(summed)).astype(BF)
    results[0].start()

    def push(weight, grads, fold, at):
        g = grads[...]

        def ahead(j):
            span = pl.ds(pl.multiple_of(j * 3 * chans, 16), 3 * chans)
            high, low = split(dot(weight[span, :], g))
            for i in range(3):
                part = slice(i * chans, (i + 1) * chans)
                pushed[3 * j + i, 0:chans, :] = high[part]
                pushed[3 * j + i, chans : 2 * chans, :] = low[part]

        unrolled(0, koff // 3, ahead)
        both = returned(slots, slots + LANE)
        border = both[0:chans] + both[chans : 2 * chans]
        fs[at, 0] = border
        fs[at, 1] = border
        fold.start()

    def returned(low, high):
        part = dot_nt(pushed[0], oh[0, low:high, :])
        for k in range(1, koff):
            part = part + dot_nt(pushed[k], oh[k, low:high, :])
        return part

    def own_columns():
        ret[...] = returned(0, slots)

    def folded(fold, at):
        own = ret[0:chans, :] + ret[chans : 2 * chans, :]
        fold.wait()
        for part in split(fr[at, 0] * has_prev):
            own = own + dot_nt(part, lend_prev)
        for part in split(fr[at, 1] * has_next):
            own = own + dot_nt(part, lend_next)
        return own

    share2.wait()
    push(w2, full_g.at[0], fold2, 0)
    own_columns()
    total2.give(gath2, full_g.at[0])
    grad_hidden = folded(fold2, 0)
    full_g[1, mine, :] = (grad_hidden * keep1 * slope_silu(conv1)).astype(BF)
    share1.start()
    total2.keep(gath2, full_g.at[0])
    total2.to_first()
    share1.wait()
    total1.give(gath1, full_g.at[1])
    push(w1, full_g.at[1], fold1, 1)
    total1.keep(gath1, full_g.at[1])
    total1.to_first()
    own_columns()
    total2.to_second()
    grad_voxels = (grad_pre + folded(fold1, 1)).astype(BF)
    wide = jnp.concatenate([grad_voxels, jnp.zeros((LANE - chans, slots), BF)], axis=0)
    bb_send[...] = dot_nt(em[...], wide).astype(BF)
    back_b.start()
    own_rows(bb_send, bb_recv, q, qa)
    perm_back = onehot(pc == (pr % qs) * qa + ((pr // qs) % 2) * ys + pr // ya)
    total1.to_second()
    total2.to_third()
    back_b.wait()
    ba_send[...] = dot(perm_back, bb_recv[...]).astype(BF)
    back_a.start()
    own_rows(ba_send, ba_recv, y, ya)
    total1.to_third()
    total2.to_fourth()
    total1.to_fourth()
    back_a.wait()
    gf = dot(ba_recv[...].astype(F32).T.astype(BF), pm[...])
    gf_ref[...] = gf[0:chans, :].astype(BF)
    results[1].start()
    total2.to_last()
    for swap in (
        swap_a,
        swap_b,
        back_b,
        back_a,
        halo1,
        halo2,
        fold2,
        fold1,
        sum1,
        sum2,
        share2,
        share1,
        *total2.all[:-2],
        *total1.all[:-4],
    ):
        swap.done()
    total2.finish()
    results[2].start()
    total1.to_last()

    @pl.when(core == 0)
    def _():
        results[3].start()

    @pl.when(core == 1)
    def _():
        results[4].start()

    for swap in (*total2.last, *total1.fourth):
        swap.done()
    total1.finish()

    @pl.when(core == 1)
    def _():
        results[3].start()

    @pl.when(core == 0)
    def _():
        results[4].start()

    for swap in total1.last:
        swap.done()
    for result in results:
        result.wait()


def store(*refs):
    sources, targets, sem = refs[0:4], refs[4:8], refs[8]
    copies = [
        pltpu.make_async_copy(source.at[pl.ds(0, target.shape[0])], target, sem.at[i])
        for i, (source, target) in enumerate(zip(sources, targets))
    ]
    for copy in copies:
        copy.start()
    for copy in copies:
        copy.wait()


def local(ys, features, owner_map, kernel_map, send_lists, drop1, drop2, w1, w2, cotangent):
    bricks, chs = lax.axis_size("brick"), lax.axis_size("ch")
    chans, scan = features.shape
    koff, slots = kernel_map.shape
    outs = w1.shape[2]
    zs, rows, padded, half, first, second = sizes(bricks, ys, koff, chans, outs)
    qs = zs * CORES
    rim = send_lists.shape[1]
    dims = (
        bricks, ys, zs, chs, koff, chans, rows, padded, half, first, second,
        float(bricks * slots) ** -0.5,
    )
    prows = 2 * bricks
    vm = pltpu.VMEM
    table = slots + LANE
    scratch = [
        vm((chans, scan), BF),
        vm((1, scan), I32),
        vm(send_lists.shape, I32),
        vm((koff, slots), I32),
        vm((chans, slots), I32),
        vm((chans, slots), I32),
        vm((rows, outs), BF),
        vm((rows, outs), BF),
        vm((chans, slots), BF),
        vm((chans, slots), BF),
        vm((chans, scan), BF),
        vm((padded, outs), BF),
        vm((padded, outs), BF),
        vm((2, outs, slots), BF),
        pltpu.SemaphoreType.DMA((14,)),
        vm((koff, table, slots), BF),
        vm((outs, padded), BF),
        vm((outs, padded), BF),
        vm((padded, slots), BF),
        vm((padded, slots), BF),
        vm((koff, 2 * chans, slots), BF),
        vm((2 * chans, slots), F32),
        vm((prows, scan), BF),
        vm((prows, slots), BF),
        vm((prows, prows), BF),
        *[vm((prows, LANE), BF)] * 8,
        vm((2, 2, chans, LANE), BF),
        vm((2, 2, chans, LANE), BF),
        vm((2, 2, chans, LANE), F32),
        vm((2, 2, chans, LANE), F32),
        vm((2, outs, slots), F32),
        vm((2, chs - 1, chans, slots), BF),
        vm((2, outs, slots), BF),
        vm((2, half, outs), F32),
        vm((2, half, outs), BF),
        vm((2, half, outs), BF),
        vm((2, half, outs), BF),
        vm((2, ys - 1, first, LANE), BF),
        vm((2, zs - 1, first, LANE), BF),
        vm((2, 2, first, LANE), F32),
        vm((2, zs - 1, second, LANE), F32),
        vm((2, ys - 1, second, LANE), F32),
        vm((2, 2, second, LANE), BF),
        vm((2, 2, max(ys, zs) * second, LANE), BF),
    ]
    weight_sums = [2, ys - 1, zs - 1, zs - 1, ys - 1, zs - 1, ys - 1, ys - 1, zs - 1, ys, zs]
    copies = [ys - 1, qs - 1, qs - 1, ys - 1, 2, 2, 2, 2] + [chs - 1] * 4 + weight_sums * 2
    for n in copies:
        scratch += [pltpu.SemaphoreType.DMA((n,))] * 2
    shape = jax.ShapeDtypeStruct
    spec = pl.BlockSpec(memory_space=pltpu.VMEM)
    anywhere = pl.BlockSpec(memory_space=pl.ANY)
    results = pl.pallas_call(
        functools.partial(kernel, dims),
        out_shape=(
            shape((chans, slots), BF),
            shape((chans, scan), BF),
            shape((rows, outs), BF),
            shape((rows, outs), BF),
        ),
        in_specs=[anywhere] * 9,
        out_specs=(anywhere,) * 4,
        scratch_shapes=scratch,
        compiler_params=pltpu.CompilerParams(
            collective_id=0, has_side_effects=True, vmem_limit_bytes=56 * 2**20
        ),
        name="block",
    )(
        features, owner_map.reshape(1, scan), send_lists, kernel_map, drop1, drop2,
        w1.reshape(rows, outs), w2.reshape(rows, outs), cotangent,
    )
    block_out, grad_features, wg1, wg2 = pl.pallas_call(
        store,
        out_shape=(
            shape((chans, slots), BF),
            shape((chans, scan), BF),
            shape((rows, outs), BF),
            shape((rows, outs), BF),
        ),
        in_specs=[spec] * 4,
        out_specs=(anywhere,) * 4,
        scratch_shapes=[pltpu.SemaphoreType.DMA((4,))],
        name="store",
    )(*results)
    return block_out, grad_features, wg1.reshape(w1.shape), wg2.reshape(w2.shape)


def rows_of_chips(bricks):
    ys = 1
    while ys * ys * CORES < bricks:
        ys *= 2
    return ys


def solution(mesh):
    return jax.shard_map(
        functools.partial(local, rows_of_chips(mesh.shape["brick"])),
        mesh=mesh,
        in_specs=(
            P("ch", "brick"),
            P("brick", None),
            P(None, "brick"),
            P(None, "brick"),
            P("ch", "brick"),
            P("ch", "brick"),
            P(None, "ch", None),
            P(None, "ch", None),
            P("ch", "brick"),
        ),
        out_specs=(P("ch", "brick"), P("ch", "brick"), P(None, "ch", None), P(None, "ch", None)),
        check_vma=False,
    )
```
